128 devices in a mesh: fsdp: 16 (over y_hi, x, core), ctx: 8 (over z, y_lo).
Axes of the slice: x: 4, y: 4 (y_hi: 2, y_lo: 2; y = y_hi * 2 + y_lo), z: 4, core: 2. Of those that a mesh axis runs over, the one named last changes fastest.
Arguments:
- tokens: bfloat16 [16, 2048, 960], P('fsdp', 'ctx'), may hold values from -6 to 6
- attn_gain: bfloat16 [960], P('fsdp'), may hold values from 0.5 to 1.5
- w_query: bfloat16 [960, 960], P('fsdp'), may hold values from -0.1875 to 0.1875
- key_weight: bfloat16 [960, 320], P('fsdp'), may hold values from -0.1875 to 0.1875
- value_weight: bfloat16 [960, 320], P('fsdp'), may hold values from -0.1875 to 0.1875
- w_out: bfloat16 [960, 960], P('fsdp'), may hold values from -0.5 to 0.5
- ffn_gain: bfloat16 [960], P('fsdp'), may hold values from 0.5 to 1.5
- w_gate: bfloat16 [960, 2560], P('fsdp'), may hold values from -0.1875 to 0.1875
- w_up: bfloat16 [960, 2560], P('fsdp'), may hold values from -0.1875 to 0.1875
- w_down: bfloat16 [2560, 960], P('fsdp'), may hold values from -0.125 to 0.125
- d_out: bfloat16 [16, 2048, 960], P('fsdp', 'ctx'), may hold values from -6 to 6
Outputs:
- output: bfloat16 [16, 2048, 960], P('fsdp', 'ctx')
- d_tokens: bfloat16 [16, 2048, 960], P('fsdp', 'ctx')
- grad_attn_gain: float32 [960], P('fsdp')
- grad_query: float32 [960, 960], P('fsdp')
- grad_key: float32 [960, 320], P('fsdp')
- grad_value: float32 [960, 320], P('fsdp')
- grad_out: float32 [960, 960], P('fsdp')
- grad_ffn_gain: float32 [960], P('fsdp')
- grad_gate: float32 [960, 2560], P('fsdp')
- grad_up: float32 [960, 2560], P('fsdp')
- grad_down: float32 [2560, 960], P('fsdp')
The draws below stay inside these ranges and needn't reach their ends.
All inputs are finite; a program needn't handle non-finite values.
Results may differ from the reference program's by a relative error of at most 0.025.
Values may be sent and summed in bfloat16 or wider, within the bound.
A program may use at most 192 MiB of HBM per device.

```python
import jax
import jax.numpy as jnp
from jax import lax

MODEL_WIDTH = 960
QUERY_HEADS = 15
KEY_VALUE_HEADS = 5
HEAD_WIDTH = 64
FF = 2560
LENGTH = 2048
SEQS = 16


def steps_of(stream_key, extent, pieces, smallest, largest):
    factor_of, own = 1.0, jax.random.fold_in(stream_key, 6)
    for position, shards_of in pieces:
        heights = jnp.exp(jax.random.uniform(jax.random.fold_in(own, position), (shards_of,), jnp.float32, smallest / len(pieces), largest / len(pieces)))
        factor_of = factor_of * jnp.repeat(heights, extent[position] // shards_of).reshape([-1 if axis == position else 1 for axis in range(len(extent))])
    return factor_of


def noise(own_key, shape, width, bound, cuts=(), kind=jnp.bfloat16):
    level = steps_of(own_key, shape, cuts, -0.22, 0.18) if cuts else 1.0
    entries = jax.random.normal(own_key, shape, jnp.float32) * width * level
    return jnp.minimum(jnp.maximum(entries, -bound), bound).astype(kind)


def setup_inputs(seed: int = 0) -> dict:
    keys = jax.random.split(jax.random.key(seed), 12)
    tokens = noise(keys[0], (SEQS, LENGTH, MODEL_WIDTH), 1.0, 6.0, ((0, 16), (1, 8)))
    attn_gain = jnp.clip(1.0 + 0.1 * jax.random.normal(keys[1], (MODEL_WIDTH,), jnp.float32), 0.5, 1.5).astype(jnp.bfloat16)
    w_query = noise(keys[2], (MODEL_WIDTH, QUERY_HEADS * HEAD_WIDTH), MODEL_WIDTH ** -0.5, 0.1875, ((0, 16),))
    key_weight = noise(keys[3], (MODEL_WIDTH, KEY_VALUE_HEADS * HEAD_WIDTH), MODEL_WIDTH ** -0.5, 0.1875, ((0, 16),))
    value_weight = noise(keys[4], (MODEL_WIDTH, KEY_VALUE_HEADS * HEAD_WIDTH), MODEL_WIDTH ** -0.5, 0.1875, ((0, 16),))
    w_out = noise(keys[5], (QUERY_HEADS * HEAD_WIDTH, MODEL_WIDTH), (QUERY_HEADS * HEAD_WIDTH // 8) ** -0.5, 0.5, ((0, 16),))
    ffn_gain = jnp.clip(1.0 + 0.1 * jax.random.normal(keys[6], (MODEL_WIDTH,), jnp.float32), 0.5, 1.5).astype(jnp.bfloat16)
    w_gate = noise(keys[7], (MODEL_WIDTH, FF), MODEL_WIDTH ** -0.5, 0.1875, ((0, 16),))
    w_up = noise(keys[8], (MODEL_WIDTH, FF), MODEL_WIDTH ** -0.5, 0.1875, ((0, 16),))
    w_down = noise(keys[9], (FF, MODEL_WIDTH), FF ** -0.5, 0.125, ((0, 16),))
    d_out = noise(keys[10], (SEQS, LENGTH, MODEL_WIDTH), 1.0, 6.0, ((0, 16), (1, 8)))
    return {"tokens": tokens, "attn_gain": attn_gain, "w_query": w_query, "key_weight": key_weight, "value_weight": value_weight, "w_out": w_out, "ffn_gain": ffn_gain, "w_gate": w_gate, "w_up": w_up, "w_down": w_down, "d_out": d_out}


EPS = 1e-05
ROPE_BASE = 10000.0

@jax.custom_vjp
def reduced_precision(v):
    return lax.optimization_barrier(v.astype(jnp.bfloat16)).astype(jnp.float32)

@jax.custom_vjp
def reduced_precision_backward(v):
    return v

def low_keep(v):
    return (reduced_precision(v), None)

def low_pass(kept, grad):
    return (grad,)

def back_keep(v):
    return (v, None)

def back_low(kept, grad):
    return (reduced_precision(grad),)
reduced_precision.defvjp(low_keep, low_pass)
reduced_precision_backward.defvjp(back_keep, back_low)

def matrix_multiply(left, right):
    return jnp.dot(left, right, precision=lax.Precision.HIGHEST, preferred_element_type=jnp.float32)

def rms_norm(value_rows, gain):
    return value_rows * lax.rsqrt(lax.optimization_barrier(jnp.mean(value_rows * value_rows, axis=-1, keepdims=True)) + EPS) * gain

def apply_rotary(value_rows, token_positions):
    half = value_rows.shape[-1] // 2
    freqs = ROPE_BASE ** (-jnp.arange(half, dtype=jnp.float32) * 2.0 / value_rows.shape[-1])
    angles = token_positions.astype(jnp.float32)[:, None] * freqs[None, :]
    cosine_table = jnp.cos(angles)[:, None, :]
    sine_table = jnp.sin(angles)[:, None, :]
    first = value_rows[..., :half]
    second = value_rows[..., half:]
    return jnp.concatenate([first * cosine_table - second * sine_table, second * cosine_table + first * sine_table], axis=-1)

def layer(sequence, attn_gain, w_query, key_weight, value_weight, w_out, ffn_gain, w_gate, w_up, w_down):
    sequence_length = sequence.shape[0]
    query_group = QUERY_HEADS // KEY_VALUE_HEADS
    token_positions = jnp.arange(sequence_length, dtype=jnp.int32)
    normalized_input = reduced_precision(rms_norm(sequence, attn_gain))
    query_rows = reduced_precision_backward(matrix_multiply(normalized_input, w_query)).reshape(sequence_length, QUERY_HEADS, HEAD_WIDTH)
    key_rows = reduced_precision_backward(matrix_multiply(normalized_input, key_weight)).reshape(sequence_length, KEY_VALUE_HEADS, HEAD_WIDTH)
    value_rows = reduced_precision(reduced_precision_backward(matrix_multiply(normalized_input, value_weight))).reshape(sequence_length, KEY_VALUE_HEADS, HEAD_WIDTH)
    query_rows = reduced_precision(apply_rotary(query_rows, token_positions)).reshape(sequence_length, KEY_VALUE_HEADS, query_group, HEAD_WIDTH)
    key_rows = reduced_precision(apply_rotary(key_rows, token_positions))
    scores = reduced_precision_backward(jnp.einsum('lhge,mhe->hglm', query_rows, key_rows, precision=lax.Precision.HIGHEST) * HEAD_WIDTH ** (-0.5))
    causal = token_positions[:, None] >= token_positions[None, :]
    scores = jnp.where(causal, scores, -1e+30)
    probs = reduced_precision(jax.nn.softmax(scores, axis=-1))
    mixed = jnp.einsum('hglm,mhe->lhge', probs, value_rows, precision=lax.Precision.HIGHEST)
    mixed = reduced_precision(reduced_precision_backward(mixed)).reshape(sequence_length, QUERY_HEADS * HEAD_WIDTH)
    resid = sequence + reduced_precision_backward(matrix_multiply(mixed, w_out))
    normed_two = reduced_precision(rms_norm(resid, ffn_gain))
    gate = reduced_precision_backward(matrix_multiply(normed_two, w_gate))
    up_part = reduced_precision_backward(matrix_multiply(normed_two, w_up))
    hidden = reduced_precision(jax.nn.silu(gate) * up_part)
    return resid + matrix_multiply(hidden, w_down)

def reference(tokens, attn_gain, w_query, key_weight, value_weight, w_out, ffn_gain, w_gate, w_up, w_down, d_out):
    params = tuple((item.astype(jnp.float32) for item in (attn_gain, w_query, key_weight, value_weight, w_out, ffn_gain, w_gate, w_up, w_down)))

    def forward(inputs, *weights):

        def one_layer(sequence):
            return layer(sequence, *weights)
        checked = jax.checkpoint(one_layer)

        def advance(carry, sequence):
            return (carry, checked(sequence))
        _, outputs = lax.scan(advance, jnp.zeros((), jnp.float32), inputs)
        return outputs
    outputs, pullback = jax.vjp(forward, tokens.astype(jnp.float32), *params)
    grads = pullback(d_out.astype(jnp.float32))
    return (outputs.astype(jnp.bfloat16), grads[0].astype(jnp.bfloat16), grads[1], grads[2], grads[3], grads[4], grads[5], grads[6], grads[7], grads[8], grads[9])
```

```python
import functools
import math

import jax
import jax.numpy as jnp
from jax import lax
from jax.experimental import pallas as pl
from jax.experimental.pallas import tpu as pltpu
from jax.sharding import PartitionSpec as P

QUERY_HEADS = 15
KEY_VALUE_HEADS = 5
HEAD_WIDTH = 64
GROUP = QUERY_HEADS // KEY_VALUE_HEADS
WIDTH = 960
ROWS = 60
PAD = 64
SHARDS = 16
PADDED = SHARDS * PAD
KV_WIDTH = KEY_VALUE_HEADS * HEAD_WIDTH
QKV_WIDTH = 1664

EPS = 1e-05
ROPE_BASE = 10000.0
MESH = pl.DeviceIdType.MESH
BF16 = jnp.bfloat16
F32 = jnp.float32


def place():
    f, t = lax.axis_index("fsdp"), lax.axis_index("ctx")
    return f // 8, (f // 2) % 4, f % 2, t // 2, t % 2


def device(yh, x, c, z, yl):
    return ((yh * 4 + x) * 2 + c, z * 2 + yl)


class Places:
    def __init__(self):
        yh, x, c, z, yl = place()
        self.yh, self.x, self.c, self.z, self.yl = yh, x, c, z, yl
        self.sib = device(yh, x, 1 - c, z, yl)
        self.ypair = device(1 - yh, x, c, z, 1 - yl)
        self.ylo = device(yh, x, c, z, 1 - yl)
        self.xs = [(x + 1) % 4, (x + 3) % 4, (x + 2) % 4]
        self.zs = [(z + 1) % 4, (z + 3) % 4, (z + 2) % 4]
        self.xdev = [device(yh, k, c, z, yl) for k in self.xs]
        self.zdev = [device(yh, x, c, k, yl) for k in self.zs]
        self.xfrom = [self.xs[1], self.xs[0], self.xs[2]]
        self.zfrom = [self.zs[1], self.zs[0], self.zs[2]]


def greet(devices):
    barrier = pltpu.get_barrier_semaphore()
    for d in devices:
        pl.semaphore_signal(barrier, inc=1, device_id=d, device_id_type=MESH)
    pl.semaphore_wait(barrier, len(devices))


class Sems:
    def __init__(self, send, recv):
        self.send, self.recv, self.at, self.open = send, recv, 0, []

    def take(self, count=1):
        at = self.at
        self.at += count
        return at

    def push(self, slot, src, dst, dev):
        copy = pltpu.make_async_remote_copy(
            src_ref=src,
            dst_ref=dst,
            send_sem=self.send.at[slot],
            recv_sem=self.recv.at[slot],
            device_id=dev,
            device_id_type=MESH,
        )
        copy.start()
        self.open.append(copy)

    def arrived(self, slot, dst, dev):
        pltpu.make_async_remote_copy(
            src_ref=dst,
            dst_ref=dst,
            send_sem=self.send.at[slot],
            recv_sem=self.recv.at[slot],
            device_id=dev,
            device_id_type=MESH,
        ).wait_recv()

    def finish(self):
        for copy in self.open:
            copy.wait_send()
        self.open = []


GATHER_SEMS = 24


def gather_steps(pc, sems, local_sem, shard, out, split):
    rows = shard.shape[0]
    quarter = rows // 4
    yh, x, c, z = pc.yh, pc.x, pc.c, pc.z
    s_y = sems.take()
    s_x = [[sems.take() for _ in range(2)] for _ in range(3)]
    s_z = [[sems.take() for _ in range(3)] for _ in range(3)] if split else None
    s_s = [sems.take() for _ in range(4)]
    band = pl.ds(pl.multiple_of(z * quarter, 16), quarter) if split else pl.ds(0, rows)

    own = pltpu.make_async_copy(shard, out.at[yh, x, c], local_sem)
    own.start()
    sems.push(s_y, shard, out.at[yh, x, c], pc.ypair)
    for k in (0, 1, 2):
        sems.push(s_x[k][0], shard.at[band], out.at[yh, x, c, band], pc.xdev[k])
    yield
    sems.arrived(s_y, out.at[1 - yh, x, c], pc.ypair)
    for k in (0, 1, 2):
        piece = out.at[1 - yh, x, c, band]
        sems.push(s_x[k][1], piece, piece, pc.xdev[k])
    own.wait()
    sems.push(s_s[3], out.at[:, x, c], out.at[:, x, c], pc.sib)
    yield
    for k in (0, 1, 2):
        far = pc.xfrom[k]
        sems.arrived(s_x[k][0], out.at[yh, far, c, band], pc.xdev[k])
        sems.arrived(s_x[k][1], out.at[1 - yh, far, c, band], pc.xdev[k])
        if split:
            piece = out.at[:, far, c, band]
            for j in range(3):
                sems.push(s_z[k][j], piece, piece, pc.zdev[j])
        else:
            sems.push(s_s[k], out.at[:, far, c], out.at[:, far, c], pc.sib)
    yield
    if split:
        for k in (0, 1, 2):
            far = pc.xfrom[k]
            for j in range(3):
                there = pl.ds(pl.multiple_of(pc.zfrom[j] * quarter, 16), quarter)
                sems.arrived(s_z[k][j], out.at[:, far, c, there], pc.zdev[j])
            sems.push(s_s[k], out.at[:, far, c], out.at[:, far, c], pc.sib)
        yield
    for k in (0, 1, 2, 3):
        far = x if k == 3 else pc.xfrom[k]
        sems.arrived(s_s[k], out.at[:, far, 1 - c], pc.sib)
    yield


def run_all(steps):
    live = list(steps)
    while live:
        for s in list(live):
            try:
                next(s)
            except StopIteration:
                live.remove(s)


def gather_kernel(splits, *refs):
    n = len(splits)
    shards, outs = refs[:n], refs[n : 2 * n]
    send, recv, local = refs[2 * n :]
    pc = Places()
    greet([pc.sib, pc.ypair, *pc.xdev, *pc.zdev])
    sems = Sems(send, recv)
    run_all(
        [
            gather_steps(pc, sems, local.at[k], shards[k], outs[k], splits[k])
            for k in range(n)
        ]
    )
    sems.finish()


def gather_weights(shards, splits, collective_id):
    n = len(shards)
    return pl.pallas_call(
        functools.partial(gather_kernel, splits),
        out_shape=[jax.ShapeDtypeStruct((2, 4, 2, *s.shape), s.dtype) for s in shards],
        in_specs=[pl.BlockSpec(memory_space=pl.ANY)] * n,
        out_specs=[pl.BlockSpec(memory_space=pl.ANY)] * n,
        scratch_shapes=[
            pltpu.SemaphoreType.DMA((n * GATHER_SEMS,)),
            pltpu.SemaphoreType.DMA((n * GATHER_SEMS,)),
            pltpu.SemaphoreType.DMA((n,)),
        ],
        compiler_params=pltpu.CompilerParams(
            collective_id=collective_id, has_side_effects=True, vmem_limit_bytes=60 << 20
        ),
    )(*shards)


REDUCE_SEMS = 24


def add_rows(dst, terms, shape):
    lead, rows = shape[:-2], shape[-2]
    blocks = rows // 16
    count = math.prod(lead) * blocks

    def body(i, carry):
        idx, rest = [], i // blocks
        for size in reversed(lead):
            idx.append(rest % size)
            rest = rest // size
        idx = tuple(reversed(idx))
        at = (*idx, pl.ds(pl.multiple_of((i % blocks) * 16, 16), 16))
        total = dst[at].astype(F32)
        for term in terms:
            total = total + term[at].astype(F32)
        dst[at] = total.astype(BF16)
        return carry

    lax.fori_loop(0, count, body, 0)


def reduce_scratch(rows, width, split):
    q = rows // 4
    buffers = [pltpu.VMEM((2, 4, rows, width), BF16)] * 2
    if split:
        buffers += [
            pltpu.VMEM((3, 2, 4, q, width), BF16),
            pltpu.VMEM((3, 2, q, width), BF16),
            pltpu.VMEM((q, width), BF16),
            pltpu.VMEM((q, width), BF16),
        ]
    else:
        w = width // 4
        buffers += [
            pltpu.VMEM((3, rows, w), BF16),
            pltpu.VMEM((3, 2, rows, width), BF16),
            pltpu.VMEM((rows, width), BF16),
            pltpu.VMEM((rows, w), BF16),
        ]
    return buffers


def reduce_steps(pc, sems, local_sem, part, final, buffers, split):
    yh, x, c, z = pc.yh, pc.x, pc.c, pc.z
    acc, from_sib, from_z, from_x, from_y, from_l = buffers
    rows, width = part.shape[-2:]
    s_s, s_y, s_l = sems.take(), sems.take(), sems.take()
    s_x = [sems.take() for _ in range(3)]
    s_z = [sems.take() for _ in range(3)]
    s_f = [sems.take() for _ in range(3)]
    if split:
        q = rows // 4

        def band(k):
            return (pl.ds(pl.multiple_of(k * q, 16), q), slice(None))
    else:
        q = width // 4

        def band(k):
            return (slice(None), pl.ds(pl.multiple_of(k * q, 128), q))

    here = band(z)
    sems.push(s_s, part.at[:, :, 1 - c], from_sib, pc.sib)
    own = pltpu.make_async_copy(part.at[:, :, c], acc, local_sem)
    own.start()
    yield
    own.wait()
    sems.arrived(s_s, from_sib, pc.sib)
    add_rows(acc, [from_sib], acc.shape)
    if split:
        for j in range(3):
            there = band(pc.zs[j])
            sems.push(s_z[j], acc.at[:, :, *there], from_z.at[j], pc.zdev[j])
        yield
        for j in range(3):
            sems.arrived(s_z[j], from_z.at[j], pc.zdev[j])
        mine = acc.at[:, :, *here]
        add_rows(mine, [from_z.at[j] for j in range(3)], (2, 4, q, width))
        for k in range(3):
            sems.push(s_x[k], acc.at[:, pc.xs[k], *here], from_x.at[k], pc.xdev[k])
        yield
        for k in range(3):
            sems.arrived(s_x[k], from_x.at[k], pc.xdev[k])
        add_rows(acc.at[:, x, *here], [from_x.at[k] for k in range(3)], (2, q, width))
        sems.push(s_y, acc.at[1 - yh, x, *here], from_y, pc.ypair)
        yield
        sems.arrived(s_y, from_y, pc.ypair)
        mine = acc.at[yh, x, *here]
        add_rows(mine, [from_y], (q, width))
    else:
        for k in range(3):
            sems.push(s_x[k], acc.at[:, pc.xs[k]], from_x.at[k], pc.xdev[k])
        yield
        for k in range(3):
            sems.arrived(s_x[k], from_x.at[k], pc.xdev[k])
        add_rows(acc.at[:, x], [from_x.at[k] for k in range(3)], (2, rows, width))
        sems.push(s_y, acc.at[1 - yh, x], from_y, pc.ypair)
        yield
        sems.arrived(s_y, from_y, pc.ypair)
        add_rows(acc.at[yh, x], [from_y], (rows, width))
        for j in range(3):
            there = band(pc.zs[j])
            sems.push(s_z[j], acc.at[yh, x, *there], from_z.at[j], pc.zdev[j])
        yield
        for j in range(3):
            sems.arrived(s_z[j], from_z.at[j], pc.zdev[j])
        mine = acc.at[yh, x, *here]
        add_rows(mine, [from_z.at[j] for j in range(3)], (rows, q))
    sems.push(s_l, mine, from_l, pc.ylo)
    yield
    sems.arrived(s_l, from_l, pc.ylo)
    final[here] = (mine[...].astype(F32) + from_l[...].astype(F32)).astype(BF16)
    for j in range(3):
        sems.push(s_f[j], final.at[here], final.at[here], pc.zdev[j])
    yield
    for j in range(3):
        sems.arrived(s_f[j], final.at[band(pc.zfrom[j])], pc.zdev[j])
    yield


def reduce_kernel(splits, *refs):
    n = len(splits)
    parts, finals = refs[:n], refs[n : 2 * n]
    scratch = refs[2 * n :]
    send, recv, local = scratch[:3]
    buffers = [scratch[3 + 6 * k : 9 + 6 * k] for k in range(n)]
    pc = Places()
    greet([pc.sib, pc.ypair, pc.ylo, *pc.xdev, *pc.zdev])
    sems = Sems(send, recv)
    run_all(
        [
            reduce_steps(pc, sems, local.at[k], parts[k], finals[k], buffers[k], splits[k])
            for k in range(n)
        ]
    )
    sems.finish()


def reduce_grads(parts, splits, collective_id):
    n = len(parts)
    scratch = [
        pltpu.SemaphoreType.DMA((n * REDUCE_SEMS,)),
        pltpu.SemaphoreType.DMA((n * REDUCE_SEMS,)),
        pltpu.SemaphoreType.DMA((n,)),
    ]
    for p, s in zip(parts, splits):
        scratch += reduce_scratch(*p.shape[-2:], s)
    return pl.pallas_call(
        functools.partial(reduce_kernel, splits),
        out_shape=[jax.ShapeDtypeStruct(p.shape[-2:], p.dtype) for p in parts],
        in_specs=[pl.BlockSpec(memory_space=pl.ANY)] * n,
        out_specs=[pl.BlockSpec(memory_space=pltpu.VMEM)] * n,
        scratch_shapes=scratch,
        compiler_params=pltpu.CompilerParams(
            collective_id=collective_id, has_side_effects=True, vmem_limit_bytes=60 << 20
        ),
    )(*parts)


def ctx_places():
    f, t = lax.axis_index("fsdp"), lax.axis_index("ctx")
    return t, [((t + k) % 8, (f, (t + k) % 8)) for k in range(1, 8)]


def spread_kernel(block, out, send, recv, local):
    t, others = ctx_places()
    greet([d for _, d in others])
    sems = Sems(send, recv)
    own = pltpu.make_async_copy(block, out.at[t], local)
    own.start()
    for k, (_, d) in enumerate(others):
        sems.push(k, block, out.at[t], d)
    own.wait()
    for k in range(7):
        source, d = others[6 - k]
        sems.arrived(k, out.at[source], d)
    sems.finish()


def spread_blocks(block, collective_id):
    return pl.pallas_call(
        spread_kernel,
        out_shape=jax.ShapeDtypeStruct((8, *block.shape), block.dtype),
        in_specs=[pl.BlockSpec(memory_space=pl.ANY)],
        out_specs=pl.BlockSpec(memory_space=pl.ANY),
        scratch_shapes=[
            pltpu.SemaphoreType.DMA((7,)),
            pltpu.SemaphoreType.DMA((7,)),
            pltpu.SemaphoreType.DMA,
        ],
        compiler_params=pltpu.CompilerParams(
            collective_id=collective_id, has_side_effects=True, vmem_limit_bytes=60 << 20
        ),
    )(block)


def collect_kernel(parts, out, landed, send, recv):
    t, others = ctx_places()
    greet([d for _, d in others])
    sems = Sems(send, recv)
    for k, (there, d) in enumerate(others):
        sems.push(k, parts.at[there], landed.at[k], d)
    for k in range(7):
        sems.arrived(k, landed.at[k], others[6 - k][1])
    rows = out.shape[0]

    def body(i, carry):
        at = pl.ds(pl.multiple_of(i * 16, 16), 16)
        total = parts[t, at].astype(F32)
        for k in range(7):
            total = total + landed[k, at].astype(F32)
        out[at] = total
        return carry

    lax.fori_loop(0, rows // 16, body, 0)
    sems.finish()


def collect_blocks(parts, collective_id):
    return pl.pallas_call(
        collect_kernel,
        out_shape=jax.ShapeDtypeStruct(parts.shape[1:], F32),
        in_specs=[pl.BlockSpec(memory_space=pltpu.VMEM)],
        out_specs=pl.BlockSpec(memory_space=pltpu.VMEM),
        scratch_shapes=[
            pltpu.VMEM((7, *parts.shape[1:]), parts.dtype),
            pltpu.SemaphoreType.DMA((7,)),
            pltpu.SemaphoreType.DMA((7,)),
        ],
        compiler_params=pltpu.CompilerParams(
            collective_id=collective_id, has_side_effects=True, vmem_limit_bytes=60 << 20
        ),
    )(parts)


def rotary_tables(token_positions):
    half = HEAD_WIDTH // 2
    freqs = ROPE_BASE ** (-jnp.arange(half, dtype=F32) * 2.0 / HEAD_WIDTH)
    angles = token_positions.astype(F32)[:, None] * freqs[None, :]
    return jnp.cos(angles)[:, None, :], jnp.sin(angles)[:, None, :]


def rotate(rows, cosine, sine):
    half = HEAD_WIDTH // 2
    heads = rows.reshape(rows.shape[0], -1, HEAD_WIDTH)
    a, b = heads[..., :half], heads[..., half:]
    out = jnp.concatenate([a * cosine - b * sine, b * cosine + a * sine], axis=-1)
    return out.reshape(rows.shape)


def dot(a, b):
    return jnp.dot(a, b, preferred_element_type=F32)


def dot_tn(a, b):
    return lax.dot_general(a, b, (((0,), (0,)), ((), ())), preferred_element_type=F32)


def dot_nt(a, b):
    return lax.dot_general(a, b, (((1,), (1,)), ((), ())), preferred_element_type=F32)


def norm_scale(rows):
    return lax.rsqrt(jnp.sum(rows * rows, axis=-1, keepdims=True) * (1.0 / WIDTH) + EPS)


def norm_back(grad_normed, rows, scale, gain):
    unit = rows * scale
    grad_gain = jnp.sum(grad_normed * unit, axis=0)
    grad_unit = grad_normed * gain
    mean = jnp.sum(grad_unit * unit, axis=-1, keepdims=True) * (1.0 / WIDTH)
    return scale * (grad_unit - unit * mean), grad_gain


def head_scores(query_head, keys_head, token_positions):
    scores = jnp.einsum("gle,me->glm", query_head, keys_head, preferred_element_type=F32)
    scores = scores * HEAD_WIDTH ** (-0.5)
    causal = token_positions[:, None] >= jnp.arange(keys_head.shape[0], dtype=jnp.int32)[None, :]
    return jnp.where(causal, scores, -1e30)


def split_heads(rows):
    return jnp.moveaxis(rows.reshape(rows.shape[0], KEY_VALUE_HEADS, GROUP, HEAD_WIDTH), 0, 2)


def join_heads(heads):
    return jnp.moveaxis(heads, 2, 0).reshape(heads.shape[2], QUERY_HEADS * HEAD_WIDTH)


def on_device(
    tokens,
    attn_gain,
    w_query,
    key_weight,
    value_weight,
    w_out,
    ffn_gain,
    w_gate,
    w_up,
    w_down,
    d_out,
):
    block = tokens.shape[1]
    token_positions = lax.axis_index("ctx") * block + jnp.arange(block, dtype=jnp.int32)
    cosine, sine = rotary_tables(token_positions)
    factor = HEAD_WIDTH ** (-0.5)
    feature = jnp.arange(WIDTH, dtype=jnp.int32)
    place_of = feature // ROWS * PAD + feature % ROWS
    select = (place_of[:, None] == jnp.arange(PADDED, dtype=jnp.int32)[None, :]).astype(BF16)

    pad_rows = ((0, PAD - ROWS), (0, 0))
    qkv_shard = jnp.pad(
        jnp.concatenate(
            [w_query, key_weight, value_weight, attn_gain[:, None], ffn_gain[:, None]], axis=1
        ),
        ((0, PAD - ROWS), (0, QKV_WIDTH - WIDTH - 2 * KV_WIDTH - 2)),
    )
    out_shard = jnp.pad(dot(w_out, select).astype(BF16), pad_rows)
    gate_shard = jnp.pad(w_gate, pad_rows)
    up_shard = jnp.pad(w_up, pad_rows)
    down_shard = dot(w_down, select).astype(BF16)

    qkv_w, out_w = gather_weights((qkv_shard, out_shard), (True, False), 0)
    qkv_w, out_w = qkv_w.reshape(PADDED, QKV_WIDTH), out_w.reshape(PADDED, PADDED)
    gains = qkv_w[:, WIDTH + 2 * KV_WIDTH : WIDTH + 2 * KV_WIDTH + 2].astype(F32)
    gain_one, gain_two = gains[:, 0], gains[:, 1]

    flat = dot(tokens[0], select)
    grad_flat = dot(d_out[0], select).astype(BF16)
    scale_one = norm_scale(flat)
    normed = (flat * scale_one * gain_one).astype(BF16)
    qkv = dot(normed, qkv_w)
    query = rotate(qkv[:, :WIDTH], cosine, sine).astype(BF16)
    keys = rotate(qkv[:, WIDTH : WIDTH + KV_WIDTH], cosine, sine).astype(BF16)
    values = qkv[:, WIDTH + KV_WIDTH : WIDTH + 2 * KV_WIDTH].astype(BF16)
    kv = spread_blocks(jnp.concatenate([keys, values], axis=1), 1)
    kv = kv.reshape(8 * block, 2 * KV_WIDTH)
    gate_w, up_w, down_w = gather_weights(
        (gate_shard, up_shard, down_shard), (True, True, False), 2
    )
    gate_w, up_w = gate_w.reshape(PADDED, -1), up_w.reshape(PADDED, -1)
    down_w = down_w.reshape(-1, PADDED)

    query_heads = split_heads(query)
    kv_heads = jnp.moveaxis(kv.reshape(8 * block, 2, KEY_VALUE_HEADS, HEAD_WIDTH), 0, 2)
    keys_heads, values_heads = kv_heads[0], kv_heads[1]

    def head_forward(operands):
        query_head, keys_head, values_head = operands
        scores = head_scores(query_head, keys_head, token_positions)
        peak = jnp.max(scores, axis=-1, keepdims=True)
        logsum = peak + jnp.log(jnp.sum(jnp.exp(scores - peak), axis=-1, keepdims=True))
        probs_low = jnp.exp(scores - logsum).astype(BF16)
        mixed = jnp.einsum("glm,me->gle", probs_low, values_head, preferred_element_type=F32)
        return mixed.astype(BF16), logsum

    mixed_heads, logsums = lax.map(head_forward, (query_heads, keys_heads, values_heads))
    mixed = dot(join_heads(mixed_heads), select).astype(BF16)

    resid = flat + dot(mixed, out_w)
    scale_two = norm_scale(resid)
    normed_two = (resid * scale_two * gain_two).astype(BF16)
    gate = dot(normed_two, gate_w)
    up = dot(normed_two, up_w)
    sigmoid = jax.nn.sigmoid(gate)
    swish = gate * sigmoid
    hidden = (swish * up).astype(BF16)
    output = (resid + dot(hidden, down_w)).astype(BF16)
    output = dot_nt(output, select).astype(BF16)
    grad_down = dot_tn(hidden, grad_flat)
    grad_hidden = dot_nt(grad_flat, down_w)
    grad_gate_v = (grad_hidden * up * sigmoid * (1.0 + gate * (1.0 - sigmoid))).astype(BF16)
    grad_up_v = (grad_hidden * swish).astype(BF16)
    grad_gate = dot_tn(normed_two, grad_gate_v)
    grad_up = dot_tn(normed_two, grad_up_v)
    grad_normed_two = dot_nt(grad_gate_v, gate_w) + dot_nt(grad_up_v, up_w)
    resid_term, grad_gain_two = norm_back(grad_normed_two, resid, scale_two, gain_two)
    grad_resid = grad_flat.astype(F32) + resid_term
    grad_branch = grad_resid.astype(BF16)
    grad_out = dot_tn(mixed, grad_branch)
    grad_mixed = dot_nt(dot_nt(grad_branch, out_w).astype(BF16), select).astype(BF16)
    ffn = (
        grad_gate.astype(BF16).reshape(2, 4, 2, PAD, -1),
        grad_up.astype(BF16).reshape(2, 4, 2, PAD, -1),
        grad_down.astype(BF16).reshape(2, 4, 2, -1, PADDED),
    )
    sum_gate, sum_up, sum_down = reduce_grads(ffn, (True, True, False), 3)

    def head_backward(operands):
        query_head, keys_head, values_head, grad_head, logsum = operands
        scores = head_scores(query_head, keys_head, token_positions)
        probs = jnp.exp(scores - logsum)
        probs_low = probs.astype(BF16)
        grad_probs = jnp.einsum("gle,me->glm", grad_head, values_head, preferred_element_type=F32)
        grad_values = jnp.einsum("glm,gle->me", probs_low, grad_head, preferred_element_type=F32)
        grad_scores = probs * (grad_probs - jnp.sum(probs * grad_probs, axis=-1, keepdims=True))
        grad_scores = grad_scores.astype(BF16)
        grad_query = jnp.einsum("glm,me->gle", grad_scores, keys_head, preferred_element_type=F32)
        grad_keys = jnp.einsum("glm,gle->me", grad_scores, query_head, preferred_element_type=F32)
        return grad_query * factor, grad_keys * factor, grad_values

    grad_query_heads, grad_keys_heads, grad_values_heads = lax.map(
        head_backward,
        (query_heads, keys_heads, values_heads, split_heads(grad_mixed), logsums),
    )
    grad_kv = jnp.stack([grad_keys_heads, grad_values_heads]).astype(BF16)
    grad_kv = jnp.moveaxis(grad_kv, 2, 0).reshape(8, block, 2 * KV_WIDTH)
    grad_kv = collect_blocks(grad_kv, 4)
    grad_query = rotate(join_heads(grad_query_heads), cosine, -sine)
    grad_keys = rotate(grad_kv[:, :KV_WIDTH], cosine, -sine)
    grad_qkv = jnp.concatenate([grad_query, grad_keys, grad_kv[:, KV_WIDTH:]], axis=1).astype(BF16)
    grad_qkv_w = dot_tn(normed, grad_qkv)
    grad_normed = dot_nt(grad_qkv, qkv_w[:, : WIDTH + 2 * KV_WIDTH])
    token_term, grad_gain_one = norm_back(grad_normed, flat, scale_one, gain_one)
    d_tokens = dot_nt((grad_resid + token_term).astype(BF16), select).astype(BF16)
    qkv_part = jnp.concatenate(
        [
            grad_qkv_w,
            grad_gain_one[:, None],
            grad_gain_two[:, None],
            jnp.zeros((PADDED, QKV_WIDTH - WIDTH - 2 * KV_WIDTH - 2), F32),
        ],
        axis=1,
    ).astype(BF16)
    attn = (
        qkv_part.reshape(2, 4, 2, PAD, QKV_WIDTH),
        grad_out.astype(BF16).reshape(2, 4, 2, PAD, PADDED),
    )
    sum_qkv, sum_out = reduce_grads(attn, (True, False), 5)
    sum_qkv = sum_qkv[:ROWS].astype(F32)
    ends = (WIDTH, WIDTH + KV_WIDTH, WIDTH + 2 * KV_WIDTH)
    return (
        output[None],
        d_tokens[None],
        sum_qkv[:, ends[2]],
        sum_qkv[:, : ends[0]],
        sum_qkv[:, ends[0] : ends[1]],
        sum_qkv[:, ends[1] : ends[2]],
        dot_nt(sum_out[:ROWS], select),
        sum_qkv[:, ends[2] + 1],
        sum_gate[:ROWS].astype(F32),
        sum_up[:ROWS].astype(F32),
        dot_nt(sum_down, select),
    )


def solution(mesh):
    rows, whole, line = P("fsdp", None), P("fsdp", "ctx", None), P("fsdp")
    weights = (line, rows, rows, rows, rows, line, rows, rows, rows)
    return jax.shard_map(
        on_device,
        mesh=mesh,
        in_specs=(whole, *weights, whole),
        out_specs=(whole, whole, *weights),
        check_vma=False,
    )
```

```python
import functools
import math

import jax
import jax.numpy as jnp
from jax import lax
from jax.experimental import pallas as pl
from jax.experimental.pallas import tpu as pltpu
from jax.sharding import PartitionSpec as P

QUERY_HEADS = 15
KEY_VALUE_HEADS = 5
HEAD_WIDTH = 64
GROUP = QUERY_HEADS // KEY_VALUE_HEADS
WIDTH = 960
ROWS = 60
PAD = 64
SHARDS = 16
PADDED = SHARDS * PAD
KV_WIDTH = KEY_VALUE_HEADS * HEAD_WIDTH
QKV_WIDTH = 1664

EPS = 1e-05
ROPE_BASE = 10000.0
MESH = pl.DeviceIdType.MESH
BF16 = jnp.bfloat16
F32 = jnp.float32


def place():
    f, t = lax.axis_index("fsdp"), lax.axis_index("ctx")
    return f // 8, (f // 2) % 4, f % 2, t // 2, t % 2


def device(yh, x, c, z, yl):
    return ((yh * 4 + x) * 2 + c, z * 2 + yl)


class Places:
    def __init__(self):
        yh, x, c, z, yl = place()
        self.yh, self.x, self.c, self.z, self.yl = yh, x, c, z, yl
        self.sib = device(yh, x, 1 - c, z, yl)
        self.ypair = device(1 - yh, x, c, z, 1 - yl)
        self.ylo = device(yh, x, c, z, 1 - yl)
        self.xs = [(x + 1) % 4, (x + 3) % 4, (x + 2) % 4]
        self.zs = [(z + 1) % 4, (z + 3) % 4, (z + 2) % 4]
        self.xdev = [device(yh, k, c, z, yl) for k in self.xs]
        self.zdev = [device(yh, x, c, k, yl) for k in self.zs]
        self.xfrom = [self.xs[1], self.xs[0], self.xs[2]]
        self.zfrom = [self.zs[1], self.zs[0], self.zs[2]]


def greet(devices):
    barrier = pltpu.get_barrier_semaphore()
    for d in devices:
        pl.semaphore_signal(barrier, inc=1, device_id=d, device_id_type=MESH)
    pl.semaphore_wait(barrier, len(devices))


class Sems:
    def __init__(self, send, recv):
        self.send, self.recv, self.at, self.open = send, recv, 0, []

    def take(self, count=1):
        at = self.at
        self.at += count
        return at

    def push(self, slot, src, dst, dev):
        copy = pltpu.make_async_remote_copy(
            src_ref=src,
            dst_ref=dst,
            send_sem=self.send.at[slot],
            recv_sem=self.recv.at[slot],
            device_id=dev,
            device_id_type=MESH,
        )
        copy.start()
        self.open.append(copy)

    def arrived(self, slot, dst, dev):
        pltpu.make_async_remote_copy(
            src_ref=dst,
            dst_ref=dst,
            send_sem=self.send.at[slot],
            recv_sem=self.recv.at[slot],
            device_id=dev,
            device_id_type=MESH,
        ).wait_recv()

    def finish(self):
        for copy in self.open:
            copy.wait_send()
        self.open = []


GATHER_SEMS = 24


def gather_steps(pc, sems, local_sem, shard, out, split):
    rows = shard.shape[0]
    quarter = rows // 4
    yh, x, c, z = pc.yh, pc.x, pc.c, pc.z
    s_y = sems.take()
    s_x = [[sems.take() for _ in range(2)] for _ in range(3)]
    s_z = [[sems.take() for _ in range(3)] for _ in range(3)] if split else None
    s_s = [sems.take() for _ in range(4)]
    band = pl.ds(pl.multiple_of(z * quarter, 16), quarter) if split else pl.ds(0, rows)

    own = pltpu.make_async_copy(shard, out.at[yh, x, c], local_sem)
    own.start()
    sems.push(s_y, shard, out.at[yh, x, c], pc.ypair)
    for k in (0, 1, 2):
        sems.push(s_x[k][0], shard.at[band], out.at[yh, x, c, band], pc.xdev[k])
    yield
    sems.arrived(s_y, out.at[1 - yh, x, c], pc.ypair)
    for k in (0, 1, 2):
        piece = out.at[1 - yh, x, c, band]
        sems.push(s_x[k][1], piece, piece, pc.xdev[k])
    own.wait()
    sems.push(s_s[3], out.at[:, x, c], out.at[:, x, c], pc.sib)
    yield
    for k in (0, 1, 2):
        far = pc.xfrom[k]
        sems.arrived(s_x[k][0], out.at[yh, far, c, band], pc.xdev[k])
        sems.arrived(s_x[k][1], out.at[1 - yh, far, c, band], pc.xdev[k])
        if split:
            piece = out.at[:, far, c, band]
            for j in range(3):
                sems.push(s_z[k][j], piece, piece, pc.zdev[j])
        else:
            sems.push(s_s[k], out.at[:, far, c], out.at[:, far, c], pc.sib)
    yield
    if split:
        for k in (0, 1, 2):
            far = pc.xfrom[k]
            for j in range(3):
                there = pl.ds(pl.multiple_of(pc.zfrom[j] * quarter, 16), quarter)
                sems.arrived(s_z[k][j], out.at[:, far, c, there], pc.zdev[j])
            sems.push(s_s[k], out.at[:, far, c], out.at[:, far, c], pc.sib)
        yield
    for k in (0, 1, 2, 3):
        far = x if k == 3 else pc.xfrom[k]
        sems.arrived(s_s[k], out.at[:, far, 1 - c], pc.sib)
    yield


def run_all(steps):
    live = list(steps)
    while live:
        for s in list(live):
            try:
                next(s)
            except StopIteration:
                live.remove(s)


REDUCE_SEMS = 24


def add_rows(dst, terms, shape):
    lead, rows = shape[:-2], shape[-2]
    blocks = rows // 16
    count = math.prod(lead) * blocks

    def body(i, carry):
        idx, rest = [], i // blocks
        for size in reversed(lead):
            idx.append(rest % size)
            rest = rest // size
        idx = tuple(reversed(idx))
        at = (*idx, pl.ds(pl.multiple_of((i % blocks) * 16, 16), 16))
        total = dst[at].astype(F32)
        for term in terms:
            total = total + term[at].astype(F32)
        dst[at] = total.astype(BF16)
        return carry

    lax.fori_loop(0, count, body, 0)


def reduce_scratch(rows, width, split):
    q = rows // 4
    buffers = [pltpu.VMEM((2, 4, rows, width), BF16)] * 2
    if split:
        buffers += [
            pltpu.VMEM((3, 2, 4, q, width), BF16),
            pltpu.VMEM((3, 2, q, width), BF16),
            pltpu.VMEM((q, width), BF16),
            pltpu.VMEM((q, width), BF16),
        ]
    else:
        w = width // 4
        buffers += [
            pltpu.VMEM((3, rows, w), BF16),
            pltpu.VMEM((3, 2, rows, width), BF16),
            pltpu.VMEM((rows, width), BF16),
            pltpu.VMEM((rows, w), BF16),
        ]
    return buffers


def reduce_steps(pc, sems, local_sem, part, final, buffers, split):
    yh, x, c, z = pc.yh, pc.x, pc.c, pc.z
    acc, from_sib, from_z, from_x, from_y, from_l = buffers
    rows, width = part.shape[-2:]
    s_s, s_y, s_l = sems.take(), sems.take(), sems.take()
    s_x = [sems.take() for _ in range(3)]
    s_z = [sems.take() for _ in range(3)]
    s_f = [sems.take() for _ in range(3)]
    if split:
        q = rows // 4

        def band(k):
            return (pl.ds(pl.multiple_of(k * q, 16), q), slice(None))
    else:
        q = width // 4

        def band(k):
            return (slice(None), pl.ds(pl.multiple_of(k * q, 128), q))

    here = band(z)
    sems.push(s_s, part.at[:, :, 1 - c], from_sib, pc.sib)
    own = pltpu.make_async_copy(part.at[:, :, c], acc, local_sem)
    own.start()
    yield
    own.wait()
    sems.arrived(s_s, from_sib, pc.sib)
    add_rows(acc, [from_sib], acc.shape)
    if split:
        for j in range(3):
            there = band(pc.zs[j])
            sems.push(s_z[j], acc.at[:, :, *there], from_z.at[j], pc.zdev[j])
        yield
        for j in range(3):
            sems.arrived(s_z[j], from_z.at[j], pc.zdev[j])
        mine = acc.at[:, :, *here]
        add_rows(mine, [from_z.at[j] for j in range(3)], (2, 4, q, width))
        for k in range(3):
            sems.push(s_x[k], acc.at[:, pc.xs[k], *here], from_x.at[k], pc.xdev[k])
        yield
        for k in range(3):
            sems.arrived(s_x[k], from_x.at[k], pc.xdev[k])
        add_rows(acc.at[:, x, *here], [from_x.at[k] for k in range(3)], (2, q, width))
        sems.push(s_y, acc.at[1 - yh, x, *here], from_y, pc.ypair)
        yield
        sems.arrived(s_y, from_y, pc.ypair)
        mine = acc.at[yh, x, *here]
        add_rows(mine, [from_y], (q, width))
    else:
        for k in range(3):
            sems.push(s_x[k], acc.at[:, pc.xs[k]], from_x.at[k], pc.xdev[k])
        yield
        for k in range(3):
            sems.arrived(s_x[k], from_x.at[k], pc.xdev[k])
        add_rows(acc.at[:, x], [from_x.at[k] for k in range(3)], (2, rows, width))
        sems.push(s_y, acc.at[1 - yh, x], from_y, pc.ypair)
        yield
        sems.arrived(s_y, from_y, pc.ypair)
        add_rows(acc.at[yh, x], [from_y], (rows, width))
        for j in range(3):
            there = band(pc.zs[j])
            sems.push(s_z[j], acc.at[yh, x, *there], from_z.at[j], pc.zdev[j])
        yield
        for j in range(3):
            sems.arrived(s_z[j], from_z.at[j], pc.zdev[j])
        mine = acc.at[yh, x, *here]
        add_rows(mine, [from_z.at[j] for j in range(3)], (rows, q))
    sems.push(s_l, mine, from_l, pc.ylo)
    yield
    sems.arrived(s_l, from_l, pc.ylo)
    final[here] = (mine[...].astype(F32) + from_l[...].astype(F32)).astype(BF16)
    for j in range(3):
        sems.push(s_f[j], final.at[here], final.at[here], pc.zdev[j])
    yield
    for j in range(3):
        sems.arrived(s_f[j], final.at[band(pc.zfrom[j])], pc.zdev[j])
    yield


def ctx_places():
    f, t = lax.axis_index("fsdp"), lax.axis_index("ctx")
    return t, [((t + k) % 8, (f, (t + k) % 8)) for k in range(1, 8)]


def dot(a, b):
    return jnp.dot(a, b, preferred_element_type=F32)


def dot_tn(a, b):
    return lax.dot_general(a, b, (((0,), (0,)), ((), ())), preferred_element_type=F32)


def dot_nt(a, b):
    return lax.dot_general(a, b, (((1,), (1,)), ((), ())), preferred_element_type=F32)


def norm_scale(rows):
    return lax.rsqrt(jnp.sum(rows * rows, axis=-1, keepdims=True) * (1.0 / WIDTH) + EPS)


def norm_back(grad_normed, rows, scale, gain):
    unit = rows * scale
    grad_gain = jnp.sum(grad_normed * unit, axis=0)
    grad_unit = grad_normed * gain
    mean = jnp.sum(grad_unit * unit, axis=-1, keepdims=True) * (1.0 / WIDTH)
    return scale * (grad_unit - unit * mean), grad_gain


BLOCK = 256
PAIR = 2 * HEAD_WIDTH
STACK = GROUP * BLOCK
TILES = QKV_WIDTH // PAIR
FACTOR = HEAD_WIDTH ** (-0.5)


def low_half(shape):
    return lax.broadcasted_iota(jnp.int32, shape, 1) % PAIR < HEAD_WIDTH


def swap_halves(tile):
    lane = lax.broadcasted_iota(jnp.int32, tile.shape, 1) % HEAD_WIDTH
    half = HEAD_WIDTH // 2
    return jnp.where(
        lane < half, pltpu.roll(tile, PAIR - half, 1), pltpu.roll(tile, half, 1)
    )


def flip(a):
    return a.astype(F32).T.astype(a.dtype)


def advance(*steps):
    for s in steps:
        next(s, None)


def drain(*steps):
    run_all(steps)


def forward_kernel(
    flat,
    cosine,
    sine,
    qkv_shard,
    out_shard,
    gate_shard,
    up_shard,
    down_shard,
    qkv_w,
    out_w,
    gate_w,
    up_w,
    down_w,
    normed,
    q_t,
    kv_all,
    o_t,
    lse,
    mixed,
    peak,
    wide,
    send,
    recv,
    local,
    kv_send,
    kv_recv,
):
    pc = Places()
    t, others = ctx_places()
    greet([pc.sib, pc.ypair, *pc.xdev, *[d for _, d in others]])
    sems, kv_sems = Sems(send, recv), Sems(kv_send, kv_recv)
    g_qkv = gather_steps(pc, sems, local.at[0], qkv_shard, qkv_w, True)
    g_out = gather_steps(pc, sems, local.at[1], out_shard, out_w, False)
    g_gate = gather_steps(pc, sems, local.at[2], gate_shard, gate_w, True)
    g_up = gather_steps(pc, sems, local.at[3], up_shard, up_w, True)
    g_down = gather_steps(pc, sems, local.at[4], down_shard, down_w, False)
    advance(g_qkv, g_out)
    x = flat[...]
    scale = norm_scale(x)
    advance(g_qkv, g_out)
    advance(g_qkv)
    advance(g_gate, g_up)
    advance(g_qkv, g_out)
    advance(g_gate, g_up)
    advance(g_qkv)

    pick = lax.broadcasted_iota(jnp.int32, (8, PAIR), 1) == HEAD_WIDTH
    last = qkv_w[:, :, :, :, QKV_WIDTH - PAIR :].reshape(PADDED, PAIR)
    gain = dot_nt(pick.astype(BF16), last)[0:1]
    normed[...] = (x * scale * gain).astype(BF16)
    rows = normed[...]
    cos, sin = cosine[...], sine[...]
    low = low_half((BLOCK, PAIR))
    for tile in range(TILES):
        w = qkv_w[:, :, :, :, tile * PAIR : (tile + 1) * PAIR].reshape(PADDED, PAIR)
        product = dot(rows, w)
        if tile < 10:
            product = product * cos + swap_halves(product) * sin
        if tile < 8:
            turned = (product * FACTOR).T.astype(BF16)
            for side in range(2):
                head = 2 * tile + side
                if head < QUERY_HEADS:
                    h, g = head // GROUP, head % GROUP
                    q_t[h, 0:HEAD_WIDTH, g * BLOCK : (g + 1) * BLOCK] = turned[
                        side * HEAD_WIDTH : (side + 1) * HEAD_WIDTH
                    ]
                    q_t[h, HEAD_WIDTH:PAIR, g * BLOCK : (g + 1) * BLOCK] = jnp.zeros(
                        (HEAD_WIDTH, BLOCK), BF16
                    )
        if tile >= 7:
            wide[tile - 7] = product
    for h in range(KEY_VALUE_HEADS):
        k_tile, k_high = (h + 1) // 2, (h + 1) % 2
        v_tile, v_high = 3 + h // 2, h % 2
        k_part, v_part = wide[k_tile], wide[v_tile]
        if k_high:
            k_part = pltpu.roll(k_part, HEAD_WIDTH, 1)
        if not v_high:
            v_part = pltpu.roll(v_part, HEAD_WIDTH, 1)
        kv_all[t, h] = jnp.where(low, k_part, v_part).astype(BF16)
    for k in range(1, 8):

        @pl.when(t + k < 8)
        def _(k=k):
            kv_sems.push(k - 1, kv_all.at[t], kv_all.at[t], others[k - 1][1])

    advance(g_down)

    peak[...] = jnp.full_like(peak, -1e30)
    o_t[...] = jnp.zeros_like(o_t)

    def visit(j, diagonal):
        def per_head(h, carry):
            kv = kv_all[j, h]
            kv_t = flip(kv)
            ones = lax.broadcasted_iota(jnp.int32, (PAIR, BLOCK), 0) < HEAD_WIDTH
            ones_v = jnp.where(ones, 1.0, kv_t.astype(F32)).astype(BF16)
            scores = dot(kv, q_t[h])
            if diagonal:
                key = lax.broadcasted_iota(jnp.int32, (BLOCK, STACK), 0)
                query = lax.broadcasted_iota(jnp.int32, (BLOCK, STACK), 1) % BLOCK
                scores = jnp.where(key <= query, scores, -1e30)
            old = peak[h]
            new = jnp.maximum(old, jnp.max(scores, axis=0, keepdims=True))
            probs = jnp.exp(scores - new[0:1]).astype(BF16)
            o_t[h] = o_t[h] * jnp.exp(old - new)[0:1] + dot(ones_v, probs)
            peak[h] = new
            return carry

        lax.fori_loop(0, KEY_VALUE_HEADS, per_head, 0)

    visit(t, True)
    for k in range(1, 8):

        @pl.when(t - k >= 0)
        def _(k=k):
            kv_sems.arrived(k - 1, kv_all.at[t - k], others[k - 1][1])
            visit(t - k, False)

        if k == 1:
            advance(g_gate, g_up, g_down)
        if k == 3:
            advance(g_gate, g_up, g_down)

    for h in range(KEY_VALUE_HEADS):
        total = o_t[h, 0:1]
        o_t[h] = o_t[h] * (1.0 / total)
        lse[h] = peak[h] + jnp.log(total)
    for tile in range(8):
        parts = []
        for head in (2 * tile, min(2 * tile + 1, QUERY_HEADS - 1)):
            h, g = head // GROUP, head % GROUP
            parts.append(o_t[h, HEAD_WIDTH:PAIR, g * BLOCK : (g + 1) * BLOCK])
        joined = jnp.concatenate(parts, axis=0).T.astype(BF16)
        if tile < 7:
            mixed[:, tile * PAIR : (tile + 1) * PAIR] = joined
        else:
            mixed[:, tile * PAIR : tile * PAIR + HEAD_WIDTH] = joined[:, :HEAD_WIDTH]
    drain(g_gate, g_up, g_down, g_out)
    for k in range(1, 8):

        @pl.when(t + k < 8)
        def _(k=k):
            pltpu.make_async_remote_copy(
                src_ref=kv_all.at[t],
                dst_ref=kv_all.at[t],
                send_sem=kv_send.at[k - 1],
                recv_sem=kv_recv.at[k - 1],
                device_id=others[k - 1][1],
                device_id_type=MESH,
            ).wait_send()

    sems.finish()


def forward(flat, cosine, sine, shards, collective_id):
    vmem, hbm = pl.BlockSpec(memory_space=pltpu.VMEM), pl.BlockSpec(memory_space=pl.ANY)
    gathered = [jax.ShapeDtypeStruct((2, 4, 2, *s.shape), BF16) for s in shards]
    return pl.pallas_call(
        forward_kernel,
        out_shape=[
            *gathered,
            jax.ShapeDtypeStruct((BLOCK, PADDED), BF16),
            jax.ShapeDtypeStruct((KEY_VALUE_HEADS, PAIR, STACK), BF16),
            jax.ShapeDtypeStruct((8, KEY_VALUE_HEADS, BLOCK, PAIR), BF16),
            jax.ShapeDtypeStruct((KEY_VALUE_HEADS, PAIR, STACK), F32),
            jax.ShapeDtypeStruct((KEY_VALUE_HEADS, 8, STACK), F32),
            jax.ShapeDtypeStruct((BLOCK, WIDTH), BF16),
        ],
        in_specs=[vmem, vmem, vmem] + [hbm] * 5,
        out_specs=[vmem] + [hbm] * 4 + [vmem] * 6,
        scratch_shapes=[
            pltpu.VMEM((KEY_VALUE_HEADS, 8, STACK), F32),
            pltpu.VMEM((TILES - 7, BLOCK, PAIR), F32),
            pltpu.SemaphoreType.DMA((5 * GATHER_SEMS,)),
            pltpu.SemaphoreType.DMA((5 * GATHER_SEMS,)),
            pltpu.SemaphoreType.DMA((5,)),
            pltpu.SemaphoreType.DMA((7,)),
            pltpu.SemaphoreType.DMA((7,)),
        ],
        compiler_params=pltpu.CompilerParams(
            collective_id=collective_id, has_side_effects=True, vmem_limit_bytes=60 << 20
        ),
    )(flat, cosine, sine, *shards)


def backward_kernel(
    gate_part,
    up_part,
    down_part,
    out_part,
    flat,
    grad_resid,
    gain_row,
    cosine,
    sine,
    qkv_w,
    normed,
    q_t,
    kv_all,
    o_t,
    lse,
    grad_mixed,
    gate_sum,
    up_sum,
    down_sum,
    out_sum,
    qkv_sum,
    d_tokens,
    do_t,
    do_n,
    q_n,
    dq_t,
    delta,
    dkv,
    landed,
    grad_qkv,
    qkv_part,
    send,
    recv,
    local,
    kv_send,
    kv_recv,
    *buffers,
):
    pc = Places()
    t, others = ctx_places()
    greet([pc.sib, pc.ypair, *pc.xdev, *[d for _, d in others]])
    sems, kv_sems = Sems(send, recv), Sems(kv_send, kv_recv)
    parts = (gate_part, up_part, down_part, out_part, qkv_part)
    finals = (gate_sum, up_sum, down_sum, out_sum, qkv_sum)
    reduces = [
        reduce_steps(
            pc,
            sems,
            local.at[k],
            parts[k],
            finals[k],
            buffers[6 * k : 6 * k + 6],
            REDUCE_SPLITS[k],
        )
        for k in range(5)
    ]
    early, late = reduces[:4], reduces[4]
    advance(*early)

    do_t[...] = jnp.zeros_like(do_t)
    for tile in range(8):
        if tile < 7:
            turned = flip(grad_mixed[:, tile * PAIR : (tile + 1) * PAIR])
        else:
            turned = flip(grad_mixed[:, tile * PAIR : tile * PAIR + HEAD_WIDTH])
        for side in range(2):
            head = 2 * tile + side
            if head < QUERY_HEADS:
                h, g = head // GROUP, head % GROUP
                do_t[h, HEAD_WIDTH:PAIR, g * BLOCK : (g + 1) * BLOCK] = turned[
                    side * HEAD_WIDTH : (side + 1) * HEAD_WIDTH
                ]
    for h in range(KEY_VALUE_HEADS):
        do_n[h] = flip(do_t[h])
        q_n[h] = flip(q_t[h])
        both = do_t[h, HEAD_WIDTH:PAIR].astype(F32) * o_t[h, HEAD_WIDTH:PAIR]
        delta[h] = jnp.broadcast_to(jnp.sum(both, axis=0, keepdims=True), (8, STACK))
    dq_t[...] = jnp.zeros_like(dq_t)

    def visit(j, diagonal):
        def per_head(h, carry):
            kv = kv_all[j, h]
            scores = dot(kv, q_t[h])
            if diagonal:
                key = lax.broadcasted_iota(jnp.int32, (BLOCK, STACK), 0)
                query = lax.broadcasted_iota(jnp.int32, (BLOCK, STACK), 1) % BLOCK
                scores = jnp.where(key <= query, scores, -1e30)
            probs = jnp.exp(scores - lse[h][0:1])
            grad_probs = dot(kv, do_t[h])
            grad_scores = (probs * (grad_probs - delta[h][0:1])).astype(BF16)
            both = dot(grad_scores, q_n[h]) + dot(probs.astype(BF16), do_n[h])
            dkv[j, h] = both.astype(BF16)
            dq_t[h] += dot(flip(kv), grad_scores)
            return carry

        lax.fori_loop(0, KEY_VALUE_HEADS, per_head, 0)

    for k in range(1, 8):

        @pl.when(t - k >= 0)
        def _(k=k):
            visit(t - k, False)
            kv_sems.push(k - 1, dkv.at[t - k], landed.at[k - 1], others[7 - k][1])

        if k in (2, 4, 6):
            advance(*early)
    visit(t, True)
    advance(*early)

    cos, sin = cosine[...], sine[...]
    for tile in range(8):
        pieces = []
        for head in (2 * tile, min(2 * tile + 1, QUERY_HEADS - 1)):
            h, g = head // GROUP, head % GROUP
            pieces.append(dq_t[h, 0:HEAD_WIDTH, g * BLOCK : (g + 1) * BLOCK])
        joined = jnp.concatenate(pieces, axis=0).T * FACTOR
        joined = joined * cos - swap_halves(joined) * sin
        grad_qkv[:, tile * PAIR : (tile + 1) * PAIR] = joined.astype(BF16)

    for k in range(1, 8):

        @pl.when(t + k < 8)
        def _(k=k):
            kv_sems.arrived(k - 1, landed.at[k - 1], others[k - 1][1])

    low = low_half((BLOCK, PAIR))
    totals = []
    for h in range(KEY_VALUE_HEADS):

        def add(k, total, h=h):
            return total + landed[k, h].astype(F32)

        totals.append(lax.fori_loop(0, 7 - t, add, dkv[t, h].astype(F32)))
    zero = jnp.zeros((BLOCK, PAIR), F32)

    def turn(tile):
        return tile * cos - swap_halves(tile) * sin

    left = grad_qkv[:, 7 * PAIR : 8 * PAIR].astype(F32)
    first = turn(pltpu.roll(totals[0], HEAD_WIDTH, 1))
    grad_qkv[:, 7 * PAIR : 8 * PAIR] = jnp.where(low, left, first).astype(BF16)
    for n, (a, b) in enumerate(((1, 2), (3, 4))):
        keys = turn(jnp.where(low, totals[a], pltpu.roll(totals[b], HEAD_WIDTH, 1)))
        grad_qkv[:, (8 + n) * PAIR : (9 + n) * PAIR] = keys.astype(BF16)
    for n, (a, b) in enumerate(((0, 1), (2, 3), (4, None))):
        high = zero if b is None else totals[b]
        vals = jnp.where(low, pltpu.roll(totals[a], HEAD_WIDTH, 1), high)
        grad_qkv[:, (10 + n) * PAIR : (11 + n) * PAIR] = vals.astype(BF16)

    x = flat[...]
    scale = norm_scale(x)
    pick = lax.broadcasted_iota(jnp.int32, (8, PAIR), 1) == HEAD_WIDTH
    last = qkv_w[:, :, :, :, QKV_WIDTH - PAIR :].reshape(PADDED, PAIR)
    gain = dot_nt(pick.astype(BF16), last)[0:1]
    grad_normed = dot_nt(grad_qkv[...], qkv_w[...].reshape(PADDED, QKV_WIDTH))
    token_term, grad_gain = norm_back(grad_normed, x, scale, gain)
    d_tokens[...] = (grad_resid[...] + token_term).astype(BF16)
    row = lax.broadcasted_iota(jnp.int32, (8, PADDED), 0)
    gains = jnp.where(row == 0, grad_gain[None, :], jnp.where(row == 1, gain_row[...], 0.0))
    lane = lax.broadcasted_iota(jnp.int32, (8, PAIR), 1)
    which = lax.broadcasted_iota(jnp.int32, (8, PAIR), 0)
    put = (lane == which + HEAD_WIDTH) & (which < 2)
    rows = normed[...]
    for tile in range(TILES):
        product = dot_tn(rows, grad_qkv[:, tile * PAIR : (tile + 1) * PAIR])
        if tile == TILES - 1:
            product = product + dot_tn(gains.astype(BF16), put.astype(BF16))
        qkv_part[:, :, :, :, tile * PAIR : (tile + 1) * PAIR] = product.astype(BF16).reshape(
            2, 4, 2, PAD, PAIR
        )
    drain(late, *early)
    for k in range(1, 8):

        @pl.when(t - k >= 0)
        def _(k=k):
            pltpu.make_async_remote_copy(
                src_ref=dkv.at[t - k],
                dst_ref=landed.at[k - 1],
                send_sem=kv_send.at[k - 1],
                recv_sem=kv_recv.at[k - 1],
                device_id=others[7 - k][1],
                device_id_type=MESH,
            ).wait_send()

    sems.finish()


REDUCE_SPLITS = (True, True, False, False, True)


def backward(parts, values, collective_id):
    vmem, hbm = pl.BlockSpec(memory_space=pltpu.VMEM), pl.BlockSpec(memory_space=pl.ANY)
    qkv_shape = (2, 4, 2, PAD, QKV_WIDTH)
    shapes = [p.shape for p in parts] + [qkv_shape]
    scratch = [
        pltpu.VMEM((KEY_VALUE_HEADS, PAIR, STACK), BF16),
        pltpu.VMEM((KEY_VALUE_HEADS, STACK, PAIR), BF16),
        pltpu.VMEM((KEY_VALUE_HEADS, STACK, PAIR), BF16),
        pltpu.VMEM((KEY_VALUE_HEADS, PAIR, STACK), F32),
        pltpu.VMEM((KEY_VALUE_HEADS, 8, STACK), F32),
        pltpu.VMEM((8, KEY_VALUE_HEADS, BLOCK, PAIR), BF16),
        pltpu.VMEM((7, KEY_VALUE_HEADS, BLOCK, PAIR), BF16),
        pltpu.VMEM((BLOCK, QKV_WIDTH), BF16),
        pltpu.VMEM(qkv_shape, BF16),
        pltpu.SemaphoreType.DMA((5 * REDUCE_SEMS,)),
        pltpu.SemaphoreType.DMA((5 * REDUCE_SEMS,)),
        pltpu.SemaphoreType.DMA((5,)),
        pltpu.SemaphoreType.DMA((7,)),
        pltpu.SemaphoreType.DMA((7,)),
    ]
    for s, split in zip(shapes, REDUCE_SPLITS):
        scratch += reduce_scratch(*s[-2:], split)
    return pl.pallas_call(
        backward_kernel,
        out_shape=[jax.ShapeDtypeStruct(s[-2:], BF16) for s in shapes]
        + [jax.ShapeDtypeStruct((BLOCK, PADDED), BF16)],
        in_specs=[hbm] * 4 + [vmem] * len(values),
        out_specs=[vmem] * 6,
        scratch_shapes=scratch,
        compiler_params=pltpu.CompilerParams(
            collective_id=collective_id, has_side_effects=True, vmem_limit_bytes=63 << 20
        ),
    )(*parts, *values)


def rotary_tables(token_positions):
    half = HEAD_WIDTH // 2
    freqs = ROPE_BASE ** (-jnp.arange(half, dtype=F32) * 2.0 / HEAD_WIDTH)
    angles = token_positions.astype(F32)[:, None] * freqs[None, :]
    cosine, sine = jnp.cos(angles), jnp.sin(angles)
    return (
        jnp.concatenate([cosine] * 4, axis=1),
        jnp.concatenate([-sine, sine] * 2, axis=1),
    )


def on_device(
    tokens,
    attn_gain,
    w_query,
    key_weight,
    value_weight,
    w_out,
    ffn_gain,
    w_gate,
    w_up,
    w_down,
    d_out,
):
    block = tokens.shape[1]
    token_positions = lax.axis_index("ctx") * block + jnp.arange(block, dtype=jnp.int32)
    cosine, sine = rotary_tables(token_positions)
    feature = jnp.arange(WIDTH, dtype=jnp.int32)
    place_of = feature // ROWS * PAD + feature % ROWS
    select = (place_of[:, None] == jnp.arange(PADDED, dtype=jnp.int32)[None, :]).astype(BF16)

    pad_rows = ((0, PAD - ROWS), (0, 0))
    qkv_shard = jnp.pad(
        jnp.concatenate(
            [w_query, key_weight, value_weight, attn_gain[:, None], ffn_gain[:, None]], axis=1
        ),
        ((0, PAD - ROWS), (0, QKV_WIDTH - WIDTH - 2 * KV_WIDTH - 2)),
    )
    out_shard = jnp.pad(dot(w_out, select).astype(BF16), pad_rows)
    gate_shard = jnp.pad(w_gate, pad_rows)
    up_shard = jnp.pad(w_up, pad_rows)
    down_shard = dot(w_down, select).astype(BF16)

    flat = dot(tokens[0], select)
    grad_flat = dot(d_out[0], select).astype(BF16)
    qkv_w, out_w, gate_w, up_w, down_w, normed, q_t, kv_all, o_t, lse, mixed = forward(
        flat, cosine, sine, (qkv_shard, out_shard, gate_shard, up_shard, down_shard), 0
    )
    out_w, gate_w, up_w = (w.reshape(PADDED, -1) for w in (out_w, gate_w, up_w))
    down_w = down_w.reshape(-1, PADDED)
    gain_at = WIDTH + 2 * KV_WIDTH + 1
    gain_two = qkv_w.reshape(PADDED, QKV_WIDTH)[:, gain_at].astype(F32)
    mixed = dot(mixed, select).astype(BF16)

    resid = flat + dot(mixed, out_w)
    scale_two = norm_scale(resid)
    normed_two = (resid * scale_two * gain_two).astype(BF16)
    gate = dot(normed_two, gate_w)
    up = dot(normed_two, up_w)
    sigmoid = jax.nn.sigmoid(gate)
    swish = gate * sigmoid
    hidden = (swish * up).astype(BF16)
    output = (resid + dot(hidden, down_w)).astype(BF16)
    output = dot_nt(output, select).astype(BF16)
    grad_down = dot_tn(hidden, grad_flat)
    grad_hidden = dot_nt(grad_flat, down_w)
    grad_gate_v = (grad_hidden * up * sigmoid * (1.0 + gate * (1.0 - sigmoid))).astype(BF16)
    grad_up_v = (grad_hidden * swish).astype(BF16)
    grad_gate = dot_tn(normed_two, grad_gate_v)
    grad_up = dot_tn(normed_two, grad_up_v)
    grad_normed_two = dot_nt(grad_gate_v, gate_w) + dot_nt(grad_up_v, up_w)
    resid_term, grad_gain_two = norm_back(grad_normed_two, resid, scale_two, gain_two)
    grad_resid = grad_flat.astype(F32) + resid_term
    grad_branch = grad_resid.astype(BF16)
    grad_out = dot_tn(mixed, grad_branch)
    grad_mixed = dot_nt(dot_nt(grad_branch, out_w).astype(BF16), select).astype(BF16)
    parts = (
        grad_gate.astype(BF16).reshape(2, 4, 2, PAD, -1),
        grad_up.astype(BF16).reshape(2, 4, 2, PAD, -1),
        grad_down.astype(BF16).reshape(2, 4, 2, -1, PADDED),
        grad_out.astype(BF16).reshape(2, 4, 2, PAD, PADDED),
    )
    sum_gate, sum_up, sum_down, sum_out, sum_qkv, d_tokens = backward(
        parts,
        (
            flat,
            grad_resid,
            grad_gain_two[None, :],
            cosine,
            sine,
            qkv_w,
            normed,
            q_t,
            kv_all,
            o_t,
            lse,
            grad_mixed,
        ),
        1,
    )
    d_tokens = dot_nt(d_tokens, select).astype(BF16)
    sum_qkv = sum_qkv[:ROWS].astype(F32)
    ends = (WIDTH, WIDTH + KV_WIDTH, WIDTH + 2 * KV_WIDTH)
    return (
        output[None],
        d_tokens[None],
        sum_qkv[:, ends[2]],
        sum_qkv[:, : ends[0]],
        sum_qkv[:, ends[0] : ends[1]],
        sum_qkv[:, ends[1] : ends[2]],
        dot_nt(sum_out[:ROWS], select),
        sum_qkv[:, ends[2] + 1],
        sum_gate[:ROWS].astype(F32),
        sum_up[:ROWS].astype(F32),
        dot_nt(sum_down, select),
    )


def solution(mesh):
    rows, whole, line = P("fsdp", None), P("fsdp", "ctx", None), P("fsdp")
    weights = (line, rows, rows, rows, rows, line, rows, rows, rows)
    return jax.shard_map(
        on_device,
        mesh=mesh,
        in_specs=(whole, *weights, whole),
        out_specs=(whole, whole, *weights),
        check_vma=False,
    )
```

```python
import functools
import math

import jax
import jax.numpy as jnp
from jax import lax
from jax.experimental import pallas as pl
from jax.experimental.pallas import tpu as pltpu
from jax.sharding import PartitionSpec as P

QUERY_HEADS = 15
KEY_VALUE_HEADS = 5
HEAD_WIDTH = 64
GROUP = QUERY_HEADS // KEY_VALUE_HEADS
WIDTH = 960
ROWS = 60
PAD = 64
SHARDS = 16
PADDED = SHARDS * PAD
KV_WIDTH = KEY_VALUE_HEADS * HEAD_WIDTH
Q_TILES = 7
KV_TILES = 6

EPS = 1e-05
ROPE_BASE = 10000.0
MESH = pl.DeviceIdType.MESH
BF16 = jnp.bfloat16
F32 = jnp.float32


def place():
    f, t = lax.axis_index("fsdp"), lax.axis_index("ctx")
    return f // 8, (f // 2) % 4, f % 2, t // 2, t % 2


def device(yh, x, c, z, yl):
    return ((yh * 4 + x) * 2 + c, z * 2 + yl)


class Places:
    def __init__(self):
        yh, x, c, z, yl = place()
        self.yh, self.x, self.c, self.z, self.yl = yh, x, c, z, yl
        self.sib = device(yh, x, 1 - c, z, yl)
        self.ypair = device(1 - yh, x, c, z, 1 - yl)
        self.ylo = device(yh, x, c, z, 1 - yl)
        self.xs = [(x + 1) % 4, (x + 3) % 4, (x + 2) % 4]
        self.zs = [(z + 1) % 4, (z + 3) % 4, (z + 2) % 4]
        self.xdev = [device(yh, k, c, z, yl) for k in self.xs]
        self.zdev = [device(yh, x, c, k, yl) for k in self.zs]
        self.xfrom = [self.xs[1], self.xs[0], self.xs[2]]
        self.zfrom = [self.zs[1], self.zs[0], self.zs[2]]


def greet(devices):
    barrier = pltpu.get_barrier_semaphore()
    for d in devices:
        pl.semaphore_signal(barrier, inc=1, device_id=d, device_id_type=MESH)
    pl.semaphore_wait(barrier, len(devices))


class Sems:
    def __init__(self, send, recv):
        self.send, self.recv, self.at, self.open = send, recv, 0, []

    def take(self, count=1):
        at = self.at
        self.at += count
        return at

    def push(self, slot, src, dst, dev):
        copy = pltpu.make_async_remote_copy(
            src_ref=src,
            dst_ref=dst,
            send_sem=self.send.at[slot],
            recv_sem=self.recv.at[slot],
            device_id=dev,
            device_id_type=MESH,
        )
        copy.start()
        self.open.append(copy)

    def arrived(self, slot, dst, dev):
        pltpu.make_async_remote_copy(
            src_ref=dst,
            dst_ref=dst,
            send_sem=self.send.at[slot],
            recv_sem=self.recv.at[slot],
            device_id=dev,
            device_id_type=MESH,
        ).wait_recv()

    def finish(self):
        for copy in self.open:
            copy.wait_send()
        self.open = []


GATHER_SEMS = 24


def gather_steps(pc, sems, local_sem, shard, out, split):
    rows = shard.shape[0]
    quarter = rows // 4
    yh, x, c, z = pc.yh, pc.x, pc.c, pc.z
    s_y = sems.take()
    s_x = [[sems.take() for _ in range(2)] for _ in range(3)]
    s_z = [[sems.take() for _ in range(3)] for _ in range(3)] if split else None
    s_s = [sems.take() for _ in range(4)]
    band = pl.ds(pl.multiple_of(z * quarter, 16), quarter) if split else pl.ds(0, rows)
    straight = (0, 1, 2) if split else (0, 1)

    own = pltpu.make_async_copy(shard, out.at[yh, x, c], local_sem)
    own.start()
    sems.push(s_y, shard, out.at[yh, x, c], pc.ypair)
    yield
    for k in straight:
        sems.push(s_x[k][0], shard.at[band], out.at[yh, x, c, band], pc.xdev[k])
    yield
    sems.arrived(s_y, out.at[1 - yh, x, c], pc.ypair)
    for k in straight:
        piece = out.at[1 - yh, x, c, band]
        sems.push(s_x[k][1], piece, piece, pc.xdev[k])
    own.wait()
    sems.push(s_s[3], out.at[:, x, c], out.at[:, x, c], pc.sib)
    yield
    for k in straight:
        far = pc.xfrom[k]
        sems.arrived(s_x[k][0], out.at[yh, far, c, band], pc.xdev[k])
        sems.arrived(s_x[k][1], out.at[1 - yh, far, c, band], pc.xdev[k])
        if split:
            piece = out.at[:, far, c, band]
            for j in range(3):
                sems.push(s_z[k][j], piece, piece, pc.zdev[j])
        else:
            piece = out.at[k, far, c]
            sems.push(s_x[2][k], piece, piece, pc.xdev[k])
            sems.push(s_s[k], out.at[:, far, c], out.at[:, far, c], pc.sib)
    yield
    if split:
        for k in (0, 1, 2):
            far = pc.xfrom[k]
            for j in range(3):
                there = pl.ds(pl.multiple_of(pc.zfrom[j] * quarter, 16), quarter)
                sems.arrived(s_z[k][j], out.at[:, far, c, there], pc.zdev[j])
            sems.push(s_s[k], out.at[:, far, c], out.at[:, far, c], pc.sib)
    else:
        far = pc.xs[2]
        for k in (0, 1):
            sems.arrived(s_x[2][k], out.at[k, far, c], pc.xdev[k])
        sems.push(s_s[2], out.at[:, far, c], out.at[:, far, c], pc.sib)
    yield
    for k in (0, 1, 2, 3):
        far = x if k == 3 else pc.xfrom[k]
        sems.arrived(s_s[k], out.at[:, far, 1 - c], pc.sib)
    yield


def run_all(steps):
    live = list(steps)
    while live:
        for s in list(live):
            try:
                next(s)
            except StopIteration:
                live.remove(s)


REDUCE_SEMS = 32


def add_rows(dst, terms, shape):
    lead, rows = shape[:-2], shape[-2]
    blocks = rows // 16
    count = math.prod(lead) * blocks

    def body(i, carry):
        idx, rest = [], i // blocks
        for size in reversed(lead):
            idx.append(rest % size)
            rest = rest // size
        idx = tuple(reversed(idx))
        at = (*idx, pl.ds(pl.multiple_of((i % blocks) * 16, 16), 16))
        total = dst[at].astype(F32)
        for term in terms:
            total = total + term[at].astype(F32)
        dst[at] = total.astype(BF16)
        return carry

    lax.fori_loop(0, count, body, 0)


def reduce_scratch(rows, width, split):
    q = rows // 4
    buffers = [pltpu.VMEM((2, 4, rows, width), BF16)] * 2
    buffers += [pltpu.VMEM((3 if split else 2, 2, q if split else rows, width), BF16)]
    buffers += [pltpu.VMEM((rows, width), BF16)]
    if wide_sum(width):
        buffers += [
            pltpu.VMEM((rows // 2, width), BF16),
            pltpu.VMEM((3, rows // 2, width // 4), BF16),
        ]
    else:
        buffers += [pltpu.VMEM((q, width), BF16), pltpu.VMEM((3, q, width), BF16)]
    buffers += [pltpu.VMEM((3, 3, 2, q, width) if split else (2, rows, width), BF16)]
    return buffers


def wide_sum(width):
    return width % (4 * 128) == 0


def reduce_steps(pc, sems, local_sem, part, final, buffers, split):
    yh, x, c, z, yl = pc.yh, pc.x, pc.c, pc.z, pc.yl
    acc, from_sib, from_x, from_y, from_l, from_z, from_r = buffers
    rows, width = part.shape[-2:]
    q = rows // 4
    s_y, s_l, s_m = (sems.take() for _ in range(3))
    s_s = [sems.take() for _ in range(4)]
    s_x = [sems.take() for _ in range(3)]
    s_z = [sems.take() for _ in range(3)]
    s_f = [sems.take() for _ in range(3)]
    s_r = [[sems.take() for _ in range(3)] for _ in range(3)]

    def band(k):
        return pl.ds(pl.multiple_of(k * q, 16), q)

    targets = [pc.xs[2], pc.xs[0], pc.xs[1], x]
    own = pltpu.make_async_copy(part.at[:, :, c], acc, local_sem)
    own.start()
    for k in range(4):
        sems.push(s_s[k], part.at[:, targets[k], 1 - c], from_sib.at[:, targets[k]], pc.sib)
    yield
    own.wait()

    def with_sibling(k):
        there = targets[k]
        sems.arrived(s_s[k], from_sib.at[:, there], pc.sib)
        add_rows(acc.at[:, there], [from_sib.at[:, there]], (2, rows, width))

    if split:
        here = band(z)
        order = (2, 0, 1)
        for n, k in enumerate(order):
            with_sibling(n)
            for j in range(3):
                piece = acc.at[:, pc.xs[k], band(pc.zs[j])]
                sems.push(s_r[k][j], piece, from_r.at[j, k], pc.zdev[j])
        yield
        for k in order:
            for j in range(3):
                sems.arrived(s_r[k][j], from_r.at[j, k], pc.zdev[j])
            mine = acc.at[:, pc.xs[k], here]
            add_rows(mine, [from_r.at[j, k] for j in range(3)], (2, q, width))
            sems.push(s_x[k], mine, from_x.at[k], pc.xdev[k])
        yield
        with_sibling(3)
        for k in range(3):
            sems.arrived(s_x[k], from_x.at[k], pc.xdev[k])
        add_rows(acc.at[:, x, here], [from_x.at[k] for k in range(3)], (2, q, width))
    else:
        with_sibling(0)
        for k in range(2):
            sems.push(s_r[0][k], acc.at[k, pc.xs[2]], from_r.at[k], pc.xdev[k])
        yield
        for k in range(2):
            with_sibling(1 + k)
            sems.arrived(s_r[0][k], from_r.at[k], pc.xdev[k])
            add_rows(acc.at[k, pc.xs[k]], [from_r.at[k]], (rows, width))
            sems.push(s_x[k], acc.at[:, pc.xs[k]], from_x.at[k], pc.xdev[k])
        yield
        with_sibling(3)
        for k in range(2):
            sems.arrived(s_x[k], from_x.at[k], pc.xdev[k])
        add_rows(acc.at[:, x], [from_x.at[k] for k in range(2)], (2, rows, width))
    sems.push(s_y, acc.at[1 - yh, x], from_y, pc.ypair)
    yield
    sems.arrived(s_y, from_y, pc.ypair)
    mine = acc.at[yh, x]
    add_rows(mine, [from_y], (rows, width))
    if wide_sum(width):
        h, w = rows // 2, width // 4
        half = pl.ds(pl.multiple_of(yl * h, 16), h)
        other = pl.ds(pl.multiple_of((1 - yl) * h, 16), h)

        def column(k):
            return pl.ds(pl.multiple_of(k * w, 128), w)

        sems.push(s_l, acc.at[yh, x, other], from_l, pc.ylo)
        yield
        sems.arrived(s_l, from_l, pc.ylo)
        add_rows(acc.at[yh, x, half], [from_l], (h, width))
        for j in range(3):
            piece = acc.at[yh, x, half, column(pc.zs[j])]
            sems.push(s_z[j], piece, from_z.at[j], pc.zdev[j])
        yield
        for j in range(3):
            sems.arrived(s_z[j], from_z.at[j], pc.zdev[j])
        mine = acc.at[yh, x, half, column(z)]
        add_rows(mine, [from_z.at[j] for j in range(3)], (h, w))
        done = final.at[half, column(z)]
        done[...] = mine[...]
        for j in range(3):
            sems.push(s_f[j], done, done, pc.zdev[j])
        yield
        for j in range(3):
            sems.arrived(s_f[j], final.at[half, column(pc.zfrom[j])], pc.zdev[j])
        sems.push(s_m, final.at[half], final.at[half], pc.ylo)
        yield
        sems.arrived(s_m, final.at[other], pc.ylo)
    else:
        for j in range(3):
            piece = acc.at[yh, x, band(pc.zs[j])]
            sems.push(s_z[j], piece, from_z.at[j], pc.zdev[j])
        yield
        for j in range(3):
            sems.arrived(s_z[j], from_z.at[j], pc.zdev[j])
        mine = acc.at[yh, x, band(z)]
        add_rows(mine, [from_z.at[j] for j in range(3)], (q, width))
        sems.push(s_l, mine, from_l, pc.ylo)
        yield
        sems.arrived(s_l, from_l, pc.ylo)
        done = final.at[band(z)]
        done[...] = (mine[...].astype(F32) + from_l[...].astype(F32)).astype(BF16)
        for j in range(3):
            sems.push(s_f[j], done, done, pc.zdev[j])
        yield
        for j in range(3):
            sems.arrived(s_f[j], final.at[band(pc.zfrom[j])], pc.zdev[j])
    yield


class Column:
    def __init__(self, pc):
        self.z, self.yl = pc.z, pc.yl
        self.t = 2 * pc.z + pc.yl
        self.beside = pc.ylo
        self.pc = pc

    def own(self, step):
        return 2 * (self.z + step) + self.yl

    def other(self, step):
        return 2 * (self.z + step) + 1 - self.yl

    def device(self, step):
        pc = self.pc
        return device(pc.yh, pc.x, pc.c, (pc.z + step + 4) % 4, pc.yl)


def dot(a, b):
    return jnp.dot(a, b, preferred_element_type=F32)


def dot_tn(a, b):
    return lax.dot_general(a, b, (((0,), (0,)), ((), ())), preferred_element_type=F32)


def dot_nt(a, b):
    return lax.dot_general(a, b, (((1,), (1,)), ((), ())), preferred_element_type=F32)


def norm_scale(rows):
    return lax.rsqrt(jnp.sum(rows * rows, axis=-1, keepdims=True) * (1.0 / WIDTH) + EPS)


def norm_back(grad_normed, rows, scale, gain):
    unit = rows * scale
    grad_gain = jnp.sum(grad_normed * unit, axis=0)
    grad_unit = grad_normed * gain
    mean = jnp.sum(grad_unit * unit, axis=-1, keepdims=True) * (1.0 / WIDTH)
    return scale * (grad_unit - unit * mean), grad_gain


BLOCK = 256
PAIR = 2 * HEAD_WIDTH
STACK = GROUP * BLOCK
FACTOR = HEAD_WIDTH ** (-0.5)


def low_half(shape):
    return lax.broadcasted_iota(jnp.int32, shape, 1) % PAIR < HEAD_WIDTH


def swap_halves(tile):
    lane = lax.broadcasted_iota(jnp.int32, tile.shape, 1) % HEAD_WIDTH
    half = HEAD_WIDTH // 2
    return jnp.where(
        lane < half, pltpu.roll(tile, PAIR - half, 1), pltpu.roll(tile, half, 1)
    )


def flip(a):
    return a.astype(F32).T.astype(a.dtype)


def advance(*steps):
    for s in steps:
        next(s, None)


def drain(*steps):
    run_all(steps)


def tile_of(ref, tile):
    return ref[:, :, :, :, tile * PAIR : (tile + 1) * PAIR].reshape(PADDED, PAIR)


def gain_row(kv_w, which):
    pick = lax.broadcasted_iota(jnp.int32, (8, PAIR), 1) == HEAD_WIDTH + which
    return dot_nt(pick.astype(BF16), tile_of(kv_w, KV_TILES - 1))[0:1]


def copy_wait(sems, slot, ref, dev):
    pltpu.make_async_remote_copy(
        src_ref=ref,
        dst_ref=ref,
        send_sem=sems.send.at[slot],
        recv_sem=sems.recv.at[slot],
        device_id=dev,
        device_id_type=MESH,
    ).wait_send()


def forward_kernel(
    flat,
    cosine,
    sine,
    kv_shard,
    q_shard,
    out_shard,
    gate_shard,
    up_shard,
    down_shard,
    kv_w,
    q_w,
    out_w,
    gate_w,
    up_w,
    down_w,
    normed,
    q_t,
    kv_all,
    o_t,
    lse,
    mixed,
    peak,
    wide,
    send,
    recv,
    local,
    kv_send,
    kv_recv,
):
    pc = Places()
    col = Column(pc)
    t, z, yl = col.t, pc.z, pc.yl
    greet([pc.sib, pc.ypair, pc.ylo, *pc.xdev, *pc.zdev])
    sems, kv_sems = Sems(send, recv), Sems(kv_send, kv_recv)
    g_kv = gather_steps(pc, sems, local.at[0], kv_shard, kv_w, True)
    g_q = gather_steps(pc, sems, local.at[1], q_shard, q_w, False)
    g_out = gather_steps(pc, sems, local.at[2], out_shard, out_w, False)
    g_gate = gather_steps(pc, sems, local.at[3], gate_shard, gate_w, True)
    g_up = gather_steps(pc, sems, local.at[4], up_shard, up_w, True)
    g_down = gather_steps(pc, sems, local.at[5], down_shard, down_w, False)
    advance(g_kv, g_kv, g_q, g_gate, g_up)
    x = flat[...]
    scale = norm_scale(x)
    advance(g_kv, g_q)
    advance(g_kv, g_q, g_gate, g_up)
    advance(g_kv, g_out, g_down)
    advance(g_kv)

    normed[...] = (x * scale * gain_row(kv_w, 0)).astype(BF16)
    rows = normed[...]
    cos, sin = cosine[...], sine[...]
    low = low_half((BLOCK, PAIR))

    def place_queries(product, tile):
        turned = (product * FACTOR).T.astype(BF16)
        for side in range(2):
            head = 2 * tile + side
            if head < QUERY_HEADS:
                h, g = head // GROUP, head % GROUP
                at = slice(g * BLOCK, (g + 1) * BLOCK)
                q_t[h, 0:HEAD_WIDTH, at] = turned[side * HEAD_WIDTH : (side + 1) * HEAD_WIDTH]
                q_t[h, HEAD_WIDTH:PAIR, at] = jnp.zeros((HEAD_WIDTH, BLOCK), BF16)

    for tile in range(KV_TILES):
        product = dot(rows, tile_of(kv_w, tile))
        if tile < 3:
            product = product * cos + swap_halves(product) * sin
        wide[tile] = product
    for h in range(KEY_VALUE_HEADS):
        k_tile, k_high = (h + 1) // 2, (h + 1) % 2
        v_tile, v_high = 3 + h // 2, h % 2
        k_part, v_part = wide[k_tile], wide[v_tile]
        if k_high:
            k_part = pltpu.roll(k_part, HEAD_WIDTH, 1)
        if not v_high:
            v_part = pltpu.roll(v_part, HEAD_WIDTH, 1)
        kv_all[t, h] = jnp.where(low, k_part, v_part).astype(BF16)
    for step in (1, 2, 3):

        @pl.when(z + step < 4)
        def _(step=step):
            kv_sems.push(step - 1, kv_all.at[t], kv_all.at[t], col.device(step))

    @pl.when(yl == 0)
    def _():
        kv_sems.push(3, kv_all.at[t], kv_all.at[t], col.beside)

    advance(g_gate, g_up, g_out)
    place_queries(wide[0], 7)
    advance(g_q)
    advance(g_q)
    advance(g_q)
    for tile in range(Q_TILES):
        product = dot(rows, tile_of(q_w, tile))
        place_queries(product * cos + swap_halves(product) * sin, tile)
    peak[...] = jnp.full_like(peak, -1e30)
    o_t[...] = jnp.zeros_like(o_t)

    def visit(j, diagonal):
        def per_head(h, carry):
            kv = kv_all[j, h]
            kv_t = flip(kv)
            ones = lax.broadcasted_iota(jnp.int32, (PAIR, BLOCK), 0) < HEAD_WIDTH
            ones_v = jnp.where(ones, 1.0, kv_t.astype(F32)).astype(BF16)
            scores = dot(kv, q_t[h])
            if diagonal:
                key = lax.broadcasted_iota(jnp.int32, (BLOCK, STACK), 0)
                query = lax.broadcasted_iota(jnp.int32, (BLOCK, STACK), 1) % BLOCK
                scores = jnp.where(key <= query, scores, -1e30)
            old = peak[h]
            new = jnp.maximum(old, jnp.max(scores, axis=0, keepdims=True))
            probs = jnp.exp(scores - new[0:1]).astype(BF16)
            o_t[h] = o_t[h] * jnp.exp(old - new)[0:1] + dot(ones_v, probs)
            peak[h] = new
            return carry

        lax.fori_loop(0, KEY_VALUE_HEADS, per_head, 0)

    advance(g_gate, g_up, g_out, g_down)
    visit(t, True)
    for step in (1, 2, 3):

        @pl.when(z - step >= 0)
        def _(step=step):
            block = kv_all.at[col.own(-step)]
            kv_sems.arrived(step - 1, block, col.device(-step))
            kv_sems.push(3 + step, block, block, col.beside)
            visit(col.own(-step), False)

        if step == 2:
            advance(g_out, g_down)
    advance(g_gate, g_up)
    for step in (0, 1, 2, 3):

        @pl.when((yl == 1) if step == 0 else (z - step >= 0))
        def _(step=step):
            block = kv_all.at[col.other(-step)]
            kv_sems.arrived(3 + step, block, col.beside)
            visit(col.other(-step), False)

    for h in range(KEY_VALUE_HEADS):
        total = o_t[h, 0:1]
        o_t[h] = o_t[h] * (1.0 / total)
        lse[h] = peak[h] + jnp.log(total)
    for tile in range(8):
        parts = []
        for head in (2 * tile, min(2 * tile + 1, QUERY_HEADS - 1)):
            h, g = head // GROUP, head % GROUP
            parts.append(o_t[h, HEAD_WIDTH:PAIR, g * BLOCK : (g + 1) * BLOCK])
        joined = jnp.concatenate(parts, axis=0).T.astype(BF16)
        if tile < 7:
            mixed[:, tile * PAIR : (tile + 1) * PAIR] = joined
        else:
            mixed[:, tile * PAIR : tile * PAIR + HEAD_WIDTH] = joined[:, :HEAD_WIDTH]
    drain(g_gate, g_up, g_down, g_out)
    for step in (1, 2, 3):

        @pl.when(z + step < 4)
        def _(step=step):
            copy_wait(kv_sems, step - 1, kv_all.at[t], col.device(step))

        @pl.when(z - step >= 0)
        def _(step=step):
            copy_wait(kv_sems, 3 + step, kv_all.at[t], col.beside)

    @pl.when(yl == 0)
    def _():
        copy_wait(kv_sems, 3, kv_all.at[t], col.beside)

    sems.finish()


def forward(flat, cosine, sine, shards, collective_id):
    vmem, hbm = pl.BlockSpec(memory_space=pltpu.VMEM), pl.BlockSpec(memory_space=pl.ANY)
    gathered = [jax.ShapeDtypeStruct((2, 4, 2, *s.shape), BF16) for s in shards]
    return pl.pallas_call(
        forward_kernel,
        out_shape=[
            *gathered,
            jax.ShapeDtypeStruct((BLOCK, PADDED), BF16),
            jax.ShapeDtypeStruct((KEY_VALUE_HEADS, PAIR, STACK), BF16),
            jax.ShapeDtypeStruct((8, KEY_VALUE_HEADS, BLOCK, PAIR), BF16),
            jax.ShapeDtypeStruct((KEY_VALUE_HEADS, PAIR, STACK), F32),
            jax.ShapeDtypeStruct((KEY_VALUE_HEADS, 8, STACK), F32),
            jax.ShapeDtypeStruct((BLOCK, WIDTH), BF16),
        ],
        in_specs=[vmem, vmem, vmem] + [hbm] * 6,
        out_specs=[vmem] * 2 + [hbm] * 4 + [vmem] * 6,
        scratch_shapes=[
            pltpu.VMEM((KEY_VALUE_HEADS, 8, STACK), F32),
            pltpu.VMEM((KV_TILES, BLOCK, PAIR), F32),
            pltpu.SemaphoreType.DMA((6 * GATHER_SEMS,)),
            pltpu.SemaphoreType.DMA((6 * GATHER_SEMS,)),
            pltpu.SemaphoreType.DMA((6,)),
            pltpu.SemaphoreType.DMA((7,)),
            pltpu.SemaphoreType.DMA((7,)),
        ],
        compiler_params=pltpu.CompilerParams(
            collective_id=collective_id, has_side_effects=True, vmem_limit_bytes=60 << 20
        ),
    )(flat, cosine, sine, *shards)


def backward_kernel(
    gate_part,
    up_part,
    down_part,
    out_part,
    flat,
    grad_resid,
    grad_gain_two,
    cosine,
    sine,
    kv_w,
    q_w,
    normed,
    q_t,
    kv_all,
    o_t,
    lse,
    grad_mixed,
    gate_sum,
    up_sum,
    down_sum,
    out_sum,
    q_sum,
    kv_sum,
    d_tokens,
    do_t,
    do_n,
    q_n,
    dq_t,
    delta,
    dkv,
    landed,
    beside,
    grad_qkv,
    q_part,
    kv_part,
    send,
    recv,
    local,
    kv_send,
    kv_recv,
    *buffers,
):
    pc = Places()
    col = Column(pc)
    t, z, yl = col.t, pc.z, pc.yl
    greet([pc.sib, pc.ypair, pc.ylo, *pc.xdev, *pc.zdev])
    sems, kv_sems = Sems(send, recv), Sems(kv_send, kv_recv)
    parts = (gate_part, up_part, down_part, out_part, q_part, kv_part)
    finals = (gate_sum, up_sum, down_sum, out_sum, q_sum, kv_sum)
    reduces = [
        reduce_steps(
            pc, sems, local.at[k], parts[k], finals[k], buffers[7 * k : 7 * k + 7], split
        )
        for k, split in enumerate(REDUCE_SPLITS)
    ]
    r_gate, r_up, r_down, r_out, r_q, r_kv = reduces
    early = (r_up, r_down, r_gate, r_out)
    advance(r_up, r_gate, r_down, r_out)

    do_t[...] = jnp.zeros_like(do_t)
    for tile in range(8):
        if tile < 7:
            turned = flip(grad_mixed[:, tile * PAIR : (tile + 1) * PAIR])
        else:
            turned = flip(grad_mixed[:, tile * PAIR : tile * PAIR + HEAD_WIDTH])
        for side in range(2):
            head = 2 * tile + side
            if head < QUERY_HEADS:
                h, g = head // GROUP, head % GROUP
                do_t[h, HEAD_WIDTH:PAIR, g * BLOCK : (g + 1) * BLOCK] = turned[
                    side * HEAD_WIDTH : (side + 1) * HEAD_WIDTH
                ]
    for h in range(KEY_VALUE_HEADS):
        do_n[h] = flip(do_t[h])
        q_n[h] = flip(q_t[h])
        both = do_t[h, HEAD_WIDTH:PAIR].astype(F32) * o_t[h, HEAD_WIDTH:PAIR]
        delta[h] = jnp.broadcast_to(jnp.sum(both, axis=0, keepdims=True), (8, STACK))
    dq_t[...] = jnp.zeros_like(dq_t)

    def visit(j, diagonal):
        def per_head(h, carry):
            kv = kv_all[j, h]
            scores = dot(kv, q_t[h])
            if diagonal:
                key = lax.broadcasted_iota(jnp.int32, (BLOCK, STACK), 0)
                query = lax.broadcasted_iota(jnp.int32, (BLOCK, STACK), 1) % BLOCK
                scores = jnp.where(key <= query, scores, -1e30)
            probs = jnp.exp(scores - lse[h][0:1])
            grad_probs = dot(kv, do_t[h])
            grad_scores = (probs * (grad_probs - delta[h][0:1])).astype(BF16)
            both = dot(grad_scores, q_n[h]) + dot(probs.astype(BF16), do_n[h])
            dkv[j, h] = both.astype(BF16)
            dq_t[h] += dot(flip(kv), grad_scores)
            return carry

        lax.fori_loop(0, KEY_VALUE_HEADS, per_head, 0)

    advance(r_up, r_gate)
    for step in (3, 2, 1, 0):

        @pl.when((yl == 1) if step == 0 else (z - step >= 0))
        def _(step=step):
            j = col.other(-step)
            visit(j, False)
            kv_sems.push(step, dkv.at[j], beside.at[step], col.beside)

        if step == 3:
            advance(r_down, r_out)
        if step == 2:
            advance(r_up)
        if step == 1:
            advance(r_down)
        if step == 0:
            advance(r_gate, r_out)
    for step in (3, 2, 1):

        @pl.when(z - step >= 0)
        def _(step=step):
            j = col.own(-step)
            visit(j, False)
            kv_sems.arrived(step, beside.at[step], col.beside)
            for h in range(KEY_VALUE_HEADS):
                total = dkv[j, h].astype(F32) + beside[step, h].astype(F32)
                dkv[j, h] = total.astype(BF16)
            kv_sems.push(3 + step, dkv.at[j], landed.at[step - 1], col.device(-step))

        if step == 2:
            advance(r_up)
    visit(t, True)
    advance(r_down)

    cos, sin = cosine[...], sine[...]

    def turn(tile):
        return tile * cos - swap_halves(tile) * sin

    for tile in range(8):
        pieces = []
        for head in (2 * tile, min(2 * tile + 1, QUERY_HEADS - 1)):
            h, g = head // GROUP, head % GROUP
            pieces.append(dq_t[h, 0:HEAD_WIDTH, g * BLOCK : (g + 1) * BLOCK])
        joined = turn(jnp.concatenate(pieces, axis=0).T * FACTOR)
        grad_qkv[:, tile * PAIR : (tile + 1) * PAIR] = joined.astype(BF16)
    rows = normed[...]
    for tile in range(Q_TILES):
        product = dot_tn(rows, grad_qkv[:, tile * PAIR : (tile + 1) * PAIR])
        q_part[:, :, :, :, tile * PAIR : (tile + 1) * PAIR] = product.astype(BF16).reshape(
            2, 4, 2, PAD, PAIR
        )
    advance(r_q)
    advance(r_up, r_gate, r_out)

    @pl.when(yl == 0)
    def _():
        kv_sems.arrived(0, beside.at[0], col.beside)
        for h in range(KEY_VALUE_HEADS):
            total = dkv[t, h].astype(F32) + beside[0, h].astype(F32)
            dkv[t, h] = total.astype(BF16)

    for step in (1, 2, 3):

        @pl.when(z + step < 4)
        def _(step=step):
            kv_sems.arrived(3 + step, landed.at[step - 1], col.device(step))

    advance(r_q)
    low = low_half((BLOCK, PAIR))
    totals = []
    for h in range(KEY_VALUE_HEADS):

        def add(k, total, h=h):
            return total + landed[k, h].astype(F32)

        totals.append(lax.fori_loop(0, 3 - z, add, dkv[t, h].astype(F32)))
    zero = jnp.zeros((BLOCK, PAIR), F32)
    left = grad_qkv[:, 7 * PAIR : 8 * PAIR].astype(F32)
    first = turn(pltpu.roll(totals[0], HEAD_WIDTH, 1))
    grad_qkv[:, 7 * PAIR : 8 * PAIR] = jnp.where(low, left, first).astype(BF16)
    for n, (a, b) in enumerate(((1, 2), (3, 4))):
        keys = turn(jnp.where(low, totals[a], pltpu.roll(totals[b], HEAD_WIDTH, 1)))
        grad_qkv[:, (8 + n) * PAIR : (9 + n) * PAIR] = keys.astype(BF16)
    for n, (a, b) in enumerate(((0, 1), (2, 3), (4, None))):
        high = zero if b is None else totals[b]
        vals = jnp.where(low, pltpu.roll(totals[a], HEAD_WIDTH, 1), high)
        grad_qkv[:, (10 + n) * PAIR : (11 + n) * PAIR] = vals.astype(BF16)

    x = flat[...]
    scale = norm_scale(x)
    grad_normed = dot_nt(
        grad_qkv[:, : Q_TILES * PAIR], q_w[...].reshape(PADDED, Q_TILES * PAIR)
    ) + dot_nt(grad_qkv[:, Q_TILES * PAIR :], kv_w[...].reshape(PADDED, KV_TILES * PAIR))
    token_term, grad_gain = norm_back(grad_normed, x, scale, gain_row(kv_w, 0))
    row = lax.broadcasted_iota(jnp.int32, (8, PADDED), 0)
    gains = jnp.where(row == 0, grad_gain[None, :], jnp.where(row == 1, grad_gain_two[...], 0.0))
    lane = lax.broadcasted_iota(jnp.int32, (8, PAIR), 1)
    which = lax.broadcasted_iota(jnp.int32, (8, PAIR), 0)
    put = (lane == which + HEAD_WIDTH) & (which < 2)
    for tile in range(KV_TILES):
        at = Q_TILES + tile
        product = dot_tn(rows, grad_qkv[:, at * PAIR : (at + 1) * PAIR])
        if tile == KV_TILES - 1:
            product = product + dot_tn(gains.astype(BF16), put.astype(BF16))
        kv_part[:, :, :, :, tile * PAIR : (tile + 1) * PAIR] = product.astype(BF16).reshape(
            2, 4, 2, PAD, PAIR
        )
    advance(r_kv)
    d_tokens[...] = (grad_resid[...] + token_term).astype(BF16)
    drain(r_kv, r_q, *early)

    for step in (0, 1, 2, 3):

        @pl.when((yl == 1) if step == 0 else (z - step >= 0))
        def _(step=step):
            copy_wait(kv_sems, step, beside.at[step], col.beside)

    for step in (1, 2, 3):

        @pl.when(z - step >= 0)
        def _(step=step):
            copy_wait(kv_sems, 3 + step, landed.at[step - 1], col.device(-step))

    sems.finish()


REDUCE_SPLITS = (True, False, False, True, False, True)


def backward(parts, values, collective_id):
    vmem, hbm = pl.BlockSpec(memory_space=pltpu.VMEM), pl.BlockSpec(memory_space=pl.ANY)
    q_shape = (2, 4, 2, PAD, Q_TILES * PAIR)
    kv_shape = (2, 4, 2, PAD, KV_TILES * PAIR)
    shapes = [p.shape for p in parts] + [q_shape, kv_shape]
    scratch = [
        pltpu.VMEM((KEY_VALUE_HEADS, PAIR, STACK), BF16),
        pltpu.VMEM((KEY_VALUE_HEADS, STACK, PAIR), BF16),
        pltpu.VMEM((KEY_VALUE_HEADS, STACK, PAIR), BF16),
        pltpu.VMEM((KEY_VALUE_HEADS, PAIR, STACK), F32),
        pltpu.VMEM((KEY_VALUE_HEADS, 8, STACK), F32),
        pltpu.VMEM((8, KEY_VALUE_HEADS, BLOCK, PAIR), BF16),
        pltpu.VMEM((3, KEY_VALUE_HEADS, BLOCK, PAIR), BF16),
        pltpu.VMEM((4, KEY_VALUE_HEADS, BLOCK, PAIR), BF16),
        pltpu.VMEM((BLOCK, (Q_TILES + KV_TILES) * PAIR), BF16),
        pltpu.VMEM(q_shape, BF16),
        pltpu.VMEM(kv_shape, BF16),
        pltpu.SemaphoreType.DMA((6 * REDUCE_SEMS,)),
        pltpu.SemaphoreType.DMA((6 * REDUCE_SEMS,)),
        pltpu.SemaphoreType.DMA((6,)),
        pltpu.SemaphoreType.DMA((7,)),
        pltpu.SemaphoreType.DMA((7,)),
    ]
    for s, split in zip(shapes, REDUCE_SPLITS):
        scratch += reduce_scratch(*s[-2:], split)
    return pl.pallas_call(
        backward_kernel,
        out_shape=[jax.ShapeDtypeStruct(s[-2:], BF16) for s in shapes]
        + [jax.ShapeDtypeStruct((BLOCK, PADDED), BF16)],
        in_specs=[hbm] * 4 + [vmem] * len(values),
        out_specs=[vmem] * 7,
        scratch_shapes=scratch,
        compiler_params=pltpu.CompilerParams(
            collective_id=collective_id, has_side_effects=True, vmem_limit_bytes=63 << 20
        ),
    )(*parts, *values)


def rotary_tables(token_positions):
    half = HEAD_WIDTH // 2
    freqs = ROPE_BASE ** (-jnp.arange(half, dtype=F32) * 2.0 / HEAD_WIDTH)
    angles = token_positions.astype(F32)[:, None] * freqs[None, :]
    cosine, sine = jnp.cos(angles), jnp.sin(angles)
    return (
        jnp.concatenate([cosine] * 4, axis=1),
        jnp.concatenate([-sine, sine] * 2, axis=1),
    )


def on_device(
    tokens,
    attn_gain,
    w_query,
    key_weight,
    value_weight,
    w_out,
    ffn_gain,
    w_gate,
    w_up,
    w_down,
    d_out,
):
    block = tokens.shape[1]
    token_positions = lax.axis_index("ctx") * block + jnp.arange(block, dtype=jnp.int32)
    cosine, sine = rotary_tables(token_positions)
    feature = jnp.arange(WIDTH, dtype=jnp.int32)
    place_of = feature // ROWS * PAD + feature % ROWS
    select = (place_of[:, None] == jnp.arange(PADDED, dtype=jnp.int32)[None, :]).astype(BF16)

    pad_rows = ((0, PAD - ROWS), (0, 0))
    qkv_shard = jnp.pad(
        jnp.concatenate(
            [w_query, key_weight, value_weight, attn_gain[:, None], ffn_gain[:, None]], axis=1
        ),
        ((0, PAD - ROWS), (0, (Q_TILES + KV_TILES) * PAIR - WIDTH - 2 * KV_WIDTH - 2)),
    )
    q_shard, kv_shard = qkv_shard[:, : Q_TILES * PAIR], qkv_shard[:, Q_TILES * PAIR :]
    out_shard = jnp.pad(dot(w_out, select).astype(BF16), pad_rows)
    gate_shard = jnp.pad(w_gate, pad_rows)
    up_shard = jnp.pad(w_up, pad_rows)
    down_shard = dot(w_down, select).astype(BF16)

    flat = dot(tokens[0], select)
    grad_flat = dot(d_out[0], select).astype(BF16)
    shards = (kv_shard, q_shard, out_shard, gate_shard, up_shard, down_shard)
    kv_w, q_w, out_w, gate_w, up_w, down_w, normed, q_t, kv_all, o_t, lse, mixed = forward(
        flat, cosine, sine, shards, 0
    )
    out_w, gate_w, up_w = (w.reshape(PADDED, -1) for w in (out_w, gate_w, up_w))
    down_w = down_w.reshape(-1, PADDED)
    gain_at = WIDTH + 2 * KV_WIDTH + 1 - Q_TILES * PAIR
    gain_two = kv_w.reshape(PADDED, KV_TILES * PAIR)[:, gain_at].astype(F32)
    mixed = dot(mixed, select).astype(BF16)

    resid = flat + dot(mixed, out_w)
    scale_two = norm_scale(resid)
    normed_two = (resid * scale_two * gain_two).astype(BF16)
    gate = dot(normed_two, gate_w)
    up = dot(normed_two, up_w)
    sigmoid = jax.nn.sigmoid(gate)
    swish = gate * sigmoid
    hidden = (swish * up).astype(BF16)
    output = (resid + dot(hidden, down_w)).astype(BF16)
    output = dot_nt(output, select).astype(BF16)
    grad_down = dot_tn(hidden, grad_flat)
    grad_hidden = dot_nt(grad_flat, down_w)
    grad_gate_v = (grad_hidden * up * sigmoid * (1.0 + gate * (1.0 - sigmoid))).astype(BF16)
    grad_up_v = (grad_hidden * swish).astype(BF16)
    grad_gate = dot_tn(normed_two, grad_gate_v)
    grad_up = dot_tn(normed_two, grad_up_v)
    grad_normed_two = dot_nt(grad_gate_v, gate_w) + dot_nt(grad_up_v, up_w)
    resid_term, grad_gain_two = norm_back(grad_normed_two, resid, scale_two, gain_two)
    grad_resid = grad_flat.astype(F32) + resid_term
    grad_branch = grad_resid.astype(BF16)
    grad_out = dot_tn(mixed, grad_branch)
    grad_mixed = dot_nt(dot_nt(grad_branch, out_w).astype(BF16), select).astype(BF16)
    parts = (
        grad_gate.astype(BF16).reshape(2, 4, 2, PAD, -1),
        grad_up.astype(BF16).reshape(2, 4, 2, PAD, -1),
        grad_down.astype(BF16).reshape(2, 4, 2, -1, PADDED),
        grad_out.astype(BF16).reshape(2, 4, 2, PAD, PADDED),
    )
    sum_gate, sum_up, sum_down, sum_out, sum_q, sum_kv, d_tokens = backward(
        parts,
        (
            flat,
            grad_resid,
            grad_gain_two[None, :],
            cosine,
            sine,
            kv_w,
            q_w,
            normed,
            q_t,
            kv_all,
            o_t,
            lse,
            grad_mixed,
        ),
        1,
    )
    d_tokens = dot_nt(d_tokens, select).astype(BF16)
    sum_qkv = jnp.concatenate([sum_q, sum_kv], axis=1)[:ROWS].astype(F32)
    ends = (WIDTH, WIDTH + KV_WIDTH, WIDTH + 2 * KV_WIDTH)
    return (
        output[None],
        d_tokens[None],
        sum_qkv[:, ends[2]],
        sum_qkv[:, : ends[0]],
        sum_qkv[:, ends[0] : ends[1]],
        sum_qkv[:, ends[1] : ends[2]],
        dot_nt(sum_out[:ROWS], select),
        sum_qkv[:, ends[2] + 1],
        sum_gate[:ROWS].astype(F32),
        sum_up[:ROWS].astype(F32),
        dot_nt(sum_down, select),
    )


def solution(mesh):
    rows, whole, line = P("fsdp", None), P("fsdp", "ctx", None), P("fsdp")
    weights = (line, rows, rows, rows, rows, line, rows, rows, rows)
    return jax.shard_map(
        on_device,
        mesh=mesh,
        in_specs=(whole, *weights, whole),
        out_specs=(whole, whole, *weights),
        check_vma=False,
    )
```

```python
import functools
import math

import jax
import jax.numpy as jnp
from jax import lax
from jax.experimental import pallas as pl
from jax.experimental.pallas import tpu as pltpu
from jax.sharding import PartitionSpec as P

QUERY_HEADS = 15
KEY_VALUE_HEADS = 5
HEAD_WIDTH = 64
GROUP = QUERY_HEADS // KEY_VALUE_HEADS
WIDTH = 960
ROWS = 60
PAD = 64
SHARDS = 16
PADDED = SHARDS * PAD
KV_WIDTH = KEY_VALUE_HEADS * HEAD_WIDTH
Q_TILES = 7
KV_TILES = 6

EPS = 1e-05
ROPE_BASE = 10000.0
MESH = pl.DeviceIdType.MESH
BF16 = jnp.bfloat16
F32 = jnp.float32


def place():
    f, t = lax.axis_index("fsdp"), lax.axis_index("ctx")
    return f // 8, (f // 2) % 4, f % 2, t // 2, t % 2


def device(yh, x, c, z, yl):
    return ((yh * 4 + x) * 2 + c, z * 2 + yl)


class Places:
    def __init__(self):
        yh, x, c, z, yl = place()
        self.yh, self.x, self.c, self.z, self.yl = yh, x, c, z, yl
        self.sib = device(yh, x, 1 - c, z, yl)
        self.ypair = device(1 - yh, x, c, z, 1 - yl)
        self.ylo = device(yh, x, c, z, 1 - yl)
        self.xs = [(x + 1) % 4, (x + 3) % 4, (x + 2) % 4]
        self.zs = [(z + 1) % 4, (z + 3) % 4, (z + 2) % 4]
        self.xdiag = [device(1 - yh, k, c, z, 1 - yl) for k in self.xs]
        self.zdiag = [device(yh, x, c, k, 1 - yl) for k in self.zs]
        self.xdev = [device(yh, k, c, z, yl) for k in self.xs]
        self.zdev = [device(yh, x, c, k, yl) for k in self.zs]
        self.xfrom = [self.xs[1], self.xs[0], self.xs[2]]
        self.zfrom = [self.zs[1], self.zs[0], self.zs[2]]


def greet(devices):
    barrier = pltpu.get_barrier_semaphore()
    for d in devices:
        pl.semaphore_signal(barrier, inc=1, device_id=d, device_id_type=MESH)
    pl.semaphore_wait(barrier, len(devices))


class Sems:
    def __init__(self, send, recv):
        self.send, self.recv, self.at, self.open = send, recv, 0, []

    def take(self, count=1):
        at = self.at
        self.at += count
        return at

    def push(self, slot, src, dst, dev):
        copy = pltpu.make_async_remote_copy(
            src_ref=src,
            dst_ref=dst,
            send_sem=self.send.at[slot],
            recv_sem=self.recv.at[slot],
            device_id=dev,
            device_id_type=MESH,
        )
        copy.start()
        self.open.append(copy)

    def arrived(self, slot, dst, dev):
        pltpu.make_async_remote_copy(
            src_ref=dst,
            dst_ref=dst,
            send_sem=self.send.at[slot],
            recv_sem=self.recv.at[slot],
            device_id=dev,
            device_id_type=MESH,
        ).wait_recv()

    def finish(self):
        for copy in self.open:
            copy.wait_send()
        self.open = []


GATHER_SEMS = 24


def gather_steps(pc, sems, local_sem, shard, out, split):
    rows = shard.shape[0]
    quarter = rows // 4
    yh, x, c, z = pc.yh, pc.x, pc.c, pc.z
    s_y = sems.take()
    s_x = [[sems.take() for _ in range(2)] for _ in range(3)]
    s_z = [[sems.take() for _ in range(3)] for _ in range(3)] if split else None
    s_s = [sems.take() for _ in range(4)]
    band = pl.ds(pl.multiple_of(z * quarter, 16), quarter) if split else pl.ds(0, rows)
    straight = (0, 1, 2) if split else (0, 1)

    own = pltpu.make_async_copy(shard, out.at[yh, x, c], local_sem)
    own.start()
    sems.push(s_y, shard, out.at[yh, x, c], pc.ypair)
    yield
    for k in straight:
        sems.push(s_x[k][0], shard.at[band], out.at[yh, x, c, band], pc.xdev[k])
    yield
    sems.arrived(s_y, out.at[1 - yh, x, c], pc.ypair)
    for k in straight:
        piece = out.at[1 - yh, x, c, band]
        sems.push(s_x[k][1], piece, piece, pc.xdev[k])
    own.wait()
    sems.push(s_s[3], out.at[:, x, c], out.at[:, x, c], pc.sib)
    yield
    for k in straight:
        far = pc.xfrom[k]
        sems.arrived(s_x[k][0], out.at[yh, far, c, band], pc.xdev[k])
        sems.arrived(s_x[k][1], out.at[1 - yh, far, c, band], pc.xdev[k])
        if split:
            piece = out.at[:, far, c, band]
            for j in range(3):
                sems.push(s_z[k][j], piece, piece, pc.zdev[j])
        else:
            piece = out.at[k, far, c]
            sems.push(s_x[2][k], piece, piece, pc.xdev[k])
            sems.push(s_s[k], out.at[:, far, c], out.at[:, far, c], pc.sib)
    yield
    if split:
        for k in (0, 1, 2):
            far = pc.xfrom[k]
            for j in range(3):
                there = pl.ds(pl.multiple_of(pc.zfrom[j] * quarter, 16), quarter)
                sems.arrived(s_z[k][j], out.at[:, far, c, there], pc.zdev[j])
            sems.push(s_s[k], out.at[:, far, c], out.at[:, far, c], pc.sib)
    else:
        far = pc.xs[2]
        for k in (0, 1):
            sems.arrived(s_x[2][k], out.at[k, far, c], pc.xdev[k])
        sems.push(s_s[2], out.at[:, far, c], out.at[:, far, c], pc.sib)
    yield
    for k in (0, 1, 2, 3):
        far = x if k == 3 else pc.xfrom[k]
        sems.arrived(s_s[k], out.at[:, far, 1 - c], pc.sib)
    yield


def run_all(steps):
    live = list(steps)
    while live:
        for s in list(live):
            try:
                next(s)
            except StopIteration:
                live.remove(s)


REDUCE_SEMS = 32


def add_rows(dst, terms, shape):
    lead, rows = shape[:-2], shape[-2]
    blocks = rows // 16
    count = math.prod(lead) * blocks

    def body(i, carry):
        idx, rest = [], i // blocks
        for size in reversed(lead):
            idx.append(rest % size)
            rest = rest // size
        idx = tuple(reversed(idx))
        at = (*idx, pl.ds(pl.multiple_of((i % blocks) * 16, 16), 16))
        total = dst[at].astype(F32)
        for term in terms:
            total = total + term[at].astype(F32)
        dst[at] = total.astype(BF16)
        return carry

    lax.fori_loop(0, count, body, 0)


def reduce_scratch(rows, width, split):
    q = rows // 4
    return [
        pltpu.VMEM((2, 4, rows, width), BF16),
        pltpu.VMEM((3 if split else 2, 2, q if split else rows, width), BF16),
        pltpu.VMEM((rows, width), BF16),
        pltpu.VMEM((rows // 2, width), BF16),
        pltpu.VMEM((3, rows // 2, width // 4), BF16),
        pltpu.VMEM((3, 3, 2, q, width) if split else (2, rows, width), BF16),
    ]


def reduce_steps(pc, sems, local_sem, part, final, buffers, split):
    yh, x, c, z, yl = pc.yh, pc.x, pc.c, pc.z, pc.yl
    acc, from_x, from_y, from_l, from_z, from_r = buffers
    rows, width = part.shape[-2:]
    q = rows // 4
    s_y, s_l, s_m = (sems.take() for _ in range(3))
    s_x = [sems.take() for _ in range(3)]
    s_z = [sems.take() for _ in range(3)]
    s_f = [sems.take() for _ in range(3)]
    s_r = [[sems.take() for _ in range(3)] for _ in range(3)]

    def band(k):
        return pl.ds(pl.multiple_of(k * q, 16), q)

    own = pltpu.make_async_copy(part, acc, local_sem)
    own.start()
    own.wait()
    if split:
        here = band(z)
        order = (2, 0, 1)
        for k in order:
            for j in range(3):
                piece = acc.at[:, pc.xs[k], band(pc.zs[j])]
                sems.push(s_r[k][j], piece, from_r.at[j, k], pc.zdev[j])
        yield
        for k in order:
            for j in range(3):
                sems.arrived(s_r[k][j], from_r.at[j, k], pc.zdev[j])
            mine = acc.at[:, pc.xs[k], here]
            add_rows(mine, [from_r.at[j, k] for j in range(3)], (2, q, width))
            sems.push(s_x[k], mine, from_x.at[k], pc.xdev[k])
        yield
        for k in range(3):
            sems.arrived(s_x[k], from_x.at[k], pc.xdev[k])
        add_rows(acc.at[:, x, here], [from_x.at[k] for k in range(3)], (2, q, width))
    else:
        for k in range(2):
            sems.push(s_r[0][k], acc.at[k, pc.xs[2]], from_r.at[k], pc.xdev[k])
        yield
        for k in range(2):
            sems.arrived(s_r[0][k], from_r.at[k], pc.xdev[k])
            add_rows(acc.at[k, pc.xs[k]], [from_r.at[k]], (rows, width))
            sems.push(s_x[k], acc.at[:, pc.xs[k]], from_x.at[k], pc.xdev[k])
        yield
        for k in range(2):
            sems.arrived(s_x[k], from_x.at[k], pc.xdev[k])
        add_rows(acc.at[:, x], [from_x.at[k] for k in range(2)], (2, rows, width))
    sems.push(s_y, acc.at[1 - yh, x], from_y, pc.ypair)
    yield
    sems.arrived(s_y, from_y, pc.ypair)
    mine = acc.at[yh, x]
    add_rows(mine, [from_y], (rows, width))
    h, w = rows // 2, width // 4
    half = pl.ds(pl.multiple_of(yl * h, 16), h)
    other = pl.ds(pl.multiple_of((1 - yl) * h, 16), h)

    def column(k):
        return pl.ds(pl.multiple_of(k * w, 128), w)

    sems.push(s_l, acc.at[yh, x, other], from_l, pc.ylo)
    yield
    sems.arrived(s_l, from_l, pc.ylo)
    add_rows(acc.at[yh, x, half], [from_l], (h, width))
    for j in range(3):
        piece = acc.at[yh, x, half, column(pc.zs[j])]
        sems.push(s_z[j], piece, from_z.at[j], pc.zdev[j])
    yield
    for j in range(3):
        sems.arrived(s_z[j], from_z.at[j], pc.zdev[j])
    mine = acc.at[yh, x, half, column(z)]
    add_rows(mine, [from_z.at[j] for j in range(3)], (h, w))
    done = final.at[half, column(z)]
    done[...] = mine[...]
    for j in range(3):
        sems.push(s_f[j], done, done, pc.zdev[j])
    yield
    for j in range(3):
        sems.arrived(s_f[j], final.at[half, column(pc.zfrom[j])], pc.zdev[j])
    sems.push(s_m, final.at[half], final.at[half], pc.ylo)
    yield
    sems.arrived(s_m, final.at[other], pc.ylo)
    yield


def small_scratch(rows, width):
    q = rows // 4
    return [
        pltpu.VMEM((2, 4, rows, width), BF16),
        pltpu.VMEM((2, 4, rows, width), BF16),
        pltpu.VMEM((3, 2, 4, q, width), BF16),
        pltpu.VMEM((7, q, width), BF16),
        pltpu.VMEM((2, rows, width), BF16),
    ]


def small_steps(pc, sems, local_sem, part, final, buffers):
    yh, x, c, z, yl = pc.yh, pc.x, pc.c, pc.z, pc.yl
    acc, from_sib, from_z, from_xy, landed = buffers
    rows, width = part.shape[-2:]
    q = rows // 4
    s_s = sems.take()
    s_z = [sems.take() for _ in range(3)]
    s_xy = [sems.take() for _ in range(7)]
    s_f = [sems.take() for _ in range(7)]

    def band(k):
        return pl.ds(pl.multiple_of(k * q, 16), q)

    here = band(z)
    own = pltpu.make_async_copy(part.at[:, :, c], acc, local_sem)
    own.start()
    sems.push(s_s, part.at[:, :, 1 - c], from_sib, pc.sib)
    yield
    own.wait()
    sems.arrived(s_s, from_sib, pc.sib)
    add_rows(acc, [from_sib], acc.shape)
    for j in range(3):
        sems.push(s_z[j], acc.at[:, :, band(pc.zs[j])], from_z.at[j], pc.zdev[j])
    yield
    for j in range(3):
        sems.arrived(s_z[j], from_z.at[j], pc.zdev[j])
    add_rows(acc.at[:, :, here], [from_z.at[j] for j in range(3)], (2, 4, q, width))
    targets = [(yh, pc.xs[k], yl) for k in range(3)]
    targets += [(1 - yh, k, 1 - yl) for k in (*pc.xs, x)]
    for n, (there, k, side) in enumerate(targets):
        sems.push(s_xy[n], acc.at[there, k, here], from_xy.at[n], device(there, k, c, z, side))
    yield
    for n in range(7):
        sems.arrived(s_xy[n], from_xy.at[n], pc.sib)
    mine = acc.at[yh, x, here]
    add_rows(mine, [from_xy.at[n] for n in range(7)], (q, width))
    landed[yl, here] = mine[...]
    for n, (k, side) in enumerate([(k, yl) for k in pc.zs] + [(k, 1 - yl) for k in (*pc.zs, z)]):
        sems.push(s_f[n], mine, landed.at[yl, here], device(yh, x, c, k, side))
    yield
    for n, (k, side) in enumerate(
        [(k, yl) for k in pc.zfrom] + [(k, 1 - yl) for k in (*pc.zfrom, z)]
    ):
        sems.arrived(s_f[n], landed.at[side, band(k)], pc.sib)

    def body(i, carry):
        at = pl.ds(pl.multiple_of(i * 16, 16), 16)
        total = landed[0, at].astype(F32) + landed[1, at].astype(F32)
        final[at] = total.astype(BF16)
        return carry

    lax.fori_loop(0, rows // 16, body, 0)
    yield


class Column:
    def __init__(self, pc):
        self.z, self.yl = pc.z, pc.yl
        self.t = 2 * pc.z + pc.yl
        self.beside = pc.ylo
        self.pc = pc

    def own(self, step):
        return 2 * (self.z + step) + self.yl

    def other(self, step):
        return 2 * (self.z + step) + 1 - self.yl

    def device(self, step):
        pc = self.pc
        return device(pc.yh, pc.x, pc.c, (pc.z + step + 4) % 4, pc.yl)


def dot(a, b):
    return jnp.dot(a, b, preferred_element_type=F32)


def dot_tn(a, b):
    return lax.dot_general(a, b, (((0,), (0,)), ((), ())), preferred_element_type=F32)


def dot_nt(a, b):
    return lax.dot_general(a, b, (((1,), (1,)), ((), ())), preferred_element_type=F32)


def norm_scale(rows):
    return lax.rsqrt(jnp.sum(rows * rows, axis=-1, keepdims=True) * (1.0 / WIDTH) + EPS)


def norm_back(grad_normed, rows, scale, gain):
    unit = rows * scale
    grad_gain = jnp.sum(grad_normed * unit, axis=0)
    grad_unit = grad_normed * gain
    mean = jnp.sum(grad_unit * unit, axis=-1, keepdims=True) * (1.0 / WIDTH)
    return scale * (grad_unit - unit * mean), grad_gain


BLOCK = 256
PAIR = 2 * HEAD_WIDTH
STACK = GROUP * BLOCK
FACTOR = HEAD_WIDTH ** (-0.5)


def low_half(shape):
    return lax.broadcasted_iota(jnp.int32, shape, 1) % PAIR < HEAD_WIDTH


def swap_halves(tile):
    lane = lax.broadcasted_iota(jnp.int32, tile.shape, 1) % HEAD_WIDTH
    half = HEAD_WIDTH // 2
    return jnp.where(
        lane < half, pltpu.roll(tile, PAIR - half, 1), pltpu.roll(tile, half, 1)
    )


def flip(a):
    return a.astype(F32).T.astype(a.dtype)


def advance(*steps):
    for s in steps:
        next(s, None)


def drain(*steps):
    run_all(steps)


def tile_of(ref, tile):
    return ref[:, :, :, :, tile * PAIR : (tile + 1) * PAIR].reshape(PADDED, PAIR)


def gain_row(kv_w, which):
    pick = lax.broadcasted_iota(jnp.int32, (8, PAIR), 1) == HEAD_WIDTH + which
    return dot_nt(pick.astype(BF16), tile_of(kv_w, KV_TILES - 1))[0:1]


def copy_wait(sems, slot, ref, dev):
    pltpu.make_async_remote_copy(
        src_ref=ref,
        dst_ref=ref,
        send_sem=sems.send.at[slot],
        recv_sem=sems.recv.at[slot],
        device_id=dev,
        device_id_type=MESH,
    ).wait_send()


def forward_kernel(
    flat,
    cosine,
    sine,
    kv_shard,
    q_shard,
    out_shard,
    gate_shard,
    up_shard,
    down_shard,
    kv_w,
    q_w,
    out_w,
    gate_w,
    up_w,
    down_w,
    normed_t,
    q_t,
    kv_all,
    o_t,
    lse,
    mixed,
    gain_two,
    peak,
    wide,
    send,
    recv,
    local,
    kv_send,
    kv_recv,
):
    pc = Places()
    col = Column(pc)
    t, z, yl = col.t, pc.z, pc.yl
    greet([pc.sib, pc.ypair, pc.ylo, *pc.xdev, *pc.zdev])
    sems, kv_sems = Sems(send, recv), Sems(kv_send, kv_recv)
    g_kv = gather_steps(pc, sems, local.at[0], kv_shard, kv_w, True)
    g_q = gather_steps(pc, sems, local.at[1], q_shard, q_w, False)
    g_out = gather_steps(pc, sems, local.at[2], out_shard, out_w, False)
    g_gate = gather_steps(pc, sems, local.at[3], gate_shard, gate_w, True)
    g_up = gather_steps(pc, sems, local.at[4], up_shard, up_w, True)
    g_down = gather_steps(pc, sems, local.at[5], down_shard, down_w, False)
    advance(g_kv, g_kv, g_q, g_gate, g_gate, g_up)
    x = flat[...]
    scale = norm_scale(x)
    advance(g_kv, g_q)
    advance(g_kv, g_q, g_gate, g_up)
    advance(g_kv, g_out, g_down)
    advance(g_kv)

    rows = (x * scale * gain_row(kv_w, 0)).astype(BF16)
    gain_two[...] = gain_row(kv_w, 1)
    cos, sin = cosine[...], sine[...]
    low = low_half((BLOCK, PAIR))

    def place_queries(product, tile):
        turned = (product * FACTOR).T.astype(BF16)
        for side in range(2):
            head = 2 * tile + side
            if head < QUERY_HEADS:
                h, g = head // GROUP, head % GROUP
                at = slice(g * BLOCK, (g + 1) * BLOCK)
                q_t[h, 0:HEAD_WIDTH, at] = turned[side * HEAD_WIDTH : (side + 1) * HEAD_WIDTH]
                q_t[h, HEAD_WIDTH:PAIR, at] = jnp.zeros((HEAD_WIDTH, BLOCK), BF16)

    for tile in range(KV_TILES):
        product = dot(rows, tile_of(kv_w, tile))
        if tile < 3:
            product = product * cos + swap_halves(product) * sin
        wide[tile] = product
    for h in range(KEY_VALUE_HEADS):
        k_tile, k_high = (h + 1) // 2, (h + 1) % 2
        v_tile, v_high = 3 + h // 2, h % 2
        k_part, v_part = wide[k_tile], wide[v_tile]
        if k_high:
            k_part = pltpu.roll(k_part, HEAD_WIDTH, 1)
        if not v_high:
            v_part = pltpu.roll(v_part, HEAD_WIDTH, 1)
        kv_all[t, h] = jnp.where(low, k_part, v_part).astype(BF16)
    for step in (1, 2, 3):

        @pl.when(z + step < 4)
        def _(step=step):
            kv_sems.push(step - 1, kv_all.at[t], kv_all.at[t], col.device(step))

    @pl.when(yl == 0)
    def _():
        kv_sems.push(3, kv_all.at[t], kv_all.at[t], col.beside)

    advance(g_gate, g_up, g_q)
    advance(g_out, g_down)
    place_queries(wide[0], 7)
    normed_t[...] = flip(rows)
    advance(g_q, g_up, g_q)
    for tile in range(Q_TILES):
        product = dot(rows, tile_of(q_w, tile))
        place_queries(product * cos + swap_halves(product) * sin, tile)
    peak[...] = jnp.full_like(peak, -1e30)
    o_t[...] = jnp.zeros_like(o_t)

    def visit(j, diagonal):
        def per_head(h, carry):
            kv = kv_all[j, h]
            kv_t = flip(kv)
            ones = lax.broadcasted_iota(jnp.int32, (PAIR, BLOCK), 0) < HEAD_WIDTH
            ones_v = jnp.where(ones, 1.0, kv_t.astype(F32)).astype(BF16)
            scores = dot(kv, q_t[h])
            if diagonal:
                key = lax.broadcasted_iota(jnp.int32, (BLOCK, STACK), 0)
                query = lax.broadcasted_iota(jnp.int32, (BLOCK, STACK), 1) % BLOCK
                scores = jnp.where(key <= query, scores, -1e30)
            old = peak[h]
            new = jnp.maximum(old, jnp.max(scores, axis=0, keepdims=True))
            probs = jnp.exp(scores - new[0:1]).astype(BF16)
            o_t[h] = o_t[h] * jnp.exp(old - new)[0:1] + dot(ones_v, probs)
            peak[h] = new
            return carry

        lax.fori_loop(0, KEY_VALUE_HEADS, per_head, 0)

    advance(g_out, g_down)
    visit(t, True)
    for step in (1, 2, 3):

        @pl.when(z - step >= 0)
        def _(step=step):
            block = kv_all.at[col.own(-step)]
            kv_sems.arrived(step - 1, block, col.device(-step))
            kv_sems.push(3 + step, block, block, col.beside)
            visit(col.own(-step), False)

        if step == 1:
            advance(g_out, g_down)
        if step == 2:
            advance(g_gate)
        if step == 3:
            advance(g_out, g_down)
    for step in (0, 1, 2, 3):

        @pl.when((yl == 1) if step == 0 else (z - step >= 0))
        def _(step=step):
            block = kv_all.at[col.other(-step)]
            kv_sems.arrived(3 + step, block, col.beside)
            visit(col.other(-step), False)

        if step == 1:
            advance(g_up)

    for h in range(KEY_VALUE_HEADS):
        total = o_t[h, 0:1]
        o_t[h] = o_t[h] * (1.0 / total)
        lse[h] = peak[h] + jnp.log(total)
    for tile in range(8):
        parts = []
        for head in (2 * tile, min(2 * tile + 1, QUERY_HEADS - 1)):
            h, g = head // GROUP, head % GROUP
            parts.append(o_t[h, HEAD_WIDTH:PAIR, g * BLOCK : (g + 1) * BLOCK])
        joined = jnp.concatenate(parts, axis=0).T.astype(BF16)
        if tile < 7:
            mixed[:, tile * PAIR : (tile + 1) * PAIR] = joined
        else:
            mixed[:, tile * PAIR : tile * PAIR + HEAD_WIDTH] = joined[:, :HEAD_WIDTH]
    drain(g_gate, g_up, g_down, g_out)
    for step in (1, 2, 3):

        @pl.when(z + step < 4)
        def _(step=step):
            copy_wait(kv_sems, step - 1, kv_all.at[t], col.device(step))

        @pl.when(z - step >= 0)
        def _(step=step):
            copy_wait(kv_sems, 3 + step, kv_all.at[t], col.beside)

    @pl.when(yl == 0)
    def _():
        copy_wait(kv_sems, 3, kv_all.at[t], col.beside)

    sems.finish()


def forward(flat, cosine, sine, shards, collective_id):
    vmem, hbm = pl.BlockSpec(memory_space=pltpu.VMEM), pl.BlockSpec(memory_space=pl.ANY)
    gathered = [jax.ShapeDtypeStruct((2, 4, 2, *s.shape), BF16) for s in shards]
    return pl.pallas_call(
        forward_kernel,
        out_shape=[
            *gathered,
            jax.ShapeDtypeStruct((PADDED, BLOCK), BF16),
            jax.ShapeDtypeStruct((KEY_VALUE_HEADS, PAIR, STACK), BF16),
            jax.ShapeDtypeStruct((8, KEY_VALUE_HEADS, BLOCK, PAIR), BF16),
            jax.ShapeDtypeStruct((KEY_VALUE_HEADS, PAIR, STACK), F32),
            jax.ShapeDtypeStruct((KEY_VALUE_HEADS, 8, STACK), F32),
            jax.ShapeDtypeStruct((BLOCK, WIDTH), BF16),
            jax.ShapeDtypeStruct((1, PADDED), F32),
        ],
        in_specs=[vmem, vmem, vmem] + [hbm] * 6,
        out_specs=[vmem] * 2 + [hbm] * 4 + [vmem] * 7,
        scratch_shapes=[
            pltpu.VMEM((KEY_VALUE_HEADS, 8, STACK), F32),
            pltpu.VMEM((KV_TILES, BLOCK, PAIR), F32),
            pltpu.SemaphoreType.DMA((6 * GATHER_SEMS,)),
            pltpu.SemaphoreType.DMA((6 * GATHER_SEMS,)),
            pltpu.SemaphoreType.DMA((6,)),
            pltpu.SemaphoreType.DMA((7,)),
            pltpu.SemaphoreType.DMA((7,)),
        ],
        compiler_params=pltpu.CompilerParams(
            collective_id=collective_id, has_side_effects=True, vmem_limit_bytes=60 << 20
        ),
    )(flat, cosine, sine, *shards)


PARTS = 4
STEP = 640


def middle_kernel(
    flat,
    grad_flat,
    mixed,
    gain_two,
    select,
    out_w,
    gate_w,
    up_w,
    down_w,
    output,
    grad_resid,
    grad_gain_two,
    grad_mixed,
    gate_acc,
    up_acc,
    down_acc,
    out_acc,
    gate_buf,
    up_buf,
    down_buf,
    gate_stage,
    up_stage,
    down_stage,
    out_stage,
    gate_sib,
    up_sib,
    down_sib,
    out_sib,
    total,
    back,
    load,
    local,
    send,
    recv,
):
    pc = Places()
    c = pc.c

    def loads(i):
        at = pl.ds(i * STEP, STEP)
        slot = i % 2
        return (
            pltpu.make_async_copy(gate_w.at[:, at], gate_buf.at[slot], load.at[slot, 0]),
            pltpu.make_async_copy(up_w.at[:, at], up_buf.at[slot], load.at[slot, 1]),
            pltpu.make_async_copy(down_w.at[at], down_buf.at[slot], load.at[slot, 2]),
        )

    def remote(src, dst, k):
        return pltpu.make_async_remote_copy(
            src_ref=src,
            dst_ref=dst,
            send_sem=send.at[k],
            recv_sem=recv.at[k],
            device_id=pc.sib,
            device_id_type=MESH,
        )

    def sends(i):
        at, slot = pl.ds(i * STEP, STEP), i % 2
        yh, xs = i // 2, pl.ds(2 * (i % 2), 2)
        gate, up, down = gate_stage.at[slot], up_stage.at[slot], down_stage.at[slot]
        return (
            remote(gate.at[:, :, 1 - c], gate_sib.at[:, :, :, at], 3 * i),
            remote(up.at[:, :, 1 - c], up_sib.at[:, :, :, at], 3 * i + 1),
            remote(down.at[:, 1 - c], down_sib.at[yh, xs], 3 * i + 2),
            pltpu.make_async_copy(gate.at[:, :, c], gate_acc.at[:, :, :, at], local.at[slot, 0]),
            pltpu.make_async_copy(up.at[:, :, c], up_acc.at[:, :, :, at], local.at[slot, 1]),
            pltpu.make_async_copy(down.at[:, c], down_acc.at[yh, xs], local.at[slot, 2]),
        )

    def sent(i):
        copies = sends(i)
        for copy in copies[:3]:
            copy.wait_send()
        for copy in copies[3:]:
            copy.wait()

    for copy in loads(0):
        copy.start()
    greet([pc.sib])
    mixed_p = dot(mixed[...], select[...]).astype(BF16)
    resid = flat[...] + dot(mixed_p, out_w[...])
    scale = norm_scale(resid)
    gain = gain_two[...]
    normed = (resid * scale * gain).astype(BF16)
    normed_t = flip(normed)
    grad = grad_flat[...]
    total[...] = resid
    back[...] = jnp.zeros_like(back)
    for i in range(PARTS):
        slot = i % 2
        if i + 1 < PARTS:
            for copy in loads(i + 1):
                copy.start()
        for copy in loads(i):
            copy.wait()
        if i >= 2:
            sent(i - 2)
        w_gate, w_up, w_down = gate_buf[slot], up_buf[slot], down_buf[slot]
        gate = dot(normed, w_gate)
        up = dot(normed, w_up)
        grad_hidden = dot_nt(grad, w_down)
        sigmoid = 1.0 / (1.0 + jnp.exp(-gate))
        swish = gate * sigmoid
        hidden = (swish * up).astype(BF16)
        grad_up_v = (grad_hidden * swish).astype(BF16)
        grad_gate_v = (grad_hidden * up * sigmoid * (1.0 + gate * (1.0 - sigmoid))).astype(BF16)
        total[...] += dot(hidden, w_down)
        back[...] += dot_nt(grad_gate_v, w_gate) + dot_nt(grad_up_v, w_up)
        shape = (2, 4, 2, PAD, STEP)
        gate_stage[slot] = dot(normed_t, grad_gate_v).astype(BF16).reshape(shape)
        up_stage[slot] = dot(normed_t, grad_up_v).astype(BF16).reshape(shape)
        down = dot(flip(hidden), grad).astype(BF16)
        down_stage[slot] = down.reshape(2, 2, STEP // 4, PADDED)
        for copy in sends(i):
            copy.start()
    output[...] = dot_nt(total[...].astype(BF16), select[...]).astype(BF16)
    term, grad_gain = norm_back(back[...], resid, scale, gain)
    grad_gain_two[...] = grad_gain[None, :]
    full = grad.astype(F32) + term
    grad_resid[...] = full
    branch = full.astype(BF16)
    out_stage[...] = dot(flip(mixed_p), branch).astype(BF16).reshape(2, 4, 2, PAD, PADDED)
    out_send = remote(out_stage.at[:, :, 1 - c], out_sib, 3 * PARTS)
    out_send.start()
    out_copy = pltpu.make_async_copy(out_stage.at[:, :, c], out_acc, local.at[0, 3])
    out_copy.start()
    inner = dot_nt(branch, out_w[...]).astype(BF16)
    grad_mixed[...] = dot_nt(inner, select[...]).astype(BF16)
    for i in (PARTS - 2, PARTS - 1):
        sent(i)
    for i in range(PARTS):
        for copy in sends(i)[:3]:
            copy.wait_recv()
    add_rows(gate_acc, [gate_sib], gate_acc.shape)
    add_rows(up_acc, [up_sib], up_acc.shape)
    add_rows(down_acc, [down_sib], down_acc.shape)
    out_send.wait()
    out_copy.wait()
    add_rows(out_acc, [out_sib], out_acc.shape)


def middle(values, weights, collective_id):
    vmem, hbm = pl.BlockSpec(memory_space=pltpu.VMEM), pl.BlockSpec(memory_space=pl.ANY)
    hidden = weights[0].shape[1]
    tall = hidden // SHARDS
    accs = [(2, 4, PAD, hidden), (2, 4, PAD, hidden), (2, 4, tall, PADDED), (2, 4, PAD, PADDED)]
    return pl.pallas_call(
        middle_kernel,
        out_shape=[
            jax.ShapeDtypeStruct((BLOCK, WIDTH), BF16),
            jax.ShapeDtypeStruct((BLOCK, PADDED), F32),
            jax.ShapeDtypeStruct((1, PADDED), F32),
            jax.ShapeDtypeStruct((BLOCK, WIDTH), BF16),
            *[jax.ShapeDtypeStruct(a, BF16) for a in accs],
        ],
        in_specs=[vmem] * len(values) + [hbm] * 3,
        out_specs=[vmem] * 8,
        scratch_shapes=[
            pltpu.VMEM((2, PADDED, STEP), BF16),
            pltpu.VMEM((2, PADDED, STEP), BF16),
            pltpu.VMEM((2, STEP, PADDED), BF16),
            pltpu.VMEM((2, 2, 4, 2, PAD, STEP), BF16),
            pltpu.VMEM((2, 2, 4, 2, PAD, STEP), BF16),
            pltpu.VMEM((2, 2, 2, STEP // 4, PADDED), BF16),
            pltpu.VMEM((2, 4, 2, PAD, PADDED), BF16),
            *[pltpu.VMEM(a, BF16) for a in accs],
            pltpu.VMEM((BLOCK, PADDED), F32),
            pltpu.VMEM((BLOCK, PADDED), F32),
            pltpu.SemaphoreType.DMA((2, 3)),
            pltpu.SemaphoreType.DMA((2, 4)),
            pltpu.SemaphoreType.DMA((3 * PARTS + 1,)),
            pltpu.SemaphoreType.DMA((3 * PARTS + 1,)),
        ],
        compiler_params=pltpu.CompilerParams(
            collective_id=collective_id, has_side_effects=True, vmem_limit_bytes=62 << 20
        ),
    )(*values, *weights)


def backward_kernel(
    gate_part,
    up_part,
    down_part,
    out_part,
    flat,
    grad_resid,
    grad_gain_two,
    cosine,
    sine,
    kv_w,
    q_w,
    normed_t,
    q_t,
    kv_all,
    o_t,
    lse,
    grad_mixed,
    gate_sum,
    up_sum,
    down_sum,
    out_sum,
    q_sum,
    kv_sum,
    d_tokens,
    do_t,
    do_n,
    q_n,
    dq_t,
    delta,
    dkv,
    landed,
    beside,
    grad_qkv,
    q_part,
    kv_part,
    send,
    recv,
    local,
    kv_send,
    kv_recv,
    *buffers,
):
    pc = Places()
    col = Column(pc)
    t, z, yl = col.t, pc.z, pc.yl
    greet([pc.sib, pc.ypair, pc.ylo, *pc.xdev, *pc.zdev, *pc.xdiag, *pc.zdiag])
    sems, kv_sems = Sems(send, recv), Sems(kv_send, kv_recv)
    parts = (gate_part, up_part, down_part, out_part, q_part, kv_part)
    finals = (gate_sum, up_sum, down_sum, out_sum, q_sum, kv_sum)
    reduces = [
        reduce_steps(
            pc, sems, local.at[k], parts[k], finals[k], buffers[6 * k : 6 * k + 6], split
        )
        for k, split in enumerate(REDUCE_SPLITS)
    ]
    reduces += [
        small_steps(pc, sems, local.at[4 + k], parts[4 + k], finals[4 + k], buffers[24 + 5 * k : 29 + 5 * k])
        for k in range(2)
    ]
    r_gate, r_up, r_down, r_out, r_q, r_kv = reduces
    early = (r_up, r_down, r_gate, r_out)
    advance(r_up, r_gate, r_down, r_out)

    do_t[...] = jnp.zeros_like(do_t)
    for tile in range(8):
        if tile < 7:
            turned = flip(grad_mixed[:, tile * PAIR : (tile + 1) * PAIR])
        else:
            turned = flip(grad_mixed[:, tile * PAIR : tile * PAIR + HEAD_WIDTH])
        for side in range(2):
            head = 2 * tile + side
            if head < QUERY_HEADS:
                h, g = head // GROUP, head % GROUP
                do_t[h, HEAD_WIDTH:PAIR, g * BLOCK : (g + 1) * BLOCK] = turned[
                    side * HEAD_WIDTH : (side + 1) * HEAD_WIDTH
                ]
    for h in range(KEY_VALUE_HEADS):
        do_n[h] = flip(do_t[h])
        q_n[h] = flip(q_t[h])
        both = do_t[h, HEAD_WIDTH:PAIR].astype(F32) * o_t[h, HEAD_WIDTH:PAIR]
        delta[h] = jnp.broadcast_to(jnp.sum(both, axis=0, keepdims=True), (8, STACK))
    dq_t[...] = jnp.zeros_like(dq_t)

    def visit(j, diagonal):
        def per_head(h, carry):
            kv = kv_all[j, h]
            scores = dot(kv, q_t[h])
            if diagonal:
                key = lax.broadcasted_iota(jnp.int32, (BLOCK, STACK), 0)
                query = lax.broadcasted_iota(jnp.int32, (BLOCK, STACK), 1) % BLOCK
                scores = jnp.where(key <= query, scores, -1e30)
            probs = jnp.exp(scores - lse[h][0:1])
            grad_probs = dot(kv, do_t[h])
            grad_scores = (probs * (grad_probs - delta[h][0:1])).astype(BF16)
            both = dot(grad_scores, q_n[h]) + dot(probs.astype(BF16), do_n[h])
            dkv[j, h] = both.astype(BF16)
            dq_t[h] += dot(flip(kv), grad_scores)
            return carry

        lax.fori_loop(0, KEY_VALUE_HEADS, per_head, 0)


    for step in (3, 2, 1, 0):

        @pl.when((yl == 1) if step == 0 else (z - step >= 0))
        def _(step=step):
            j = col.other(-step)
            visit(j, False)
            kv_sems.push(step, dkv.at[j], beside.at[step], col.beside)

        if step == 3:
            pass
        if step == 2:
            advance(r_up)
        if step == 1:
            pass
        if step == 0:
            advance(r_down)
    for step in (3, 2, 1):

        @pl.when(z - step >= 0)
        def _(step=step):
            j = col.own(-step)
            visit(j, False)
            kv_sems.arrived(step, beside.at[step], col.beside)
            for h in range(KEY_VALUE_HEADS):
                total = dkv[j, h].astype(F32) + beside[step, h].astype(F32)
                dkv[j, h] = total.astype(BF16)
            kv_sems.push(3 + step, dkv.at[j], landed.at[step - 1], col.device(-step))

        if step == 3:
            pass
        if step == 2:
            pass
        if step == 1:
            pass
    visit(t, True)
    advance(r_gate, r_out)

    cos, sin = cosine[...], sine[...]

    def turn(tile):
        return tile * cos - swap_halves(tile) * sin

    for tile in range(8):
        pieces = []
        for head in (2 * tile, min(2 * tile + 1, QUERY_HEADS - 1)):
            h, g = head // GROUP, head % GROUP
            pieces.append(dq_t[h, 0:HEAD_WIDTH, g * BLOCK : (g + 1) * BLOCK])
        joined = turn(jnp.concatenate(pieces, axis=0).T * FACTOR)
        grad_qkv[:, tile * PAIR : (tile + 1) * PAIR] = joined.astype(BF16)
    rows = normed_t[...]
    for tile in range(Q_TILES):
        product = dot(rows, grad_qkv[:, tile * PAIR : (tile + 1) * PAIR])
        q_part[:, :, :, :, tile * PAIR : (tile + 1) * PAIR] = product.astype(BF16).reshape(
            2, 4, 2, PAD, PAIR
        )
    advance(r_q)
    advance(r_up)
    from_queries = dot_nt(
        grad_qkv[:, : Q_TILES * PAIR], q_w[...].reshape(PADDED, Q_TILES * PAIR)
    )

    @pl.when(yl == 0)
    def _():
        kv_sems.arrived(0, beside.at[0], col.beside)
        for h in range(KEY_VALUE_HEADS):
            total = dkv[t, h].astype(F32) + beside[0, h].astype(F32)
            dkv[t, h] = total.astype(BF16)

    for step in (1, 2, 3):

        @pl.when(z + step < 4)
        def _(step=step):
            kv_sems.arrived(3 + step, landed.at[step - 1], col.device(step))

    advance(r_q)
    low = low_half((BLOCK, PAIR))
    totals = []
    for h in range(KEY_VALUE_HEADS):

        def add(k, total, h=h):
            return total + landed[k, h].astype(F32)

        totals.append(lax.fori_loop(0, 3 - z, add, dkv[t, h].astype(F32)))
    zero = jnp.zeros((BLOCK, PAIR), F32)
    left = grad_qkv[:, 7 * PAIR : 8 * PAIR].astype(F32)
    first = turn(pltpu.roll(totals[0], HEAD_WIDTH, 1))
    grad_qkv[:, 7 * PAIR : 8 * PAIR] = jnp.where(low, left, first).astype(BF16)
    for n, (a, b) in enumerate(((1, 2), (3, 4))):
        keys = turn(jnp.where(low, totals[a], pltpu.roll(totals[b], HEAD_WIDTH, 1)))
        grad_qkv[:, (8 + n) * PAIR : (9 + n) * PAIR] = keys.astype(BF16)
    for n, (a, b) in enumerate(((0, 1), (2, 3), (4, None))):
        high = zero if b is None else totals[b]
        vals = jnp.where(low, pltpu.roll(totals[a], HEAD_WIDTH, 1), high)
        grad_qkv[:, (10 + n) * PAIR : (11 + n) * PAIR] = vals.astype(BF16)

    x = flat[...]
    scale = norm_scale(x)
    grad_normed = from_queries + dot_nt(
        grad_qkv[:, Q_TILES * PAIR :], kv_w[...].reshape(PADDED, KV_TILES * PAIR)
    )
    token_term, grad_gain = norm_back(grad_normed, x, scale, gain_row(kv_w, 0))
    row = lax.broadcasted_iota(jnp.int32, (8, PADDED), 0)
    gains = jnp.where(row == 0, grad_gain[None, :], jnp.where(row == 1, grad_gain_two[...], 0.0))
    lane = lax.broadcasted_iota(jnp.int32, (8, PAIR), 1)
    which = lax.broadcasted_iota(jnp.int32, (8, PAIR), 0)
    put = (lane == which + HEAD_WIDTH) & (which < 2)
    for tile in range(KV_TILES):
        at = Q_TILES + tile
        product = dot(rows, grad_qkv[:, at * PAIR : (at + 1) * PAIR])
        if tile == KV_TILES - 1:
            product = product + dot_tn(gains.astype(BF16), put.astype(BF16))
        kv_part[:, :, :, :, tile * PAIR : (tile + 1) * PAIR] = product.astype(BF16).reshape(
            2, 4, 2, PAD, PAIR
        )
    advance(r_kv)
    advance(r_down)
    d_tokens[...] = (grad_resid[...] + token_term).astype(BF16)

    drain(r_kv, r_q, *early)

    for step in (0, 1, 2, 3):

        @pl.when((yl == 1) if step == 0 else (z - step >= 0))
        def _(step=step):
            copy_wait(kv_sems, step, beside.at[step], col.beside)

    for step in (1, 2, 3):

        @pl.when(z - step >= 0)
        def _(step=step):
            copy_wait(kv_sems, 3 + step, landed.at[step - 1], col.device(-step))

    sems.finish()


REDUCE_SPLITS = (True, False, False, True)


def backward(parts, values, collective_id):
    vmem, hbm = pl.BlockSpec(memory_space=pltpu.VMEM), pl.BlockSpec(memory_space=pl.ANY)
    q_shape = (2, 4, 2, PAD, Q_TILES * PAIR)
    kv_shape = (2, 4, 2, PAD, KV_TILES * PAIR)
    shapes = [p.shape for p in parts] + [q_shape, kv_shape]
    scratch = [
        pltpu.VMEM((KEY_VALUE_HEADS, PAIR, STACK), BF16),
        pltpu.VMEM((KEY_VALUE_HEADS, STACK, PAIR), BF16),
        pltpu.VMEM((KEY_VALUE_HEADS, STACK, PAIR), BF16),
        pltpu.VMEM((KEY_VALUE_HEADS, PAIR, STACK), F32),
        pltpu.VMEM((KEY_VALUE_HEADS, 8, STACK), F32),
        pltpu.VMEM((8, KEY_VALUE_HEADS, BLOCK, PAIR), BF16),
        pltpu.VMEM((3, KEY_VALUE_HEADS, BLOCK, PAIR), BF16),
        pltpu.VMEM((4, KEY_VALUE_HEADS, BLOCK, PAIR), BF16),
        pltpu.VMEM((BLOCK, (Q_TILES + KV_TILES) * PAIR), BF16),
        pltpu.VMEM(q_shape, BF16),
        pltpu.VMEM(kv_shape, BF16),
        pltpu.SemaphoreType.DMA((6 * REDUCE_SEMS,)),
        pltpu.SemaphoreType.DMA((6 * REDUCE_SEMS,)),
        pltpu.SemaphoreType.DMA((6,)),
        pltpu.SemaphoreType.DMA((7,)),
        pltpu.SemaphoreType.DMA((7,)),
    ]
    for s, split in zip(shapes, REDUCE_SPLITS):
        scratch += reduce_scratch(*s[-2:], split)
    scratch += small_scratch(*q_shape[-2:]) + small_scratch(*kv_shape[-2:])
    return pl.pallas_call(
        backward_kernel,
        out_shape=[jax.ShapeDtypeStruct(s[-2:], BF16) for s in shapes]
        + [jax.ShapeDtypeStruct((BLOCK, PADDED), BF16)],
        in_specs=[hbm] * 4 + [vmem] * len(values),
        out_specs=[vmem] * 7,
        scratch_shapes=scratch,
        compiler_params=pltpu.CompilerParams(
            collective_id=collective_id, has_side_effects=True, vmem_limit_bytes=63 << 20
        ),
    )(*parts, *values)


def rotary_tables(token_positions):
    half = HEAD_WIDTH // 2
    freqs = ROPE_BASE ** (-jnp.arange(half, dtype=F32) * 2.0 / HEAD_WIDTH)
    angles = token_positions.astype(F32)[:, None] * freqs[None, :]
    cosine, sine = jnp.cos(angles), jnp.sin(angles)
    return (
        jnp.concatenate([cosine] * 4, axis=1),
        jnp.concatenate([-sine, sine] * 2, axis=1),
    )


def on_device(
    tokens,
    attn_gain,
    w_query,
    key_weight,
    value_weight,
    w_out,
    ffn_gain,
    w_gate,
    w_up,
    w_down,
    d_out,
):
    block = tokens.shape[1]
    token_positions = lax.axis_index("ctx") * block + jnp.arange(block, dtype=jnp.int32)
    cosine, sine = rotary_tables(token_positions)
    feature = jnp.arange(WIDTH, dtype=jnp.int32)
    place_of = feature // ROWS * PAD + feature % ROWS
    select = (place_of[:, None] == jnp.arange(PADDED, dtype=jnp.int32)[None, :]).astype(BF16)

    pad_rows = ((0, PAD - ROWS), (0, 0))
    qkv_shard = jnp.pad(
        jnp.concatenate(
            [w_query, key_weight, value_weight, attn_gain[:, None], ffn_gain[:, None]], axis=1
        ),
        ((0, PAD - ROWS), (0, (Q_TILES + KV_TILES) * PAIR - WIDTH - 2 * KV_WIDTH - 2)),
    )
    q_shard, kv_shard = qkv_shard[:, : Q_TILES * PAIR], qkv_shard[:, Q_TILES * PAIR :]
    out_shard = jnp.pad(dot(w_out, select).astype(BF16), pad_rows)
    gate_shard = jnp.pad(w_gate, pad_rows)
    up_shard = jnp.pad(w_up, pad_rows)
    down_shard = dot(w_down, select).astype(BF16)

    flat = dot(tokens[0], select)
    grad_flat = dot(d_out[0], select).astype(BF16)
    shards = (kv_shard, q_shard, out_shard, gate_shard, up_shard, down_shard)
    kv_w, q_w, out_w, gate_w, up_w, down_w, normed_t, q_t, kv_all, o_t, lse, mixed, gain_two = forward(
        flat, cosine, sine, shards, 0
    )
    out_w, gate_w, up_w = (w.reshape(PADDED, -1) for w in (out_w, gate_w, up_w))
    down_w = down_w.reshape(-1, PADDED)
    output, grad_resid, grad_gain_two, grad_mixed, *parts = middle(
        (flat, grad_flat, mixed, gain_two, select, out_w), (gate_w, up_w, down_w), 2
    )
    sum_gate, sum_up, sum_down, sum_out, sum_q, sum_kv, d_tokens = backward(
        parts,
        (
            flat,
            grad_resid,
            grad_gain_two,
            cosine,
            sine,
            kv_w,
            q_w,
            normed_t,
            q_t,
            kv_all,
            o_t,
            lse,
            grad_mixed,
        ),
        1,
    )
    d_tokens = dot_nt(d_tokens, select).astype(BF16)
    sum_qkv = jnp.concatenate([sum_q, sum_kv], axis=1)[:ROWS].astype(F32)
    ends = (WIDTH, WIDTH + KV_WIDTH, WIDTH + 2 * KV_WIDTH)
    return (
        output[None],
        d_tokens[None],
        sum_qkv[:, ends[2]],
        sum_qkv[:, : ends[0]],
        sum_qkv[:, ends[0] : ends[1]],
        sum_qkv[:, ends[1] : ends[2]],
        dot_nt(sum_out[:ROWS], select),
        sum_qkv[:, ends[2] + 1],
        sum_gate[:ROWS].astype(F32),
        sum_up[:ROWS].astype(F32),
        dot_nt(sum_down, select),
    )


def solution(mesh):
    rows, whole, line = P("fsdp", None), P("fsdp", "ctx", None), P("fsdp")
    weights = (line, rows, rows, rows, rows, line, rows, rows, rows)
    return jax.shard_map(
        on_device,
        mesh=mesh,
        in_specs=(whole, *weights, whole),
        out_specs=(whole, whole, *weights),
        check_vma=False,
    )
```

```python
import functools
import math

import jax
import jax.numpy as jnp
from jax import lax
from jax.experimental import pallas as pl
from jax.experimental.pallas import tpu as pltpu
from jax.sharding import PartitionSpec as P

QUERY_HEADS = 15
KEY_VALUE_HEADS = 5
HEAD_WIDTH = 64
GROUP = QUERY_HEADS // KEY_VALUE_HEADS
WIDTH = 960
ROWS = 60
PAD = 64
SHARDS = 16
PADDED = SHARDS * PAD
KV_WIDTH = KEY_VALUE_HEADS * HEAD_WIDTH
Q_TILES = 7
KV_TILES = 6

EPS = 1e-05
ROPE_BASE = 10000.0
MESH = pl.DeviceIdType.MESH
BF16 = jnp.bfloat16
F32 = jnp.float32


def place():
    f, t = lax.axis_index("fsdp"), lax.axis_index("ctx")
    return f // 8, (f // 2) % 4, f % 2, t // 2, t % 2


def device(yh, x, c, z, yl):
    return ((yh * 4 + x) * 2 + c, z * 2 + yl)


class Places:
    def __init__(self):
        yh, x, c, z, yl = place()
        self.yh, self.x, self.c, self.z, self.yl = yh, x, c, z, yl
        self.sib = device(yh, x, 1 - c, z, yl)
        self.ypair = device(1 - yh, x, c, z, 1 - yl)
        self.ylo = device(yh, x, c, z, 1 - yl)
        self.xs = [(x + 1) % 4, (x + 3) % 4, (x + 2) % 4]
        self.zs = [(z + 1) % 4, (z + 3) % 4, (z + 2) % 4]
        self.xdiag = [device(1 - yh, k, c, z, 1 - yl) for k in self.xs]
        self.zdiag = [device(yh, x, c, k, 1 - yl) for k in self.zs]
        self.xdev = [device(yh, k, c, z, yl) for k in self.xs]
        self.zdev = [device(yh, x, c, k, yl) for k in self.zs]
        self.xfrom = [self.xs[1], self.xs[0], self.xs[2]]
        self.zfrom = [self.zs[1], self.zs[0], self.zs[2]]


def greet(devices):
    barrier = pltpu.get_barrier_semaphore()
    for d in devices:
        pl.semaphore_signal(barrier, inc=1, device_id=d, device_id_type=MESH)
    pl.semaphore_wait(barrier, len(devices))


class Sems:
    def __init__(self, send, recv):
        self.send, self.recv, self.at, self.open = send, recv, 0, []

    def take(self, count=1):
        at = self.at
        self.at += count
        return at

    def push(self, slot, src, dst, dev):
        copy = pltpu.make_async_remote_copy(
            src_ref=src,
            dst_ref=dst,
            send_sem=self.send.at[slot],
            recv_sem=self.recv.at[slot],
            device_id=dev,
            device_id_type=MESH,
        )
        copy.start()
        self.open.append(copy)

    def arrived(self, slot, dst, dev):
        pltpu.make_async_remote_copy(
            src_ref=dst,
            dst_ref=dst,
            send_sem=self.send.at[slot],
            recv_sem=self.recv.at[slot],
            device_id=dev,
            device_id_type=MESH,
        ).wait_recv()

    def finish(self):
        for copy in self.open:
            copy.wait_send()
        self.open = []


GATHER_SEMS = 24


def gather_steps(pc, sems, local_sem, shard, out, split):
    rows = shard.shape[0]
    quarter = rows // 4
    yh, x, c, z = pc.yh, pc.x, pc.c, pc.z
    s_y = sems.take()
    s_x = [[sems.take() for _ in range(2)] for _ in range(3)]
    s_z = [[sems.take() for _ in range(3)] for _ in range(3)] if split else None
    s_s = [sems.take() for _ in range(4)]
    band = pl.ds(pl.multiple_of(z * quarter, 16), quarter) if split else pl.ds(0, rows)
    straight = (0, 1, 2) if split else (0, 1)

    own = pltpu.make_async_copy(shard, out.at[yh, x, c], local_sem)
    own.start()
    sems.push(s_y, shard, out.at[yh, x, c], pc.ypair)
    yield
    for k in straight:
        sems.push(s_x[k][0], shard.at[band], out.at[yh, x, c, band], pc.xdev[k])
    yield
    sems.arrived(s_y, out.at[1 - yh, x, c], pc.ypair)
    for k in straight:
        piece = out.at[1 - yh, x, c, band]
        sems.push(s_x[k][1], piece, piece, pc.xdev[k])
    own.wait()
    sems.push(s_s[3], out.at[:, x, c], out.at[:, x, c], pc.sib)
    yield
    for k in straight:
        far = pc.xfrom[k]
        sems.arrived(s_x[k][0], out.at[yh, far, c, band], pc.xdev[k])
        sems.arrived(s_x[k][1], out.at[1 - yh, far, c, band], pc.xdev[k])
        if split:
            piece = out.at[:, far, c, band]
            for j in range(3):
                sems.push(s_z[k][j], piece, piece, pc.zdev[j])
        else:
            piece = out.at[k, far, c]
            sems.push(s_x[2][k], piece, piece, pc.xdev[k])
            sems.push(s_s[k], out.at[:, far, c], out.at[:, far, c], pc.sib)
    yield
    if split:
        for k in (0, 1, 2):
            far = pc.xfrom[k]
            for j in range(3):
                there = pl.ds(pl.multiple_of(pc.zfrom[j] * quarter, 16), quarter)
                sems.arrived(s_z[k][j], out.at[:, far, c, there], pc.zdev[j])
            sems.push(s_s[k], out.at[:, far, c], out.at[:, far, c], pc.sib)
    else:
        far = pc.xs[2]
        for k in (0, 1):
            sems.arrived(s_x[2][k], out.at[k, far, c], pc.xdev[k])
        sems.push(s_s[2], out.at[:, far, c], out.at[:, far, c], pc.sib)
    yield
    for k in (0, 1, 2, 3):
        far = x if k == 3 else pc.xfrom[k]
        sems.arrived(s_s[k], out.at[:, far, 1 - c], pc.sib)
    yield


def run_all(steps):
    live = list(steps)
    while live:
        for s in list(live):
            try:
                next(s)
            except StopIteration:
                live.remove(s)


REDUCE_SEMS = 32


def add_rows(dst, terms, shape):
    lead, rows = shape[:-2], shape[-2]
    blocks = rows // 16
    count = math.prod(lead) * blocks

    def body(i, carry):
        idx, rest = [], i // blocks
        for size in reversed(lead):
            idx.append(rest % size)
            rest = rest // size
        idx = tuple(reversed(idx))
        at = (*idx, pl.ds(pl.multiple_of((i % blocks) * 16, 16), 16))
        total = dst[at].astype(F32)
        for term in terms:
            total = total + term[at].astype(F32)
        dst[at] = total.astype(BF16)
        return carry

    lax.fori_loop(0, count, body, 0)


def reduce_scratch(rows, width, split):
    q = rows // 4
    return [
        pltpu.VMEM((2, 4, rows, width), BF16),
        pltpu.VMEM((3 if split else 2, 2, q if split else rows, width), BF16),
        pltpu.VMEM((rows, width), BF16),
        pltpu.VMEM((rows // 2, width), BF16),
        pltpu.VMEM((3, rows // 2, width // 4), BF16),
        pltpu.VMEM((3, 3, 2, q, width) if split else (2, rows, width), BF16),
    ]


def reduce_steps(pc, sems, local_sem, part, final, buffers, split):
    yh, x, c, z, yl = pc.yh, pc.x, pc.c, pc.z, pc.yl
    acc, from_x, from_y, from_l, from_z, from_r = buffers
    rows, width = part.shape[-2:]
    q = rows // 4
    s_y, s_l, s_m = (sems.take() for _ in range(3))
    s_x = [sems.take() for _ in range(3)]
    s_z = [sems.take() for _ in range(3)]
    s_f = [sems.take() for _ in range(3)]
    s_r = [[sems.take() for _ in range(3)] for _ in range(3)]

    def band(k):
        return pl.ds(pl.multiple_of(k * q, 16), q)

    own = pltpu.make_async_copy(part, acc, local_sem)
    own.start()
    own.wait()
    if split:
        here = band(z)
        order = (2, 0, 1)
        for k in order:
            for j in range(3):
                piece = acc.at[:, pc.xs[k], band(pc.zs[j])]
                sems.push(s_r[k][j], piece, from_r.at[j, k], pc.zdev[j])
        yield
        for k in order:
            for j in range(3):
                sems.arrived(s_r[k][j], from_r.at[j, k], pc.zdev[j])
            mine = acc.at[:, pc.xs[k], here]
            add_rows(mine, [from_r.at[j, k] for j in range(3)], (2, q, width))
            sems.push(s_x[k], mine, from_x.at[k], pc.xdev[k])
        yield
        for k in range(3):
            sems.arrived(s_x[k], from_x.at[k], pc.xdev[k])
        add_rows(acc.at[:, x, here], [from_x.at[k] for k in range(3)], (2, q, width))
    else:
        for k in range(2):
            sems.push(s_r[0][k], acc.at[k, pc.xs[2]], from_r.at[k], pc.xdev[k])
        yield
        for k in range(2):
            sems.arrived(s_r[0][k], from_r.at[k], pc.xdev[k])
            add_rows(acc.at[k, pc.xs[k]], [from_r.at[k]], (rows, width))
            sems.push(s_x[k], acc.at[:, pc.xs[k]], from_x.at[k], pc.xdev[k])
        yield
        for k in range(2):
            sems.arrived(s_x[k], from_x.at[k], pc.xdev[k])
        add_rows(acc.at[:, x], [from_x.at[k] for k in range(2)], (2, rows, width))
    sems.push(s_y, acc.at[1 - yh, x], from_y, pc.ypair)
    yield
    sems.arrived(s_y, from_y, pc.ypair)
    mine = acc.at[yh, x]
    add_rows(mine, [from_y], (rows, width))
    h, w = rows // 2, width // 4
    half = pl.ds(pl.multiple_of(yl * h, 16), h)
    other = pl.ds(pl.multiple_of((1 - yl) * h, 16), h)

    def column(k):
        return pl.ds(pl.multiple_of(k * w, 128), w)

    sems.push(s_l, acc.at[yh, x, other], from_l, pc.ylo)
    yield
    sems.arrived(s_l, from_l, pc.ylo)
    add_rows(acc.at[yh, x, half], [from_l], (h, width))
    for j in range(3):
        piece = acc.at[yh, x, half, column(pc.zs[j])]
        sems.push(s_z[j], piece, from_z.at[j], pc.zdev[j])
    yield
    for j in range(3):
        sems.arrived(s_z[j], from_z.at[j], pc.zdev[j])
    mine = acc.at[yh, x, half, column(z)]
    add_rows(mine, [from_z.at[j] for j in range(3)], (h, w))
    done = final.at[half, column(z)]
    done[...] = mine[...]
    for j in range(3):
        sems.push(s_f[j], done, done, pc.zdev[j])
    yield
    for j in range(3):
        sems.arrived(s_f[j], final.at[half, column(pc.zfrom[j])], pc.zdev[j])
    sems.push(s_m, final.at[half], final.at[half], pc.ylo)
    yield
    sems.arrived(s_m, final.at[other], pc.ylo)
    yield


def small_scratch(rows, width):
    q = rows // 4
    return [
        pltpu.VMEM((2, 4, rows, width), BF16),
        pltpu.VMEM((2, 4, rows, width), BF16),
        pltpu.VMEM((3, 2, 4, q, width), BF16),
        pltpu.VMEM((7, q, width), BF16),
        pltpu.VMEM((2, rows, width), BF16),
    ]


def small_steps(pc, sems, local_sem, part, final, buffers):
    yh, x, c, z, yl = pc.yh, pc.x, pc.c, pc.z, pc.yl
    acc, from_sib, from_z, from_xy, landed = buffers
    rows, width = part.shape[-2:]
    q = rows // 4
    s_s = sems.take()
    s_z = [sems.take() for _ in range(3)]
    s_xy = [sems.take() for _ in range(7)]
    s_f = [sems.take() for _ in range(7)]

    def band(k):
        return pl.ds(pl.multiple_of(k * q, 16), q)

    here = band(z)
    own = pltpu.make_async_copy(part.at[:, :, c], acc, local_sem)
    own.start()
    sems.push(s_s, part.at[:, :, 1 - c], from_sib, pc.sib)
    yield
    own.wait()
    sems.arrived(s_s, from_sib, pc.sib)
    add_rows(acc, [from_sib], acc.shape)
    for j in range(3):
        sems.push(s_z[j], acc.at[:, :, band(pc.zs[j])], from_z.at[j], pc.zdev[j])
    yield
    for j in range(3):
        sems.arrived(s_z[j], from_z.at[j], pc.zdev[j])
    add_rows(acc.at[:, :, here], [from_z.at[j] for j in range(3)], (2, 4, q, width))
    targets = [(yh, pc.xs[k], yl) for k in range(3)]
    targets += [(1 - yh, k, 1 - yl) for k in (*pc.xs, x)]
    for n, (there, k, side) in enumerate(targets):
        sems.push(s_xy[n], acc.at[there, k, here], from_xy.at[n], device(there, k, c, z, side))
    yield
    for n in range(7):
        sems.arrived(s_xy[n], from_xy.at[n], pc.sib)
    mine = acc.at[yh, x, here]
    add_rows(mine, [from_xy.at[n] for n in range(7)], (q, width))
    landed[yl, here] = mine[...]
    for n, (k, side) in enumerate([(k, yl) for k in pc.zs] + [(k, 1 - yl) for k in (*pc.zs, z)]):
        sems.push(s_f[n], mine, landed.at[yl, here], device(yh, x, c, k, side))
    yield
    for n, (k, side) in enumerate(
        [(k, yl) for k in pc.zfrom] + [(k, 1 - yl) for k in (*pc.zfrom, z)]
    ):
        sems.arrived(s_f[n], landed.at[side, band(k)], pc.sib)

    def body(i, carry):
        at = pl.ds(pl.multiple_of(i * 16, 16), 16)
        total = landed[0, at].astype(F32) + landed[1, at].astype(F32)
        final[at] = total.astype(BF16)
        return carry

    lax.fori_loop(0, rows // 16, body, 0)
    yield


class Column:
    def __init__(self, pc):
        self.z, self.yl = pc.z, pc.yl
        self.t = 2 * pc.z + pc.yl
        self.beside = pc.ylo
        self.pc = pc

    def own(self, step):
        return 2 * (self.z + step) + self.yl

    def other(self, step):
        return 2 * (self.z + step) + 1 - self.yl

    def device(self, step):
        pc = self.pc
        return device(pc.yh, pc.x, pc.c, (pc.z + step + 4) % 4, pc.yl)


def dot(a, b):
    return jnp.dot(a, b, preferred_element_type=F32)


def dot_tn(a, b):
    return lax.dot_general(a, b, (((0,), (0,)), ((), ())), preferred_element_type=F32)


def dot_nt(a, b):
    return lax.dot_general(a, b, (((1,), (1,)), ((), ())), preferred_element_type=F32)


def norm_scale(rows):
    return lax.rsqrt(jnp.sum(rows * rows, axis=-1, keepdims=True) * (1.0 / WIDTH) + EPS)


def norm_back(grad_normed, rows, scale, gain):
    unit = rows * scale
    grad_gain = jnp.sum(grad_normed * unit, axis=0)
    grad_unit = grad_normed * gain
    mean = jnp.sum(grad_unit * unit, axis=-1, keepdims=True) * (1.0 / WIDTH)
    return scale * (grad_unit - unit * mean), grad_gain


BLOCK = 256
PAIR = 2 * HEAD_WIDTH
STACK = GROUP * BLOCK
FACTOR = HEAD_WIDTH ** (-0.5)


def low_half(shape):
    return lax.broadcasted_iota(jnp.int32, shape, 1) % PAIR < HEAD_WIDTH


def swap_halves(tile):
    lane = lax.broadcasted_iota(jnp.int32, tile.shape, 1) % HEAD_WIDTH
    half = HEAD_WIDTH // 2
    return jnp.where(
        lane < half, pltpu.roll(tile, PAIR - half, 1), pltpu.roll(tile, half, 1)
    )


def flip(a):
    return a.astype(F32).T.astype(a.dtype)


def advance(*steps):
    for s in steps:
        next(s, None)


def drain(*steps):
    run_all(steps)


def tile_of(ref, tile):
    return ref[:, :, :, :, tile * PAIR : (tile + 1) * PAIR].reshape(PADDED, PAIR)


def gain_row(kv_w, which):
    pick = lax.broadcasted_iota(jnp.int32, (8, PAIR), 1) == HEAD_WIDTH + which
    return dot_nt(pick.astype(BF16), tile_of(kv_w, KV_TILES - 1))[0:1]


def copy_wait(sems, slot, ref, dev):
    pltpu.make_async_remote_copy(
        src_ref=ref,
        dst_ref=ref,
        send_sem=sems.send.at[slot],
        recv_sem=sems.recv.at[slot],
        device_id=dev,
        device_id_type=MESH,
    ).wait_send()


def forward_kernel(
    tokens,
    cosine,
    sine,
    select,
    kv_shard,
    q_shard,
    own_out,
    own_gate,
    own_up,
    own_down,
    kv_w,
    q_w,
    out_w,
    gate_w,
    up_w,
    down_w,
    normed_t,
    q_t,
    kv_all,
    o_t,
    lse,
    mixed,
    gain_two,
    flat,
    peak,
    wide,
    out_shard,
    gate_shard,
    up_shard,
    down_shard,
    send,
    recv,
    local,
    kv_send,
    kv_recv,
):
    pc = Places()
    col = Column(pc)
    t, z, yl = col.t, pc.z, pc.yl
    greet([pc.sib, pc.ypair, pc.ylo, *pc.xdev, *pc.zdev])
    sems, kv_sems = Sems(send, recv), Sems(kv_send, kv_recv)
    g_kv = gather_steps(pc, sems, local.at[0], kv_shard, kv_w, True)
    g_q = gather_steps(pc, sems, local.at[1], q_shard, q_w, False)
    g_out = gather_steps(pc, sems, local.at[2], out_shard, out_w, False)
    g_gate = gather_steps(pc, sems, local.at[3], gate_shard, gate_w, True)
    g_up = gather_steps(pc, sems, local.at[4], up_shard, up_w, True)
    g_down = gather_steps(pc, sems, local.at[5], down_shard, down_w, False)
    advance(g_kv, g_kv, g_q)
    ones = (
        lax.broadcasted_iota(jnp.int32, (PAD, ROWS), 0)
        == lax.broadcasted_iota(jnp.int32, (PAD, ROWS), 1)
    ).astype(BF16)
    gate_shard[...] = dot(ones, own_gate[...]).astype(BF16)
    advance(g_gate, g_gate)
    up_shard[...] = dot(ones, own_up[...]).astype(BF16)
    advance(g_up)
    down_shard[...] = dot(own_down[...], select[...]).astype(BF16)
    out_shard[...] = dot(ones, dot(own_out[...], select[...]).astype(BF16)).astype(BF16)
    x = dot(tokens[...], select[...])
    flat[...] = x
    scale = norm_scale(x)
    advance(g_kv, g_q)
    advance(g_kv, g_q, g_gate, g_up)
    advance(g_kv, g_out, g_down)
    advance(g_kv)

    rows = (x * scale * gain_row(kv_w, 0)).astype(BF16)
    gain_two[...] = gain_row(kv_w, 1)
    cos, sin = cosine[...], sine[...]
    low = low_half((BLOCK, PAIR))

    def place_queries(product, tile):
        turned = (product * FACTOR).T.astype(BF16)
        for side in range(2):
            head = 2 * tile + side
            if head < QUERY_HEADS:
                h, g = head // GROUP, head % GROUP
                at = slice(g * BLOCK, (g + 1) * BLOCK)
                q_t[h, 0:HEAD_WIDTH, at] = turned[side * HEAD_WIDTH : (side + 1) * HEAD_WIDTH]
                q_t[h, HEAD_WIDTH:PAIR, at] = jnp.zeros((HEAD_WIDTH, BLOCK), BF16)

    for tile in range(KV_TILES):
        product = dot(rows, tile_of(kv_w, tile))
        if tile < 3:
            product = product * cos + swap_halves(product) * sin
        wide[tile] = product
    for h in range(KEY_VALUE_HEADS):
        k_tile, k_high = (h + 1) // 2, (h + 1) % 2
        v_tile, v_high = 3 + h // 2, h % 2
        k_part, v_part = wide[k_tile], wide[v_tile]
        if k_high:
            k_part = pltpu.roll(k_part, HEAD_WIDTH, 1)
        if not v_high:
            v_part = pltpu.roll(v_part, HEAD_WIDTH, 1)
        kv_all[t, h] = jnp.where(low, k_part, v_part).astype(BF16)
    for step in (1, 2, 3):

        @pl.when(z + step < 4)
        def _(step=step):
            kv_sems.push(step - 1, kv_all.at[t], kv_all.at[t], col.device(step))

    @pl.when(yl == 0)
    def _():
        kv_sems.push(3, kv_all.at[t], kv_all.at[t], col.beside)

    advance(g_gate, g_up, g_q)
    advance(g_out, g_down)
    place_queries(wide[0], 7)
    normed_t[...] = flip(rows)
    advance(g_q, g_up, g_q)
    for tile in range(Q_TILES):
        product = dot(rows, tile_of(q_w, tile))
        place_queries(product * cos + swap_halves(product) * sin, tile)
    peak[...] = jnp.full_like(peak, -1e30)
    o_t[...] = jnp.zeros_like(o_t)

    def visit(j, diagonal):
        def per_head(h, carry):
            kv = kv_all[j, h]
            kv_t = flip(kv)
            ones = lax.broadcasted_iota(jnp.int32, (PAIR, BLOCK), 0) < HEAD_WIDTH
            ones_v = jnp.where(ones, 1.0, kv_t.astype(F32)).astype(BF16)
            scores = dot(kv, q_t[h])
            if diagonal:
                key = lax.broadcasted_iota(jnp.int32, (BLOCK, STACK), 0)
                query = lax.broadcasted_iota(jnp.int32, (BLOCK, STACK), 1) % BLOCK
                scores = jnp.where(key <= query, scores, -1e30)
            old = peak[h]
            new = jnp.maximum(old, jnp.max(scores, axis=0, keepdims=True))
            probs = jnp.exp(scores - new[0:1]).astype(BF16)
            o_t[h] = o_t[h] * jnp.exp(old - new)[0:1] + dot(ones_v, probs)
            peak[h] = new
            return carry

        lax.fori_loop(0, KEY_VALUE_HEADS, per_head, 0)

    advance(g_out, g_down)
    visit(t, True)
    for step in (1, 2, 3):

        @pl.when(z - step >= 0)
        def _(step=step):
            block = kv_all.at[col.own(-step)]
            kv_sems.arrived(step - 1, block, col.device(-step))
            kv_sems.push(3 + step, block, block, col.beside)
            visit(col.own(-step), False)

        if step == 1:
            advance(g_out, g_down)
        if step == 2:
            advance(g_gate)
        if step == 3:
            advance(g_out, g_down)
    for step in (0, 1, 2, 3):

        @pl.when((yl == 1) if step == 0 else (z - step >= 0))
        def _(step=step):
            block = kv_all.at[col.other(-step)]
            kv_sems.arrived(3 + step, block, col.beside)
            visit(col.other(-step), False)

        if step == 1:
            advance(g_up)

    for h in range(KEY_VALUE_HEADS):
        total = o_t[h, 0:1]
        o_t[h] = o_t[h] * (1.0 / total)
        lse[h] = peak[h] + jnp.log(total)
    for tile in range(8):
        parts = []
        for head in (2 * tile, min(2 * tile + 1, QUERY_HEADS - 1)):
            h, g = head // GROUP, head % GROUP
            parts.append(o_t[h, HEAD_WIDTH:PAIR, g * BLOCK : (g + 1) * BLOCK])
        joined = jnp.concatenate(parts, axis=0).T.astype(BF16)
        if tile < 7:
            mixed[:, tile * PAIR : (tile + 1) * PAIR] = joined
        else:
            mixed[:, tile * PAIR : tile * PAIR + HEAD_WIDTH] = joined[:, :HEAD_WIDTH]
    drain(g_gate, g_up, g_down, g_out)
    for step in (1, 2, 3):

        @pl.when(z + step < 4)
        def _(step=step):
            copy_wait(kv_sems, step - 1, kv_all.at[t], col.device(step))

        @pl.when(z - step >= 0)
        def _(step=step):
            copy_wait(kv_sems, 3 + step, kv_all.at[t], col.beside)

    @pl.when(yl == 0)
    def _():
        copy_wait(kv_sems, 3, kv_all.at[t], col.beside)

    sems.finish()


def forward(values, shards, weights, collective_id):
    vmem, hbm = pl.BlockSpec(memory_space=pltpu.VMEM), pl.BlockSpec(memory_space=pl.ANY)
    rows = [PAD, PAD, PAD, PAD, PAD, weights[3].shape[0]]
    widths = [s.shape[1] for s in shards] + [PADDED, weights[1].shape[1], weights[2].shape[1], PADDED]
    padded = list(zip(rows, widths))
    gathered = [jax.ShapeDtypeStruct((2, 4, 2, *p), BF16) for p in padded]
    return pl.pallas_call(
        forward_kernel,
        out_shape=[
            *gathered,
            jax.ShapeDtypeStruct((PADDED, BLOCK), BF16),
            jax.ShapeDtypeStruct((KEY_VALUE_HEADS, PAIR, STACK), BF16),
            jax.ShapeDtypeStruct((8, KEY_VALUE_HEADS, BLOCK, PAIR), BF16),
            jax.ShapeDtypeStruct((KEY_VALUE_HEADS, PAIR, STACK), F32),
            jax.ShapeDtypeStruct((KEY_VALUE_HEADS, 8, STACK), F32),
            jax.ShapeDtypeStruct((BLOCK, WIDTH), BF16),
            jax.ShapeDtypeStruct((1, PADDED), F32),
            jax.ShapeDtypeStruct((BLOCK, PADDED), F32),
        ],
        in_specs=[vmem] * 4 + [hbm] * 2 + [vmem] * 4,
        out_specs=[vmem] * 2 + [hbm] * 4 + [vmem] * 8,
        scratch_shapes=[
            pltpu.VMEM((KEY_VALUE_HEADS, 8, STACK), F32),
            pltpu.VMEM((KV_TILES, BLOCK, PAIR), F32),
            *[pltpu.VMEM(p, BF16) for p in padded[2:]],
            pltpu.SemaphoreType.DMA((6 * GATHER_SEMS,)),
            pltpu.SemaphoreType.DMA((6 * GATHER_SEMS,)),
            pltpu.SemaphoreType.DMA((6,)),
            pltpu.SemaphoreType.DMA((7,)),
            pltpu.SemaphoreType.DMA((7,)),
        ],
        compiler_params=pltpu.CompilerParams(
            collective_id=collective_id, has_side_effects=True, vmem_limit_bytes=60 << 20
        ),
    )(*values, *shards, *weights)


PARTS = 4
STEP = 640


def middle_kernel(
    flat,
    d_out,
    mixed,
    gain_two,
    select,
    out_w,
    gate_w,
    up_w,
    down_w,
    output,
    grad_resid,
    grad_gain_two,
    grad_mixed,
    gate_acc,
    up_acc,
    down_acc,
    out_acc,
    gate_buf,
    up_buf,
    down_buf,
    gate_stage,
    up_stage,
    down_stage,
    out_stage,
    gate_sib,
    up_sib,
    down_sib,
    out_sib,
    total,
    back,
    load,
    local,
    send,
    recv,
):
    pc = Places()
    c = pc.c

    def loads(i):
        at = pl.ds(i * STEP, STEP)
        slot = i % 2
        return (
            pltpu.make_async_copy(gate_w.at[:, at], gate_buf.at[slot], load.at[slot, 0]),
            pltpu.make_async_copy(up_w.at[:, at], up_buf.at[slot], load.at[slot, 1]),
            pltpu.make_async_copy(down_w.at[at], down_buf.at[slot], load.at[slot, 2]),
        )

    def remote(src, dst, k):
        return pltpu.make_async_remote_copy(
            src_ref=src,
            dst_ref=dst,
            send_sem=send.at[k],
            recv_sem=recv.at[k],
            device_id=pc.sib,
            device_id_type=MESH,
        )

    def sends(i):
        at, slot = pl.ds(i * STEP, STEP), i % 2
        yh, xs = i // 2, pl.ds(2 * (i % 2), 2)
        gate, up, down = gate_stage.at[slot], up_stage.at[slot], down_stage.at[slot]
        return (
            remote(gate.at[:, :, 1 - c], gate_sib.at[:, :, :, at], 3 * i),
            remote(up.at[:, :, 1 - c], up_sib.at[:, :, :, at], 3 * i + 1),
            remote(down.at[:, 1 - c], down_sib.at[yh, xs], 3 * i + 2),
            pltpu.make_async_copy(gate.at[:, :, c], gate_acc.at[:, :, :, at], local.at[slot, 0]),
            pltpu.make_async_copy(up.at[:, :, c], up_acc.at[:, :, :, at], local.at[slot, 1]),
            pltpu.make_async_copy(down.at[:, c], down_acc.at[yh, xs], local.at[slot, 2]),
        )

    def sent(i):
        copies = sends(i)
        for copy in copies[:3]:
            copy.wait_send()
        for copy in copies[3:]:
            copy.wait()

    for copy in loads(0):
        copy.start()
    greet([pc.sib])
    mixed_p = dot(mixed[...], select[...]).astype(BF16)
    resid = flat[...] + dot(mixed_p, out_w[...])
    scale = norm_scale(resid)
    gain = gain_two[...]
    normed = (resid * scale * gain).astype(BF16)
    normed_t = flip(normed)
    grad = dot(d_out[...], select[...]).astype(BF16)
    total[...] = resid
    back[...] = jnp.zeros_like(back)
    for i in range(PARTS):
        slot = i % 2
        if i + 1 < PARTS:
            for copy in loads(i + 1):
                copy.start()
        for copy in loads(i):
            copy.wait()
        if i >= 2:
            sent(i - 2)
        w_gate, w_up, w_down = gate_buf[slot], up_buf[slot], down_buf[slot]
        gate = dot(normed, w_gate)
        up = dot(normed, w_up)
        grad_hidden = dot_nt(grad, w_down)
        sigmoid = 0.5 * jnp.tanh(0.5 * gate) + 0.5
        swish = gate * sigmoid
        hidden = (swish * up).astype(BF16)
        grad_up_v = (grad_hidden * swish).astype(BF16)
        grad_gate_v = (grad_hidden * up * sigmoid * (1.0 + gate * (1.0 - sigmoid))).astype(BF16)
        total[...] += dot(hidden, w_down)
        back[...] += dot_nt(grad_gate_v, w_gate) + dot_nt(grad_up_v, w_up)
        shape = (2, 4, 2, PAD, STEP)
        gate_stage[slot] = dot(normed_t, grad_gate_v).astype(BF16).reshape(shape)
        up_stage[slot] = dot(normed_t, grad_up_v).astype(BF16).reshape(shape)
        down = dot(flip(hidden), grad).astype(BF16)
        down_stage[slot] = down.reshape(2, 2, STEP // 4, PADDED)
        for copy in sends(i):
            copy.start()
    output[...] = dot_nt(total[...].astype(BF16), select[...]).astype(BF16)
    term, grad_gain = norm_back(back[...], resid, scale, gain)
    grad_gain_two[...] = grad_gain[None, :]
    full = grad.astype(F32) + term
    grad_resid[...] = full
    branch = full.astype(BF16)
    out_stage[...] = dot(flip(mixed_p), branch).astype(BF16).reshape(2, 4, 2, PAD, PADDED)
    out_send = remote(out_stage.at[:, :, 1 - c], out_sib, 3 * PARTS)
    out_send.start()
    out_copy = pltpu.make_async_copy(out_stage.at[:, :, c], out_acc, local.at[0, 3])
    out_copy.start()
    inner = dot_nt(branch, out_w[...]).astype(BF16)
    grad_mixed[...] = dot_nt(inner, select[...]).astype(BF16)
    for i in (PARTS - 2, PARTS - 1):
        sent(i)
    for i in range(PARTS):
        for copy in sends(i)[:3]:
            copy.wait_recv()
    add_rows(gate_acc, [gate_sib], gate_acc.shape)
    add_rows(up_acc, [up_sib], up_acc.shape)
    add_rows(down_acc, [down_sib], down_acc.shape)
    out_send.wait()
    out_copy.wait()
    add_rows(out_acc, [out_sib], out_acc.shape)


def middle(values, weights, collective_id):
    vmem, hbm = pl.BlockSpec(memory_space=pltpu.VMEM), pl.BlockSpec(memory_space=pl.ANY)
    hidden = weights[0].shape[1]
    tall = hidden // SHARDS
    accs = [(2, 4, PAD, hidden), (2, 4, PAD, hidden), (2, 4, tall, PADDED), (2, 4, PAD, PADDED)]
    return pl.pallas_call(
        middle_kernel,
        out_shape=[
            jax.ShapeDtypeStruct((BLOCK, WIDTH), BF16),
            jax.ShapeDtypeStruct((BLOCK, PADDED), F32),
            jax.ShapeDtypeStruct((1, PADDED), F32),
            jax.ShapeDtypeStruct((BLOCK, WIDTH), BF16),
            *[jax.ShapeDtypeStruct(a, BF16) for a in accs],
        ],
        in_specs=[vmem] * len(values) + [hbm] * 3,
        out_specs=[vmem] * 8,
        scratch_shapes=[
            pltpu.VMEM((2, PADDED, STEP), BF16),
            pltpu.VMEM((2, PADDED, STEP), BF16),
            pltpu.VMEM((2, STEP, PADDED), BF16),
            pltpu.VMEM((2, 2, 4, 2, PAD, STEP), BF16),
            pltpu.VMEM((2, 2, 4, 2, PAD, STEP), BF16),
            pltpu.VMEM((2, 2, 2, STEP // 4, PADDED), BF16),
            pltpu.VMEM((2, 4, 2, PAD, PADDED), BF16),
            *[pltpu.VMEM(a, BF16) for a in accs],
            pltpu.VMEM((BLOCK, PADDED), F32),
            pltpu.VMEM((BLOCK, PADDED), F32),
            pltpu.SemaphoreType.DMA((2, 3)),
            pltpu.SemaphoreType.DMA((2, 4)),
            pltpu.SemaphoreType.DMA((3 * PARTS + 1,)),
            pltpu.SemaphoreType.DMA((3 * PARTS + 1,)),
        ],
        compiler_params=pltpu.CompilerParams(
            collective_id=collective_id, has_side_effects=True, vmem_limit_bytes=62 << 20
        ),
    )(*values, *weights)


def backward_kernel(
    gate_part,
    up_part,
    down_part,
    out_part,
    flat,
    grad_resid,
    grad_gain_two,
    cosine,
    sine,
    kv_w,
    q_w,
    normed_t,
    q_t,
    kv_all,
    o_t,
    lse,
    grad_mixed,
    gate_sum,
    up_sum,
    down_sum,
    out_sum,
    q_sum,
    kv_sum,
    d_tokens,
    do_t,
    do_n,
    q_n,
    dq_t,
    delta,
    dkv,
    landed,
    beside,
    grad_qkv,
    q_part,
    kv_part,
    send,
    recv,
    local,
    kv_send,
    kv_recv,
    *buffers,
):
    pc = Places()
    col = Column(pc)
    t, z, yl = col.t, pc.z, pc.yl
    greet([pc.sib, pc.ypair, pc.ylo, *pc.xdev, *pc.zdev, *pc.xdiag, *pc.zdiag])
    sems, kv_sems = Sems(send, recv), Sems(kv_send, kv_recv)
    parts = (gate_part, up_part, down_part, out_part, q_part, kv_part)
    finals = (gate_sum, up_sum, down_sum, out_sum, q_sum, kv_sum)
    reduces = [
        reduce_steps(
            pc, sems, local.at[k], parts[k], finals[k], buffers[6 * k : 6 * k + 6], split
        )
        for k, split in enumerate(REDUCE_SPLITS)
    ]
    reduces += [
        small_steps(pc, sems, local.at[4 + k], parts[4 + k], finals[4 + k], buffers[24 + 5 * k : 29 + 5 * k])
        for k in range(2)
    ]
    r_gate, r_up, r_down, r_out, r_q, r_kv = reduces
    early = (r_up, r_down, r_gate, r_out)
    advance(r_up, r_gate, r_down, r_out)

    do_t[...] = jnp.zeros_like(do_t)
    for tile in range(8):
        if tile < 7:
            turned = flip(grad_mixed[:, tile * PAIR : (tile + 1) * PAIR])
        else:
            turned = flip(grad_mixed[:, tile * PAIR : tile * PAIR + HEAD_WIDTH])
        for side in range(2):
            head = 2 * tile + side
            if head < QUERY_HEADS:
                h, g = head // GROUP, head % GROUP
                do_t[h, HEAD_WIDTH:PAIR, g * BLOCK : (g + 1) * BLOCK] = turned[
                    side * HEAD_WIDTH : (side + 1) * HEAD_WIDTH
                ]
    for h in range(KEY_VALUE_HEADS):
        do_n[h] = flip(do_t[h])
        q_n[h] = flip(q_t[h])
        both = do_t[h, HEAD_WIDTH:PAIR].astype(F32) * o_t[h, HEAD_WIDTH:PAIR]
        delta[h] = jnp.broadcast_to(jnp.sum(both, axis=0, keepdims=True), (8, STACK))
    dq_t[...] = jnp.zeros_like(dq_t)

    def visit(j, diagonal):
        def per_head(h, carry):
            kv = kv_all[j, h]
            scores = dot(kv, q_t[h])
            if diagonal:
                key = lax.broadcasted_iota(jnp.int32, (BLOCK, STACK), 0)
                query = lax.broadcasted_iota(jnp.int32, (BLOCK, STACK), 1) % BLOCK
                scores = jnp.where(key <= query, scores, -1e30)
            probs = jnp.exp(scores - lse[h][0:1])
            grad_probs = dot(kv, do_t[h])
            grad_scores = (probs * (grad_probs - delta[h][0:1])).astype(BF16)
            both = dot(grad_scores, q_n[h]) + dot(probs.astype(BF16), do_n[h])
            dkv[j, h] = both.astype(BF16)
            dq_t[h] += dot(flip(kv), grad_scores)
            return carry

        lax.fori_loop(0, KEY_VALUE_HEADS, per_head, 0)


    for step in (3, 2, 1, 0):

        @pl.when((yl == 1) if step == 0 else (z - step >= 0))
        def _(step=step):
            j = col.other(-step)
            visit(j, False)
            kv_sems.push(step, dkv.at[j], beside.at[step], col.beside)

        if step == 3:
            pass
        if step == 2:
            advance(r_up)
        if step == 1:
            pass
        if step == 0:
            advance(r_down)
    for step in (3, 2, 1):

        @pl.when(z - step >= 0)
        def _(step=step):
            j = col.own(-step)
            visit(j, False)
            kv_sems.arrived(step, beside.at[step], col.beside)
            for h in range(KEY_VALUE_HEADS):
                total = dkv[j, h].astype(F32) + beside[step, h].astype(F32)
                dkv[j, h] = total.astype(BF16)
            kv_sems.push(3 + step, dkv.at[j], landed.at[step - 1], col.device(-step))

        if step == 3:
            pass
        if step == 2:
            pass
        if step == 1:
            pass
    visit(t, True)
    advance(r_gate, r_out)

    cos, sin = cosine[...], sine[...]

    def turn(tile):
        return tile * cos - swap_halves(tile) * sin

    for tile in range(8):
        pieces = []
        for head in (2 * tile, min(2 * tile + 1, QUERY_HEADS - 1)):
            h, g = head // GROUP, head % GROUP
            pieces.append(dq_t[h, 0:HEAD_WIDTH, g * BLOCK : (g + 1) * BLOCK])
        joined = turn(jnp.concatenate(pieces, axis=0).T * FACTOR)
        grad_qkv[:, tile * PAIR : (tile + 1) * PAIR] = joined.astype(BF16)
    rows = normed_t[...]
    for tile in range(Q_TILES):
        product = dot(rows, grad_qkv[:, tile * PAIR : (tile + 1) * PAIR])
        q_part[:, :, :, :, tile * PAIR : (tile + 1) * PAIR] = product.astype(BF16).reshape(
            2, 4, 2, PAD, PAIR
        )
    advance(r_q)
    advance(r_up)
    from_queries = dot_nt(
        grad_qkv[:, : Q_TILES * PAIR], q_w[...].reshape(PADDED, Q_TILES * PAIR)
    )

    @pl.when(yl == 0)
    def _():
        kv_sems.arrived(0, beside.at[0], col.beside)
        for h in range(KEY_VALUE_HEADS):
            total = dkv[t, h].astype(F32) + beside[0, h].astype(F32)
            dkv[t, h] = total.astype(BF16)

    for step in (1, 2, 3):

        @pl.when(z + step < 4)
        def _(step=step):
            kv_sems.arrived(3 + step, landed.at[step - 1], col.device(step))

    advance(r_q)
    low = low_half((BLOCK, PAIR))
    totals = []
    for h in range(KEY_VALUE_HEADS):

        def add(k, total, h=h):
            return total + landed[k, h].astype(F32)

        totals.append(lax.fori_loop(0, 3 - z, add, dkv[t, h].astype(F32)))
    zero = jnp.zeros((BLOCK, PAIR), F32)
    left = grad_qkv[:, 7 * PAIR : 8 * PAIR].astype(F32)
    first = turn(pltpu.roll(totals[0], HEAD_WIDTH, 1))
    grad_qkv[:, 7 * PAIR : 8 * PAIR] = jnp.where(low, left, first).astype(BF16)
    for n, (a, b) in enumerate(((1, 2), (3, 4))):
        keys = turn(jnp.where(low, totals[a], pltpu.roll(totals[b], HEAD_WIDTH, 1)))
        grad_qkv[:, (8 + n) * PAIR : (9 + n) * PAIR] = keys.astype(BF16)
    for n, (a, b) in enumerate(((0, 1), (2, 3), (4, None))):
        high = zero if b is None else totals[b]
        vals = jnp.where(low, pltpu.roll(totals[a], HEAD_WIDTH, 1), high)
        grad_qkv[:, (10 + n) * PAIR : (11 + n) * PAIR] = vals.astype(BF16)

    x = flat[...]
    scale = norm_scale(x)
    grad_normed = from_queries + dot_nt(
        grad_qkv[:, Q_TILES * PAIR :], kv_w[...].reshape(PADDED, KV_TILES * PAIR)
    )
    token_term, grad_gain = norm_back(grad_normed, x, scale, gain_row(kv_w, 0))
    row = lax.broadcasted_iota(jnp.int32, (8, PADDED), 0)
    gains = jnp.where(row == 0, grad_gain[None, :], jnp.where(row == 1, grad_gain_two[...], 0.0))
    lane = lax.broadcasted_iota(jnp.int32, (8, PAIR), 1)
    which = lax.broadcasted_iota(jnp.int32, (8, PAIR), 0)
    put = (lane == which + HEAD_WIDTH) & (which < 2)
    for tile in range(KV_TILES):
        at = Q_TILES + tile
        product = dot(rows, grad_qkv[:, at * PAIR : (at + 1) * PAIR])
        if tile == KV_TILES - 1:
            product = product + dot_tn(gains.astype(BF16), put.astype(BF16))
        kv_part[:, :, :, :, tile * PAIR : (tile + 1) * PAIR] = product.astype(BF16).reshape(
            2, 4, 2, PAD, PAIR
        )
    advance(r_kv)
    advance(r_down)
    d_tokens[...] = (grad_resid[...] + token_term).astype(BF16)

    drain(r_kv, r_q, *early)

    for step in (0, 1, 2, 3):

        @pl.when((yl == 1) if step == 0 else (z - step >= 0))
        def _(step=step):
            copy_wait(kv_sems, step, beside.at[step], col.beside)

    for step in (1, 2, 3):

        @pl.when(z - step >= 0)
        def _(step=step):
            copy_wait(kv_sems, 3 + step, landed.at[step - 1], col.device(-step))

    sems.finish()


REDUCE_SPLITS = (True, False, False, False)


def backward(parts, values, collective_id):
    vmem, hbm = pl.BlockSpec(memory_space=pltpu.VMEM), pl.BlockSpec(memory_space=pl.ANY)
    q_shape = (2, 4, 2, PAD, Q_TILES * PAIR)
    kv_shape = (2, 4, 2, PAD, KV_TILES * PAIR)
    shapes = [p.shape for p in parts] + [q_shape, kv_shape]
    scratch = [
        pltpu.VMEM((KEY_VALUE_HEADS, PAIR, STACK), BF16),
        pltpu.VMEM((KEY_VALUE_HEADS, STACK, PAIR), BF16),
        pltpu.VMEM((KEY_VALUE_HEADS, STACK, PAIR), BF16),
        pltpu.VMEM((KEY_VALUE_HEADS, PAIR, STACK), F32),
        pltpu.VMEM((KEY_VALUE_HEADS, 8, STACK), F32),
        pltpu.VMEM((8, KEY_VALUE_HEADS, BLOCK, PAIR), BF16),
        pltpu.VMEM((3, KEY_VALUE_HEADS, BLOCK, PAIR), BF16),
        pltpu.VMEM((4, KEY_VALUE_HEADS, BLOCK, PAIR), BF16),
        pltpu.VMEM((BLOCK, (Q_TILES + KV_TILES) * PAIR), BF16),
        pltpu.VMEM(q_shape, BF16),
        pltpu.VMEM(kv_shape, BF16),
        pltpu.SemaphoreType.DMA((6 * REDUCE_SEMS,)),
        pltpu.SemaphoreType.DMA((6 * REDUCE_SEMS,)),
        pltpu.SemaphoreType.DMA((6,)),
        pltpu.SemaphoreType.DMA((7,)),
        pltpu.SemaphoreType.DMA((7,)),
    ]
    for s, split in zip(shapes, REDUCE_SPLITS):
        scratch += reduce_scratch(*s[-2:], split)
    scratch += small_scratch(*q_shape[-2:]) + small_scratch(*kv_shape[-2:])
    return pl.pallas_call(
        backward_kernel,
        out_shape=[jax.ShapeDtypeStruct(s[-2:], BF16) for s in shapes]
        + [jax.ShapeDtypeStruct((BLOCK, PADDED), BF16)],
        in_specs=[hbm] * 4 + [vmem] * len(values),
        out_specs=[vmem] * 7,
        scratch_shapes=scratch,
        compiler_params=pltpu.CompilerParams(
            collective_id=collective_id, has_side_effects=True, vmem_limit_bytes=63 << 20
        ),
    )(*parts, *values)


def rotary_tables(token_positions):
    half = HEAD_WIDTH // 2
    freqs = ROPE_BASE ** (-jnp.arange(half, dtype=F32) * 2.0 / HEAD_WIDTH)
    angles = token_positions.astype(F32)[:, None] * freqs[None, :]
    cosine, sine = jnp.cos(angles), jnp.sin(angles)
    return (
        jnp.concatenate([cosine] * 4, axis=1),
        jnp.concatenate([-sine, sine] * 2, axis=1),
    )


def on_device(
    tokens,
    attn_gain,
    w_query,
    key_weight,
    value_weight,
    w_out,
    ffn_gain,
    w_gate,
    w_up,
    w_down,
    d_out,
):
    block = tokens.shape[1]
    token_positions = lax.axis_index("ctx") * block + jnp.arange(block, dtype=jnp.int32)
    cosine, sine = rotary_tables(token_positions)
    feature = jnp.arange(WIDTH, dtype=jnp.int32)
    place_of = feature // ROWS * PAD + feature % ROWS
    select = (place_of[:, None] == jnp.arange(PADDED, dtype=jnp.int32)[None, :]).astype(BF16)

    qkv_shard = jnp.pad(
        jnp.concatenate(
            [w_query, key_weight, value_weight, attn_gain[:, None], ffn_gain[:, None]], axis=1
        ),
        ((0, PAD - ROWS), (0, (Q_TILES + KV_TILES) * PAIR - WIDTH - 2 * KV_WIDTH - 2)),
    )
    q_shard, kv_shard = qkv_shard[:, : Q_TILES * PAIR], qkv_shard[:, Q_TILES * PAIR :]
    kv_w, q_w, out_w, gate_w, up_w, down_w, *kept = forward(
        (tokens[0], cosine, sine, select),
        (kv_shard, q_shard),
        (w_out, w_gate, w_up, w_down),
        0,
    )
    normed_t, q_t, kv_all, o_t, lse, mixed, gain_two, flat = kept
    out_w, gate_w, up_w = (w.reshape(PADDED, -1) for w in (out_w, gate_w, up_w))
    down_w = down_w.reshape(-1, PADDED)
    output, grad_resid, grad_gain_two, grad_mixed, *parts = middle(
        (flat, d_out[0], mixed, gain_two, select, out_w), (gate_w, up_w, down_w), 2
    )
    sum_gate, sum_up, sum_down, sum_out, sum_q, sum_kv, d_tokens = backward(
        parts,
        (
            flat,
            grad_resid,
            grad_gain_two,
            cosine,
            sine,
            kv_w,
            q_w,
            normed_t,
            q_t,
            kv_all,
            o_t,
            lse,
            grad_mixed,
        ),
        1,
    )
    d_tokens = dot_nt(d_tokens, select).astype(BF16)
    sum_qkv = jnp.concatenate([sum_q, sum_kv], axis=1)[:ROWS].astype(F32)
    ends = (WIDTH, WIDTH + KV_WIDTH, WIDTH + 2 * KV_WIDTH)
    return (
        output[None],
        d_tokens[None],
        sum_qkv[:, ends[2]],
        sum_qkv[:, : ends[0]],
        sum_qkv[:, ends[0] : ends[1]],
        sum_qkv[:, ends[1] : ends[2]],
        dot_nt(sum_out[:ROWS], select),
        sum_qkv[:, ends[2] + 1],
        sum_gate[:ROWS].astype(F32),
        sum_up[:ROWS].astype(F32),
        dot_nt(sum_down, select),
    )


def solution(mesh):
    rows, whole, line = P("fsdp", None), P("fsdp", "ctx", None), P("fsdp")
    weights = (line, rows, rows, rows, rows, line, rows, rows, rows)
    return jax.shard_map(
        on_device,
        mesh=mesh,
        in_specs=(whole, *weights, whole),
        out_specs=(whole, whole, *weights),
        check_vma=False,
    )
```

```python
import functools
import math

import jax
import jax.numpy as jnp
from jax import lax
from jax.experimental import pallas as pl
from jax.experimental.pallas import tpu as pltpu
from jax.sharding import PartitionSpec as P

QUERY_HEADS = 15
KEY_VALUE_HEADS = 5
HEAD_WIDTH = 64
GROUP = QUERY_HEADS // KEY_VALUE_HEADS
WIDTH = 960
ROWS = 60
PAD = 64
SHARDS = 16
PADDED = SHARDS * PAD
KV_WIDTH = KEY_VALUE_HEADS * HEAD_WIDTH
Q_TILES = 7
KV_TILES = 6

EPS = 1e-05
ROPE_BASE = 10000.0
MESH = pl.DeviceIdType.MESH
BF16 = jnp.bfloat16
F32 = jnp.float32


def place():
    f, t = lax.axis_index("fsdp"), lax.axis_index("ctx")
    return f // 8, (f // 2) % 4, f % 2, t // 2, t % 2


def device(yh, x, c, z, yl):
    return ((yh * 4 + x) * 2 + c, z * 2 + yl)


class Places:
    def __init__(self):
        yh, x, c, z, yl = place()
        self.yh, self.x, self.c, self.z, self.yl = yh, x, c, z, yl
        self.sib = device(yh, x, 1 - c, z, yl)
        self.ypair = device(1 - yh, x, c, z, 1 - yl)
        self.ylo = device(yh, x, c, z, 1 - yl)
        self.xs = [(x + 1) % 4, (x + 3) % 4, (x + 2) % 4]
        self.zs = [(z + 1) % 4, (z + 3) % 4, (z + 2) % 4]
        self.yopp = device(1 - yh, x, c, z, yl)
        self.xdiag = [device(1 - yh, k, c, z, 1 - yl) for k in self.xs]
        self.zdiag = [device(yh, x, c, k, 1 - yl) for k in self.zs]
        self.xdev = [device(yh, k, c, z, yl) for k in self.xs]
        self.zdev = [device(yh, x, c, k, yl) for k in self.zs]
        self.xfrom = [self.xs[1], self.xs[0], self.xs[2]]
        self.zfrom = [self.zs[1], self.zs[0], self.zs[2]]


def greet(devices):
    barrier = pltpu.get_barrier_semaphore()
    for d in devices:
        pl.semaphore_signal(barrier, inc=1, device_id=d, device_id_type=MESH)
    pl.semaphore_wait(barrier, len(devices))


class Sems:
    def __init__(self, send, recv):
        self.send, self.recv, self.at, self.open = send, recv, 0, []

    def take(self, count=1):
        at = self.at
        self.at += count
        return at

    def push(self, slot, src, dst, dev):
        copy = pltpu.make_async_remote_copy(
            src_ref=src,
            dst_ref=dst,
            send_sem=self.send.at[slot],
            recv_sem=self.recv.at[slot],
            device_id=dev,
            device_id_type=MESH,
        )
        copy.start()
        self.open.append(copy)

    def arrived(self, slot, dst, dev):
        pltpu.make_async_remote_copy(
            src_ref=dst,
            dst_ref=dst,
            send_sem=self.send.at[slot],
            recv_sem=self.recv.at[slot],
            device_id=dev,
            device_id_type=MESH,
        ).wait_recv()

    def finish(self):
        for copy in self.open:
            copy.wait_send()
        self.open = []


GATHER_SEMS = 24


def gather_steps(pc, sems, local_sem, shard, out, split):
    rows = shard.shape[0]
    quarter = rows // 4
    yh, x, c, z = pc.yh, pc.x, pc.c, pc.z
    s_y = sems.take()
    s_x = [[sems.take() for _ in range(2)] for _ in range(3)]
    s_z = [[sems.take() for _ in range(3)] for _ in range(3)] if split else None
    s_s = [sems.take() for _ in range(4)]
    band = pl.ds(pl.multiple_of(z * quarter, 16), quarter) if split else pl.ds(0, rows)
    straight = (0, 1, 2) if split else (0, 1)

    own = pltpu.make_async_copy(shard, out.at[yh, x, c], local_sem)
    own.start()
    sems.push(s_y, shard, out.at[yh, x, c], pc.ypair)
    yield
    for k in straight:
        sems.push(s_x[k][0], shard.at[band], out.at[yh, x, c, band], pc.xdev[k])
    yield
    sems.arrived(s_y, out.at[1 - yh, x, c], pc.ypair)
    for k in straight:
        piece = out.at[1 - yh, x, c, band]
        sems.push(s_x[k][1], piece, piece, pc.xdev[k])
    own.wait()
    sems.push(s_s[3], out.at[:, x, c], out.at[:, x, c], pc.sib)
    yield
    for k in straight:
        far = pc.xfrom[k]
        sems.arrived(s_x[k][0], out.at[yh, far, c, band], pc.xdev[k])
        sems.arrived(s_x[k][1], out.at[1 - yh, far, c, band], pc.xdev[k])
        if split:
            piece = out.at[:, far, c, band]
            for j in range(3):
                sems.push(s_z[k][j], piece, piece, pc.zdev[j])
        else:
            piece = out.at[k, far, c]
            sems.push(s_x[2][k], piece, piece, pc.xdev[k])
            sems.push(s_s[k], out.at[:, far, c], out.at[:, far, c], pc.sib)
    yield
    if split:
        for k in (0, 1, 2):
            far = pc.xfrom[k]
            for j in range(3):
                there = pl.ds(pl.multiple_of(pc.zfrom[j] * quarter, 16), quarter)
                sems.arrived(s_z[k][j], out.at[:, far, c, there], pc.zdev[j])
            sems.push(s_s[k], out.at[:, far, c], out.at[:, far, c], pc.sib)
    else:
        far = pc.xs[2]
        for k in (0, 1):
            sems.arrived(s_x[2][k], out.at[k, far, c], pc.xdev[k])
        sems.push(s_s[2], out.at[:, far, c], out.at[:, far, c], pc.sib)
    yield
    for k in (0, 1, 2, 3):
        far = x if k == 3 else pc.xfrom[k]
        sems.arrived(s_s[k], out.at[:, far, 1 - c], pc.sib)
    yield


def run_all(steps):
    live = list(steps)
    while live:
        for s in list(live):
            try:
                next(s)
            except StopIteration:
                live.remove(s)


REDUCE_SEMS = 32


def add_rows(dst, terms, shape):
    lead, rows = shape[:-2], shape[-2]
    blocks = rows // 16
    count = math.prod(lead) * blocks

    def body(i, carry):
        idx, rest = [], i // blocks
        for size in reversed(lead):
            idx.append(rest % size)
            rest = rest // size
        idx = tuple(reversed(idx))
        at = (*idx, pl.ds(pl.multiple_of((i % blocks) * 16, 16), 16))
        total = dst[at].astype(F32)
        for term in terms:
            total = total + term[at].astype(F32)
        dst[at] = total.astype(BF16)
        return carry

    lax.fori_loop(0, count, body, 0)


def reduce_scratch(rows, width, split):
    q = rows // 4
    return [
        pltpu.VMEM((2, 4, rows, width), BF16),
        pltpu.VMEM((3 if split else 2, 2, q if split else rows, width), BF16),
        pltpu.VMEM((3, rows // 2, width), BF16),
        pltpu.VMEM((3, rows // 2, width // 4), BF16),
        pltpu.VMEM((3, 3, 2, q, width) if split else (2, rows, width), BF16),
    ]


def reduce_steps(pc, sems, local_sem, part, final, buffers, split):
    yh, x, c, z, yl = pc.yh, pc.x, pc.c, pc.z, pc.yl
    acc, from_x, from_y, from_z, from_r = buffers
    rows, width = part.shape[-2:]
    q = rows // 4
    s_m = sems.take()
    s_y = [sems.take() for _ in range(3)]
    s_x = [sems.take() for _ in range(3)]
    s_z = [sems.take() for _ in range(3)]
    s_f = [sems.take() for _ in range(3)]
    s_r = [[sems.take() for _ in range(3)] for _ in range(3)]

    def band(k):
        return pl.ds(pl.multiple_of(k * q, 16), q)

    own = pltpu.make_async_copy(part, acc, local_sem)
    own.start()
    own.wait()
    if split:
        here = band(z)
        order = (2, 0, 1)
        for k in order:
            for j in range(3):
                piece = acc.at[:, pc.xs[k], band(pc.zs[j])]
                sems.push(s_r[k][j], piece, from_r.at[j, k], pc.zdev[j])
        yield
        for k in order:
            for j in range(3):
                sems.arrived(s_r[k][j], from_r.at[j, k], pc.zdev[j])
            mine = acc.at[:, pc.xs[k], here]
            add_rows(mine, [from_r.at[j, k] for j in range(3)], (2, q, width))
            sems.push(s_x[k], mine, from_x.at[k], pc.xdev[k])
        yield
        for k in range(3):
            sems.arrived(s_x[k], from_x.at[k], pc.xdev[k])
        add_rows(acc.at[:, x, here], [from_x.at[k] for k in range(3)], (2, q, width))
    else:
        for k in range(2):
            sems.push(s_r[0][k], acc.at[k, pc.xs[2]], from_r.at[k], pc.xdev[k])
        yield
        for k in range(2):
            sems.arrived(s_r[0][k], from_r.at[k], pc.xdev[k])
            add_rows(acc.at[k, pc.xs[k]], [from_r.at[k]], (rows, width))
            sems.push(s_x[k], acc.at[:, pc.xs[k]], from_x.at[k], pc.xdev[k])
        yield
        for k in range(2):
            sems.arrived(s_x[k], from_x.at[k], pc.xdev[k])
        add_rows(acc.at[:, x], [from_x.at[k] for k in range(2)], (2, rows, width))
    h, w = rows // 2, width // 4

    def side(k):
        return pl.ds(pl.multiple_of(k * h, 16), h)

    def column(k):
        return pl.ds(pl.multiple_of(k * w, 128), w)

    half, other = side(yl), side(1 - yl)
    for n, (there, k) in enumerate(((yh, 1 - yl), (1 - yh, yl), (1 - yh, 1 - yl))):
        dev = device(there, x, c, z, k)
        sems.push(s_y[n], acc.at[there, x, side(k)], from_y.at[n], dev)
    yield
    for n in range(3):
        sems.arrived(s_y[n], from_y.at[n], pc.sib)
    add_rows(acc.at[yh, x, half], [from_y.at[n] for n in range(3)], (h, width))
    for j in range(3):
        piece = acc.at[yh, x, half, column(pc.zs[j])]
        sems.push(s_z[j], piece, from_z.at[j], pc.zdev[j])
    yield
    for j in range(3):
        sems.arrived(s_z[j], from_z.at[j], pc.zdev[j])
    mine = acc.at[yh, x, half, column(z)]
    add_rows(mine, [from_z.at[j] for j in range(3)], (h, w))
    done = final.at[half, column(z)]
    done[...] = mine[...]
    for j in range(3):
        sems.push(s_f[j], done, done, pc.zdev[j])
    yield
    for j in range(3):
        sems.arrived(s_f[j], final.at[half, column(pc.zfrom[j])], pc.zdev[j])
    sems.push(s_m, final.at[half], final.at[half], pc.ylo)
    yield
    sems.arrived(s_m, final.at[other], pc.ylo)
    yield


def small_scratch(rows, width):
    q = rows // 4
    return [
        pltpu.VMEM((2, 4, rows, width), BF16),
        pltpu.VMEM((2, 4, rows, width), BF16),
        pltpu.VMEM((3, 2, 4, q, width), BF16),
        pltpu.VMEM((7, q, width), BF16),
        pltpu.VMEM((2, rows, width), BF16),
    ]


def small_steps(pc, sems, local_sem, part, final, buffers):
    yh, x, c, z, yl = pc.yh, pc.x, pc.c, pc.z, pc.yl
    acc, from_sib, from_z, from_xy, landed = buffers
    rows, width = part.shape[-2:]
    q = rows // 4
    s_s = sems.take()
    s_z = [sems.take() for _ in range(3)]
    s_xy = [sems.take() for _ in range(7)]
    s_f = [sems.take() for _ in range(7)]

    def band(k):
        return pl.ds(pl.multiple_of(k * q, 16), q)

    here = band(z)
    own = pltpu.make_async_copy(part.at[:, :, c], acc, local_sem)
    own.start()
    sems.push(s_s, part.at[:, :, 1 - c], from_sib, pc.sib)
    yield
    own.wait()
    sems.arrived(s_s, from_sib, pc.sib)
    add_rows(acc, [from_sib], acc.shape)
    for j in range(3):
        sems.push(s_z[j], acc.at[:, :, band(pc.zs[j])], from_z.at[j], pc.zdev[j])
    yield
    for j in range(3):
        sems.arrived(s_z[j], from_z.at[j], pc.zdev[j])
    add_rows(acc.at[:, :, here], [from_z.at[j] for j in range(3)], (2, 4, q, width))
    targets = [(yh, pc.xs[k], yl) for k in range(3)]
    targets += [(1 - yh, k, 1 - yl) for k in (*pc.xs, x)]
    for n, (there, k, side) in enumerate(targets):
        sems.push(s_xy[n], acc.at[there, k, here], from_xy.at[n], device(there, k, c, z, side))
    yield
    for n in range(7):
        sems.arrived(s_xy[n], from_xy.at[n], pc.sib)
    mine = acc.at[yh, x, here]
    add_rows(mine, [from_xy.at[n] for n in range(7)], (q, width))
    landed[yl, here] = mine[...]
    for n, (k, side) in enumerate([(k, yl) for k in pc.zs] + [(k, 1 - yl) for k in (*pc.zs, z)]):
        sems.push(s_f[n], mine, landed.at[yl, here], device(yh, x, c, k, side))
    yield
    for n, (k, side) in enumerate(
        [(k, yl) for k in pc.zfrom] + [(k, 1 - yl) for k in (*pc.zfrom, z)]
    ):
        sems.arrived(s_f[n], landed.at[side, band(k)], pc.sib)

    def body(i, carry):
        at = pl.ds(pl.multiple_of(i * 16, 16), 16)
        total = landed[0, at].astype(F32) + landed[1, at].astype(F32)
        final[at] = total.astype(BF16)
        return carry

    lax.fori_loop(0, rows // 16, body, 0)
    yield


class Column:
    def __init__(self, pc):
        self.z, self.yl = pc.z, pc.yl
        self.t = 2 * pc.z + pc.yl
        self.beside = pc.ylo
        self.pc = pc

    def own(self, step):
        return 2 * (self.z + step) + self.yl

    def other(self, step):
        return 2 * (self.z + step) + 1 - self.yl

    def device(self, step):
        pc = self.pc
        return device(pc.yh, pc.x, pc.c, (pc.z + step + 4) % 4, pc.yl)


def dot(a, b):
    return jnp.dot(a, b, preferred_element_type=F32)


def dot_tn(a, b):
    return lax.dot_general(a, b, (((0,), (0,)), ((), ())), preferred_element_type=F32)


def dot_nt(a, b):
    return lax.dot_general(a, b, (((1,), (1,)), ((), ())), preferred_element_type=F32)


def norm_scale(rows):
    return lax.rsqrt(jnp.sum(rows * rows, axis=-1, keepdims=True) * (1.0 / WIDTH) + EPS)


def norm_back(grad_normed, rows, scale, gain):
    unit = rows * scale
    grad_gain = jnp.sum(grad_normed * unit, axis=0)
    grad_unit = grad_normed * gain
    mean = jnp.sum(grad_unit * unit, axis=-1, keepdims=True) * (1.0 / WIDTH)
    return scale * (grad_unit - unit * mean), grad_gain


BLOCK = 256
PAIR = 2 * HEAD_WIDTH
STACK = GROUP * BLOCK
FACTOR = HEAD_WIDTH ** (-0.5)


def low_half(shape):
    return lax.broadcasted_iota(jnp.int32, shape, 1) % PAIR < HEAD_WIDTH


def swap_halves(tile):
    lane = lax.broadcasted_iota(jnp.int32, tile.shape, 1) % HEAD_WIDTH
    half = HEAD_WIDTH // 2
    return jnp.where(
        lane < half, pltpu.roll(tile, PAIR - half, 1), pltpu.roll(tile, half, 1)
    )


def flip(a):
    return a.astype(F32).T.astype(a.dtype)


def advance(*steps):
    for s in steps:
        next(s, None)


def drain(*steps):
    run_all(steps)


def tile_of(ref, tile):
    return ref[:, :, :, :, tile * PAIR : (tile + 1) * PAIR].reshape(PADDED, PAIR)


def gain_row(kv_w, which):
    pick = lax.broadcasted_iota(jnp.int32, (8, PAIR), 1) == HEAD_WIDTH + which
    return dot_nt(pick.astype(BF16), tile_of(kv_w, KV_TILES - 1))[0:1]


def copy_wait(sems, slot, ref, dev):
    pltpu.make_async_remote_copy(
        src_ref=ref,
        dst_ref=ref,
        send_sem=sems.send.at[slot],
        recv_sem=sems.recv.at[slot],
        device_id=dev,
        device_id_type=MESH,
    ).wait_send()


def forward_kernel(
    tokens_t,
    cosine,
    sine,
    select,
    kv_shard,
    q_shard,
    own_out,
    own_gate,
    own_up,
    own_down,
    kv_w,
    q_w,
    out_w,
    gate_w,
    up_a_w,
    up_b_w,
    down_w,
    normed_t,
    q_t,
    kv_all,
    o_t,
    lse,
    mixed,
    gain_two,
    flat,
    peak,
    wide,
    out_shard,
    gate_shard,
    up_a_shard,
    up_b_shard,
    down_shard,
    send,
    recv,
    local,
    kv_send,
    kv_recv,
):
    pc = Places()
    col = Column(pc)
    t, z, yl = col.t, pc.z, pc.yl
    greet([pc.sib, pc.ypair, pc.ylo, *pc.xdev, *pc.zdev])
    sems, kv_sems = Sems(send, recv), Sems(kv_send, kv_recv)
    g_kv = gather_steps(pc, sems, local.at[0], kv_shard, kv_w, True)
    g_q = gather_steps(pc, sems, local.at[1], q_shard, q_w, False)
    g_out = gather_steps(pc, sems, local.at[2], out_shard, out_w, False)
    g_gate = gather_steps(pc, sems, local.at[3], gate_shard, gate_w, True)
    g_up = gather_steps(pc, sems, local.at[4], up_a_shard, up_a_w, True)
    g_half = gather_steps(pc, sems, local.at[5], up_b_shard, up_b_w, False)
    g_down = gather_steps(pc, sems, local.at[6], down_shard, down_w, False)
    advance(g_kv, g_kv, g_q)
    ones = (
        lax.broadcasted_iota(jnp.int32, (PAD, ROWS), 0)
        == lax.broadcasted_iota(jnp.int32, (PAD, ROWS), 1)
    ).astype(BF16)
    gate_shard[...] = dot(ones, own_gate[...]).astype(BF16)
    advance(g_gate, g_gate)
    half = up_a_shard.shape[1]
    up_a_shard[...] = dot(ones, own_up[:, :half]).astype(BF16)
    up_b_shard[...] = dot(ones, own_up[:, half:]).astype(BF16)
    advance(g_up)
    down_shard[...] = dot(own_down[...], select[...]).astype(BF16)
    out_shard[...] = dot(ones, dot(own_out[...], select[...]).astype(BF16)).astype(BF16)
    x = dot_tn(tokens_t[...], select[...])
    flat[...] = x
    scale = norm_scale(x)
    advance(g_kv, g_q)
    advance(g_kv, g_q, g_gate, g_up)
    advance(g_kv, g_out, g_half, g_down)
    advance(g_kv)

    rows = (x * scale * gain_row(kv_w, 0)).astype(BF16)
    gain_two[...] = gain_row(kv_w, 1)
    cos, sin = cosine[...], sine[...]
    low = low_half((BLOCK, PAIR))

    def place_queries(product, tile):
        turned = (product * FACTOR).T.astype(BF16)
        for side in range(2):
            head = 2 * tile + side
            if head < QUERY_HEADS:
                h, g = head // GROUP, head % GROUP
                at = slice(g * BLOCK, (g + 1) * BLOCK)
                q_t[h, 0:HEAD_WIDTH, at] = turned[side * HEAD_WIDTH : (side + 1) * HEAD_WIDTH]
                q_t[h, HEAD_WIDTH:PAIR, at] = jnp.zeros((HEAD_WIDTH, BLOCK), BF16)

    for tile in range(KV_TILES):
        product = dot(rows, tile_of(kv_w, tile))
        if tile < 3:
            product = product * cos + swap_halves(product) * sin
        wide[tile] = product
    for h in range(KEY_VALUE_HEADS):
        k_tile, k_high = (h + 1) // 2, (h + 1) % 2
        v_tile, v_high = 3 + h // 2, h % 2
        k_part, v_part = wide[k_tile], wide[v_tile]
        if k_high:
            k_part = pltpu.roll(k_part, HEAD_WIDTH, 1)
        if not v_high:
            v_part = pltpu.roll(v_part, HEAD_WIDTH, 1)
        kv_all[t, h] = jnp.where(low, k_part, v_part).astype(BF16)
    for step in (1, 2, 3):

        @pl.when(z + step < 4)
        def _(step=step):
            kv_sems.push(step - 1, kv_all.at[t], kv_all.at[t], col.device(step))

    @pl.when(yl == 0)
    def _():
        kv_sems.push(3, kv_all.at[t], kv_all.at[t], col.beside)

    advance(g_gate, g_up, g_q)
    advance(g_out, g_half, g_down)
    place_queries(wide[0], 7)
    normed_t[...] = flip(rows)
    advance(g_q, g_up, g_q)
    for tile in range(Q_TILES):
        product = dot(rows, tile_of(q_w, tile))
        place_queries(product * cos + swap_halves(product) * sin, tile)
    peak[...] = jnp.full_like(peak, -1e30)
    o_t[...] = jnp.zeros_like(o_t)

    def visit(j, diagonal):
        def per_head(h, carry):
            kv = kv_all[j, h]
            kv_t = flip(kv)
            ones = lax.broadcasted_iota(jnp.int32, (PAIR, BLOCK), 0) < HEAD_WIDTH
            ones_v = jnp.where(ones, 1.0, kv_t.astype(F32)).astype(BF16)
            scores = dot(kv, q_t[h])
            if diagonal:
                key = lax.broadcasted_iota(jnp.int32, (BLOCK, STACK), 0)
                query = lax.broadcasted_iota(jnp.int32, (BLOCK, STACK), 1) % BLOCK
                scores = jnp.where(key <= query, scores, -1e30)
            old = peak[h]
            new = jnp.maximum(old, jnp.max(scores, axis=0, keepdims=True))
            probs = jnp.exp(scores - new[0:1]).astype(BF16)
            o_t[h] = o_t[h] * jnp.exp(old - new)[0:1] + dot(ones_v, probs)
            peak[h] = new
            return carry

        lax.fori_loop(0, KEY_VALUE_HEADS, per_head, 0)

    advance(g_out, g_half, g_down)
    visit(t, True)
    for step in (1, 2, 3):

        @pl.when(z - step >= 0)
        def _(step=step):
            block = kv_all.at[col.own(-step)]
            kv_sems.arrived(step - 1, block, col.device(-step))
            kv_sems.push(3 + step, block, block, col.beside)
            visit(col.own(-step), False)

        if step == 1:
            advance(g_out, g_half, g_down)
        if step == 2:
            advance(g_gate)
        if step == 3:
            advance(g_out, g_half, g_down)
    for step in (0, 1, 2, 3):

        @pl.when((yl == 1) if step == 0 else (z - step >= 0))
        def _(step=step):
            block = kv_all.at[col.other(-step)]
            kv_sems.arrived(3 + step, block, col.beside)
            visit(col.other(-step), False)

        if step == 1:
            advance(g_up)

    for h in range(KEY_VALUE_HEADS):
        total = o_t[h, 0:1]
        o_t[h] = o_t[h] * (1.0 / total)
        lse[h] = peak[h] + jnp.log(total)
    for tile in range(8):
        parts = []
        for head in (2 * tile, min(2 * tile + 1, QUERY_HEADS - 1)):
            h, g = head // GROUP, head % GROUP
            parts.append(o_t[h, HEAD_WIDTH:PAIR, g * BLOCK : (g + 1) * BLOCK])
        joined = jnp.concatenate(parts, axis=0).T.astype(BF16)
        if tile < 7:
            mixed[:, tile * PAIR : (tile + 1) * PAIR] = joined
        else:
            mixed[:, tile * PAIR : tile * PAIR + HEAD_WIDTH] = joined[:, :HEAD_WIDTH]
    drain(g_gate, g_up, g_half, g_down, g_out)
    for step in (1, 2, 3):

        @pl.when(z + step < 4)
        def _(step=step):
            copy_wait(kv_sems, step - 1, kv_all.at[t], col.device(step))

        @pl.when(z - step >= 0)
        def _(step=step):
            copy_wait(kv_sems, 3 + step, kv_all.at[t], col.beside)

    @pl.when(yl == 0)
    def _():
        copy_wait(kv_sems, 3, kv_all.at[t], col.beside)

    sems.finish()


def forward(values, shards, weights, collective_id):
    vmem, hbm = pl.BlockSpec(memory_space=pltpu.VMEM), pl.BlockSpec(memory_space=pl.ANY)
    hidden = weights[1].shape[1]
    rows = [PAD] * 6 + [weights[3].shape[0]]
    widths = [s.shape[1] for s in shards] + [PADDED, hidden, hidden // 2, hidden // 2, PADDED]
    padded = list(zip(rows, widths))
    gathered = [jax.ShapeDtypeStruct((2, 4, 2, *p), BF16) for p in padded]
    return pl.pallas_call(
        forward_kernel,
        out_shape=[
            *gathered,
            jax.ShapeDtypeStruct((PADDED, BLOCK), BF16),
            jax.ShapeDtypeStruct((KEY_VALUE_HEADS, PAIR, STACK), BF16),
            jax.ShapeDtypeStruct((8, KEY_VALUE_HEADS, BLOCK, PAIR), BF16),
            jax.ShapeDtypeStruct((KEY_VALUE_HEADS, PAIR, STACK), F32),
            jax.ShapeDtypeStruct((KEY_VALUE_HEADS, 8, STACK), F32),
            jax.ShapeDtypeStruct((BLOCK, WIDTH), BF16),
            jax.ShapeDtypeStruct((1, PADDED), F32),
            jax.ShapeDtypeStruct((BLOCK, PADDED), F32),
        ],
        in_specs=[vmem] * 4 + [hbm] * 2 + [vmem] * 4,
        out_specs=[vmem] * 2 + [hbm] * 5 + [vmem] * 8,
        scratch_shapes=[
            pltpu.VMEM((KEY_VALUE_HEADS, 8, STACK), F32),
            pltpu.VMEM((KV_TILES, BLOCK, PAIR), F32),
            *[pltpu.VMEM(p, BF16) for p in padded[2:]],
            pltpu.SemaphoreType.DMA((7 * GATHER_SEMS,)),
            pltpu.SemaphoreType.DMA((7 * GATHER_SEMS,)),
            pltpu.SemaphoreType.DMA((7,)),
            pltpu.SemaphoreType.DMA((7,)),
            pltpu.SemaphoreType.DMA((7,)),
        ],
        compiler_params=pltpu.CompilerParams(
            collective_id=collective_id, has_side_effects=True, vmem_limit_bytes=60 << 20
        ),
    )(*values, *shards, *weights)


PARTS = 4
STEP = 640


def middle_kernel(
    flat,
    d_out_t,
    mixed,
    gain_two,
    select,
    out_w,
    gate_w,
    up_a_w,
    up_b_w,
    down_w,
    output_t,
    grad_resid,
    grad_gain_two,
    grad_mixed,
    gate_acc,
    up_acc,
    down_acc,
    out_acc,
    gate_buf,
    up_buf,
    down_buf,
    gate_stage,
    up_stage,
    down_stage,
    out_stage,
    gate_sib,
    up_sib,
    down_sib,
    out_sib,
    total,
    back,
    load,
    local,
    send,
    recv,
):
    pc = Places()
    c = pc.c

    def loads(i):
        at = pl.ds(i * STEP, STEP)
        slot = i % 2
        up_w, side = (up_a_w, up_b_w)[i // 2], pl.ds(slot * STEP, STEP)
        return (
            pltpu.make_async_copy(gate_w.at[:, at], gate_buf.at[slot], load.at[slot, 0]),
            pltpu.make_async_copy(up_w.at[:, side], up_buf.at[slot], load.at[slot, 1]),
            pltpu.make_async_copy(down_w.at[at], down_buf.at[slot], load.at[slot, 2]),
        )

    def remote(src, dst, k):
        return pltpu.make_async_remote_copy(
            src_ref=src,
            dst_ref=dst,
            send_sem=send.at[k],
            recv_sem=recv.at[k],
            device_id=pc.sib,
            device_id_type=MESH,
        )

    def sends(i):
        at, slot = pl.ds(i * STEP, STEP), i % 2
        yh, xs = i // 2, pl.ds(2 * (i % 2), 2)
        gate, up, down = gate_stage.at[slot], up_stage.at[slot], down_stage.at[slot]
        return (
            remote(gate.at[:, :, 1 - c], gate_sib.at[:, :, :, at], 3 * i),
            remote(up.at[:, :, 1 - c], up_sib.at[:, :, :, at], 3 * i + 1),
            remote(down.at[:, 1 - c], down_sib.at[yh, xs], 3 * i + 2),
            pltpu.make_async_copy(gate.at[:, :, c], gate_acc.at[:, :, :, at], local.at[slot, 0]),
            pltpu.make_async_copy(up.at[:, :, c], up_acc.at[:, :, :, at], local.at[slot, 1]),
            pltpu.make_async_copy(down.at[:, c], down_acc.at[yh, xs], local.at[slot, 2]),
        )

    def sent(i):
        copies = sends(i)
        for copy in copies[:3]:
            copy.wait_send()
        for copy in copies[3:]:
            copy.wait()

    for copy in loads(0):
        copy.start()
    greet([pc.sib])
    mixed_p = dot(mixed[...], select[...]).astype(BF16)
    resid = flat[...] + dot(mixed_p, out_w[...])
    scale = norm_scale(resid)
    gain = gain_two[...]
    normed = (resid * scale * gain).astype(BF16)
    normed_t = flip(normed)
    grad = dot_tn(d_out_t[...], select[...]).astype(BF16)
    total[...] = resid
    back[...] = jnp.zeros_like(back)
    for i in range(PARTS):
        slot = i % 2
        if i + 1 < PARTS:
            for copy in loads(i + 1):
                copy.start()
        for copy in loads(i):
            copy.wait()
        if i >= 2:
            sent(i - 2)
        w_gate, w_up, w_down = gate_buf[slot], up_buf[slot], down_buf[slot]
        gate = dot(normed, w_gate)
        up = dot(normed, w_up)
        grad_hidden = dot_nt(grad, w_down)
        sigmoid = 0.5 * jnp.tanh(0.5 * gate) + 0.5
        swish = gate * sigmoid
        hidden = (swish * up).astype(BF16)
        grad_up_v = (grad_hidden * swish).astype(BF16)
        grad_gate_v = (grad_hidden * up * sigmoid * (1.0 + gate * (1.0 - sigmoid))).astype(BF16)
        total[...] += dot(hidden, w_down)
        back[...] += dot_nt(grad_gate_v, w_gate) + dot_nt(grad_up_v, w_up)
        shape = (2, 4, 2, PAD, STEP)
        gate_stage[slot] = dot(normed_t, grad_gate_v).astype(BF16).reshape(shape)
        up_stage[slot] = dot(normed_t, grad_up_v).astype(BF16).reshape(shape)
        down = dot(flip(hidden), grad).astype(BF16)
        down_stage[slot] = down.reshape(2, 2, STEP // 4, PADDED)
        for copy in sends(i):
            copy.start()
    output_t[...] = dot_nt(select[...], total[...].astype(BF16)).astype(BF16)
    term, grad_gain = norm_back(back[...], resid, scale, gain)
    grad_gain_two[...] = grad_gain[None, :]
    full = grad.astype(F32) + term
    grad_resid[...] = full
    branch = full.astype(BF16)
    out_stage[...] = dot(flip(mixed_p), branch).astype(BF16).reshape(2, 4, 2, PAD, PADDED)
    out_send = remote(out_stage.at[:, :, 1 - c], out_sib, 3 * PARTS)
    out_send.start()
    out_copy = pltpu.make_async_copy(out_stage.at[:, :, c], out_acc, local.at[0, 3])
    out_copy.start()
    inner = dot_nt(branch, out_w[...]).astype(BF16)
    grad_mixed[...] = dot_nt(inner, select[...]).astype(BF16)
    for i in (PARTS - 2, PARTS - 1):
        sent(i)
    for i in range(PARTS):
        for copy in sends(i)[:3]:
            copy.wait_recv()
    add_rows(gate_acc, [gate_sib], gate_acc.shape)
    add_rows(up_acc, [up_sib], up_acc.shape)
    add_rows(down_acc, [down_sib], down_acc.shape)
    out_send.wait()
    out_copy.wait()
    add_rows(out_acc, [out_sib], out_acc.shape)


def middle(values, weights, collective_id):
    vmem, hbm = pl.BlockSpec(memory_space=pltpu.VMEM), pl.BlockSpec(memory_space=pl.ANY)
    hidden = weights[0].shape[1]
    tall = hidden // SHARDS
    accs = [(2, 4, PAD, hidden), (2, 4, PAD, hidden), (2, 4, tall, PADDED), (2, 4, PAD, PADDED)]
    return pl.pallas_call(
        middle_kernel,
        out_shape=[
            jax.ShapeDtypeStruct((WIDTH, BLOCK), BF16),
            jax.ShapeDtypeStruct((BLOCK, PADDED), F32),
            jax.ShapeDtypeStruct((1, PADDED), F32),
            jax.ShapeDtypeStruct((BLOCK, WIDTH), BF16),
            *[jax.ShapeDtypeStruct(a, BF16) for a in accs],
        ],
        in_specs=[vmem] * len(values) + [hbm] * 4,
        out_specs=[vmem] * 8,
        scratch_shapes=[
            pltpu.VMEM((2, PADDED, STEP), BF16),
            pltpu.VMEM((2, PADDED, STEP), BF16),
            pltpu.VMEM((2, STEP, PADDED), BF16),
            pltpu.VMEM((2, 2, 4, 2, PAD, STEP), BF16),
            pltpu.VMEM((2, 2, 4, 2, PAD, STEP), BF16),
            pltpu.VMEM((2, 2, 2, STEP // 4, PADDED), BF16),
            pltpu.VMEM((2, 4, 2, PAD, PADDED), BF16),
            *[pltpu.VMEM(a, BF16) for a in accs],
            pltpu.VMEM((BLOCK, PADDED), F32),
            pltpu.VMEM((BLOCK, PADDED), F32),
            pltpu.SemaphoreType.DMA((2, 3)),
            pltpu.SemaphoreType.DMA((2, 4)),
            pltpu.SemaphoreType.DMA((3 * PARTS + 1,)),
            pltpu.SemaphoreType.DMA((3 * PARTS + 1,)),
        ],
        compiler_params=pltpu.CompilerParams(
            collective_id=collective_id, has_side_effects=True, vmem_limit_bytes=62 << 20
        ),
    )(*values, *weights)


def backward_kernel(
    gate_part,
    up_part,
    down_part,
    out_part,
    flat,
    grad_resid,
    grad_gain_two,
    cosine,
    sine,
    kv_w,
    q_w,
    normed_t,
    q_t,
    kv_all,
    o_t,
    lse,
    grad_mixed,
    gate_sum,
    up_sum,
    down_sum,
    out_sum,
    q_sum,
    kv_sum,
    d_tokens,
    do_t,
    do_n,
    q_n,
    dq_t,
    delta,
    dkv,
    landed,
    beside,
    grad_qkv,
    q_part,
    kv_part,
    send,
    recv,
    local,
    kv_send,
    kv_recv,
    *buffers,
):
    pc = Places()
    col = Column(pc)
    t, z, yl = col.t, pc.z, pc.yl
    greet([pc.sib, pc.ypair, pc.ylo, pc.yopp, *pc.xdev, *pc.zdev, *pc.xdiag, *pc.zdiag])
    sems, kv_sems = Sems(send, recv), Sems(kv_send, kv_recv)
    parts = (gate_part, up_part, down_part, out_part, q_part, kv_part)
    finals = (gate_sum, up_sum, down_sum, out_sum, q_sum, kv_sum)
    reduces = [
        reduce_steps(
            pc, sems, local.at[k], parts[k], finals[k], buffers[5 * k : 5 * k + 5], split
        )
        for k, split in enumerate(REDUCE_SPLITS)
    ]
    reduces += [
        small_steps(pc, sems, local.at[4 + k], parts[4 + k], finals[4 + k], buffers[20 + 5 * k : 25 + 5 * k])
        for k in range(2)
    ]
    r_gate, r_up, r_down, r_out, r_q, r_kv = reduces
    early = (r_up, r_down, r_gate, r_out)
    advance(r_up, r_gate, r_down, r_out)

    do_t[...] = jnp.zeros_like(do_t)
    for tile in range(8):
        if tile < 7:
            turned = flip(grad_mixed[:, tile * PAIR : (tile + 1) * PAIR])
        else:
            turned = flip(grad_mixed[:, tile * PAIR : tile * PAIR + HEAD_WIDTH])
        for side in range(2):
            head = 2 * tile + side
            if head < QUERY_HEADS:
                h, g = head // GROUP, head % GROUP
                do_t[h, HEAD_WIDTH:PAIR, g * BLOCK : (g + 1) * BLOCK] = turned[
                    side * HEAD_WIDTH : (side + 1) * HEAD_WIDTH
                ]
    for h in range(KEY_VALUE_HEADS):
        do_n[h] = flip(do_t[h])
        q_n[h] = flip(q_t[h])
        both = do_t[h, HEAD_WIDTH:PAIR].astype(F32) * o_t[h, HEAD_WIDTH:PAIR]
        delta[h] = jnp.broadcast_to(jnp.sum(both, axis=0, keepdims=True), (8, STACK))
    dq_t[...] = jnp.zeros_like(dq_t)

    def visit(j, diagonal):
        def per_head(h, carry):
            kv = kv_all[j, h]
            scores = dot(kv, q_t[h])
            if diagonal:
                key = lax.broadcasted_iota(jnp.int32, (BLOCK, STACK), 0)
                query = lax.broadcasted_iota(jnp.int32, (BLOCK, STACK), 1) % BLOCK
                scores = jnp.where(key <= query, scores, -1e30)
            probs = jnp.exp(scores - lse[h][0:1])
            grad_probs = dot(kv, do_t[h])
            grad_scores = (probs * (grad_probs - delta[h][0:1])).astype(BF16)
            both = dot(grad_scores, q_n[h]) + dot(probs.astype(BF16), do_n[h])
            dkv[j, h] = both.astype(BF16)
            dq_t[h] += dot(flip(kv), grad_scores)
            return carry

        lax.fori_loop(0, KEY_VALUE_HEADS, per_head, 0)


    for step in (3, 2, 1, 0):

        @pl.when((yl == 1) if step == 0 else (z - step >= 0))
        def _(step=step):
            j = col.other(-step)
            visit(j, False)
            kv_sems.push(step, dkv.at[j], beside.at[step], col.beside)

        if step == 3:
            pass
        if step == 2:
            advance(r_up)
        if step == 1:
            pass
        if step == 0:
            advance(r_down)
    for step in (3, 2, 1):

        @pl.when(z - step >= 0)
        def _(step=step):
            j = col.own(-step)
            visit(j, False)
            kv_sems.arrived(step, beside.at[step], col.beside)
            for h in range(KEY_VALUE_HEADS):
                total = dkv[j, h].astype(F32) + beside[step, h].astype(F32)
                dkv[j, h] = total.astype(BF16)
            kv_sems.push(3 + step, dkv.at[j], landed.at[step - 1], col.device(-step))

        if step == 3:
            pass
        if step == 2:
            pass
        if step == 1:
            pass
    visit(t, True)
    advance(r_gate, r_out)

    cos, sin = cosine[...], sine[...]

    def turn(tile):
        return tile * cos - swap_halves(tile) * sin

    for tile in range(8):
        pieces = []
        for head in (2 * tile, min(2 * tile + 1, QUERY_HEADS - 1)):
            h, g = head // GROUP, head % GROUP
            pieces.append(dq_t[h, 0:HEAD_WIDTH, g * BLOCK : (g + 1) * BLOCK])
        joined = turn(jnp.concatenate(pieces, axis=0).T * FACTOR)
        grad_qkv[:, tile * PAIR : (tile + 1) * PAIR] = joined.astype(BF16)
    rows = normed_t[...]
    for tile in range(Q_TILES):
        product = dot(rows, grad_qkv[:, tile * PAIR : (tile + 1) * PAIR])
        q_part[:, :, :, :, tile * PAIR : (tile + 1) * PAIR] = product.astype(BF16).reshape(
            2, 4, 2, PAD, PAIR
        )
    advance(r_q)
    advance(r_up)
    from_queries = dot_nt(
        grad_qkv[:, : Q_TILES * PAIR], q_w[...].reshape(PADDED, Q_TILES * PAIR)
    )

    @pl.when(yl == 0)
    def _():
        kv_sems.arrived(0, beside.at[0], col.beside)
        for h in range(KEY_VALUE_HEADS):
            total = dkv[t, h].astype(F32) + beside[0, h].astype(F32)
            dkv[t, h] = total.astype(BF16)

    for step in (1, 2, 3):

        @pl.when(z + step < 4)
        def _(step=step):
            kv_sems.arrived(3 + step, landed.at[step - 1], col.device(step))

    advance(r_q)
    low = low_half((BLOCK, PAIR))
    totals = []
    for h in range(KEY_VALUE_HEADS):

        def add(k, total, h=h):
            return total + landed[k, h].astype(F32)

        totals.append(lax.fori_loop(0, 3 - z, add, dkv[t, h].astype(F32)))
    zero = jnp.zeros((BLOCK, PAIR), F32)
    left = grad_qkv[:, 7 * PAIR : 8 * PAIR].astype(F32)
    first = turn(pltpu.roll(totals[0], HEAD_WIDTH, 1))
    grad_qkv[:, 7 * PAIR : 8 * PAIR] = jnp.where(low, left, first).astype(BF16)
    for n, (a, b) in enumerate(((1, 2), (3, 4))):
        keys = turn(jnp.where(low, totals[a], pltpu.roll(totals[b], HEAD_WIDTH, 1)))
        grad_qkv[:, (8 + n) * PAIR : (9 + n) * PAIR] = keys.astype(BF16)
    for n, (a, b) in enumerate(((0, 1), (2, 3), (4, None))):
        high = zero if b is None else totals[b]
        vals = jnp.where(low, pltpu.roll(totals[a], HEAD_WIDTH, 1), high)
        grad_qkv[:, (10 + n) * PAIR : (11 + n) * PAIR] = vals.astype(BF16)

    x = flat[...]
    scale = norm_scale(x)
    grad_normed = from_queries + dot_nt(
        grad_qkv[:, Q_TILES * PAIR :], kv_w[...].reshape(PADDED, KV_TILES * PAIR)
    )
    token_term, grad_gain = norm_back(grad_normed, x, scale, gain_row(kv_w, 0))
    row = lax.broadcasted_iota(jnp.int32, (8, PADDED), 0)
    gains = jnp.where(row == 0, grad_gain[None, :], jnp.where(row == 1, grad_gain_two[...], 0.0))
    lane = lax.broadcasted_iota(jnp.int32, (8, PAIR), 1)
    which = lax.broadcasted_iota(jnp.int32, (8, PAIR), 0)
    put = (lane == which + HEAD_WIDTH) & (which < 2)
    for tile in range(KV_TILES):
        at = Q_TILES + tile
        product = dot(rows, grad_qkv[:, at * PAIR : (at + 1) * PAIR])
        if tile == KV_TILES - 1:
            product = product + dot_tn(gains.astype(BF16), put.astype(BF16))
        kv_part[:, :, :, :, tile * PAIR : (tile + 1) * PAIR] = product.astype(BF16).reshape(
            2, 4, 2, PAD, PAIR
        )
    advance(r_kv)
    advance(r_down)
    d_tokens[...] = (grad_resid[...] + token_term).astype(BF16)

    drain(r_kv, r_q, *early)

    for step in (0, 1, 2, 3):

        @pl.when((yl == 1) if step == 0 else (z - step >= 0))
        def _(step=step):
            copy_wait(kv_sems, step, beside.at[step], col.beside)

    for step in (1, 2, 3):

        @pl.when(z - step >= 0)
        def _(step=step):
            copy_wait(kv_sems, 3 + step, landed.at[step - 1], col.device(-step))

    sems.finish()


REDUCE_SPLITS = (True, False, False, False)


def backward(parts, values, collective_id):
    vmem, hbm = pl.BlockSpec(memory_space=pltpu.VMEM), pl.BlockSpec(memory_space=pl.ANY)
    q_shape = (2, 4, 2, PAD, Q_TILES * PAIR)
    kv_shape = (2, 4, 2, PAD, KV_TILES * PAIR)
    shapes = [p.shape for p in parts] + [q_shape, kv_shape]
    scratch = [
        pltpu.VMEM((KEY_VALUE_HEADS, PAIR, STACK), BF16),
        pltpu.VMEM((KEY_VALUE_HEADS, STACK, PAIR), BF16),
        pltpu.VMEM((KEY_VALUE_HEADS, STACK, PAIR), BF16),
        pltpu.VMEM((KEY_VALUE_HEADS, PAIR, STACK), F32),
        pltpu.VMEM((KEY_VALUE_HEADS, 8, STACK), F32),
        pltpu.VMEM((8, KEY_VALUE_HEADS, BLOCK, PAIR), BF16),
        pltpu.VMEM((3, KEY_VALUE_HEADS, BLOCK, PAIR), BF16),
        pltpu.VMEM((4, KEY_VALUE_HEADS, BLOCK, PAIR), BF16),
        pltpu.VMEM((BLOCK, (Q_TILES + KV_TILES) * PAIR), BF16),
        pltpu.VMEM(q_shape, BF16),
        pltpu.VMEM(kv_shape, BF16),
        pltpu.SemaphoreType.DMA((6 * REDUCE_SEMS,)),
        pltpu.SemaphoreType.DMA((6 * REDUCE_SEMS,)),
        pltpu.SemaphoreType.DMA((6,)),
        pltpu.SemaphoreType.DMA((7,)),
        pltpu.SemaphoreType.DMA((7,)),
    ]
    for s, split in zip(shapes, REDUCE_SPLITS):
        scratch += reduce_scratch(*s[-2:], split)
    scratch += small_scratch(*q_shape[-2:]) + small_scratch(*kv_shape[-2:])
    return pl.pallas_call(
        backward_kernel,
        out_shape=[jax.ShapeDtypeStruct(s[-2:], BF16) for s in shapes]
        + [jax.ShapeDtypeStruct((BLOCK, PADDED), BF16)],
        in_specs=[hbm] * 4 + [vmem] * len(values),
        out_specs=[vmem] * 7,
        scratch_shapes=scratch,
        compiler_params=pltpu.CompilerParams(
            collective_id=collective_id, has_side_effects=True, vmem_limit_bytes=63 << 20
        ),
    )(*parts, *values)


def rotary_tables(token_positions):
    half = HEAD_WIDTH // 2
    freqs = ROPE_BASE ** (-jnp.arange(half, dtype=F32) * 2.0 / HEAD_WIDTH)
    angles = token_positions.astype(F32)[:, None] * freqs[None, :]
    cosine, sine = jnp.cos(angles), jnp.sin(angles)
    return (
        jnp.concatenate([cosine] * 4, axis=1),
        jnp.concatenate([-sine, sine] * 2, axis=1),
    )


def on_device(
    tokens,
    attn_gain,
    w_query,
    key_weight,
    value_weight,
    w_out,
    ffn_gain,
    w_gate,
    w_up,
    w_down,
    d_out,
):
    block = tokens.shape[1]
    token_positions = lax.axis_index("ctx") * block + jnp.arange(block, dtype=jnp.int32)
    cosine, sine = rotary_tables(token_positions)
    feature = jnp.arange(WIDTH, dtype=jnp.int32)
    place_of = feature // ROWS * PAD + feature % ROWS
    select = (place_of[:, None] == jnp.arange(PADDED, dtype=jnp.int32)[None, :]).astype(BF16)

    qkv_shard = jnp.pad(
        jnp.concatenate(
            [w_query, key_weight, value_weight, jnp.stack([attn_gain, ffn_gain]).T], axis=1
        ),
        ((0, PAD - ROWS), (0, (Q_TILES + KV_TILES) * PAIR - WIDTH - 2 * KV_WIDTH - 2)),
    )
    q_shard, kv_shard = qkv_shard[:, : Q_TILES * PAIR], qkv_shard[:, Q_TILES * PAIR :]
    kv_w, q_w, out_w, gate_w, up_a_w, up_b_w, down_w, *kept = forward(
        (tokens[0].T, cosine, sine, select),
        (kv_shard, q_shard),
        (w_out, w_gate, w_up, w_down),
        0,
    )
    normed_t, q_t, kv_all, o_t, lse, mixed, gain_two, flat = kept
    out_w = out_w.reshape(PADDED, PADDED)
    ffn_w = [w.reshape(PADDED, -1) for w in (gate_w, up_a_w, up_b_w)]
    ffn_w.append(down_w.reshape(-1, PADDED))
    output_t, grad_resid, grad_gain_two, grad_mixed, *parts = middle(
        (flat, d_out[0].T, mixed, gain_two, select, out_w), ffn_w, 2
    )
    sum_gate, sum_up, sum_down, sum_out, sum_q, sum_kv, d_tokens = backward(
        parts,
        (
            flat,
            grad_resid,
            grad_gain_two,
            cosine,
            sine,
            kv_w,
            q_w,
            normed_t,
            q_t,
            kv_all,
            o_t,
            lse,
            grad_mixed,
        ),
        1,
    )
    d_tokens = dot_nt(d_tokens, select).astype(BF16)
    sum_qkv = jnp.concatenate([sum_q, sum_kv], axis=1)[:ROWS].astype(F32)
    ends = (WIDTH, WIDTH + KV_WIDTH, WIDTH + 2 * KV_WIDTH)
    return (
        output_t.T[None],
        d_tokens[None],
        sum_qkv[:, ends[2]],
        sum_qkv[:, : ends[0]],
        sum_qkv[:, ends[0] : ends[1]],
        sum_qkv[:, ends[1] : ends[2]],
        dot_nt(sum_out[:ROWS], select),
        sum_qkv[:, ends[2] + 1],
        sum_gate[:ROWS].astype(F32),
        sum_up[:ROWS].astype(F32),
        dot_nt(sum_down, select),
    )


def solution(mesh):
    rows, whole, line = P("fsdp", None), P("fsdp", "ctx", None), P("fsdp")
    weights = (line, rows, rows, rows, rows, line, rows, rows, rows)
    return jax.shard_map(
        on_device,
        mesh=mesh,
        in_specs=(whole, *weights, whole),
        out_specs=(whole, whole, *weights),
        check_vma=False,
    )
```

```python
import functools
import math

import jax
import jax.numpy as jnp
from jax import lax
from jax.experimental import pallas as pl
from jax.experimental.pallas import tpu as pltpu
from jax.sharding import PartitionSpec as P

QUERY_HEADS = 15
KEY_VALUE_HEADS = 5
HEAD_WIDTH = 64
GROUP = QUERY_HEADS // KEY_VALUE_HEADS
WIDTH = 960
ROWS = 60
PAD = 64
SHARDS = 16
PADDED = SHARDS * PAD
KV_WIDTH = KEY_VALUE_HEADS * HEAD_WIDTH
Q_TILES = 7
KV_TILES = 6

EPS = 1e-05
ROPE_BASE = 10000.0
MESH = pl.DeviceIdType.MESH
BF16 = jnp.bfloat16
F32 = jnp.float32


def place():
    f, t = lax.axis_index("fsdp"), lax.axis_index("ctx")
    return f // 8, (f // 2) % 4, f % 2, t // 2, t % 2


def device(yh, x, c, z, yl):
    return ((yh * 4 + x) * 2 + c, z * 2 + yl)


class Places:
    def __init__(self):
        yh, x, c, z, yl = place()
        self.yh, self.x, self.c, self.z, self.yl = yh, x, c, z, yl
        self.sib = device(yh, x, 1 - c, z, yl)
        self.ypair = device(1 - yh, x, c, z, 1 - yl)
        self.ylo = device(yh, x, c, z, 1 - yl)
        self.xs = [(x + 1) % 4, (x + 3) % 4, (x + 2) % 4]
        self.zs = [(z + 1) % 4, (z + 3) % 4, (z + 2) % 4]
        self.yopp = device(1 - yh, x, c, z, yl)
        self.xdiag = [device(1 - yh, k, c, z, 1 - yl) for k in self.xs]
        self.zdiag = [device(yh, x, c, k, 1 - yl) for k in self.zs]
        self.xdev = [device(yh, k, c, z, yl) for k in self.xs]
        self.zdev = [device(yh, x, c, k, yl) for k in self.zs]
        self.xfrom = [self.xs[1], self.xs[0], self.xs[2]]
        self.zfrom = [self.zs[1], self.zs[0], self.zs[2]]


def greet(devices):
    barrier = pltpu.get_barrier_semaphore()
    for d in devices:
        pl.semaphore_signal(barrier, inc=1, device_id=d, device_id_type=MESH)
    pl.semaphore_wait(barrier, len(devices))


class Sems:
    def __init__(self, send, recv):
        self.send, self.recv, self.at, self.open = send, recv, 0, []

    def take(self, count=1):
        at = self.at
        self.at += count
        return at

    def push(self, slot, src, dst, dev):
        copy = pltpu.make_async_remote_copy(
            src_ref=src,
            dst_ref=dst,
            send_sem=self.send.at[slot],
            recv_sem=self.recv.at[slot],
            device_id=dev,
            device_id_type=MESH,
        )
        copy.start()
        self.open.append(copy)

    def arrived(self, slot, dst, dev):
        pltpu.make_async_remote_copy(
            src_ref=dst,
            dst_ref=dst,
            send_sem=self.send.at[slot],
            recv_sem=self.recv.at[slot],
            device_id=dev,
            device_id_type=MESH,
        ).wait_recv()

    def finish(self):
        for copy in self.open:
            copy.wait_send()
        self.open = []


GATHER_SEMS = 24


def gather_steps(pc, sems, local_sem, shard, out, split):
    rows = shard.shape[0]
    quarter = rows // 4
    yh, x, c, z = pc.yh, pc.x, pc.c, pc.z
    s_y = sems.take()
    s_x = [[sems.take() for _ in range(2)] for _ in range(3)]
    s_z = [[sems.take() for _ in range(3)] for _ in range(3)] if split else None
    s_s = [sems.take() for _ in range(4)]
    band = pl.ds(pl.multiple_of(z * quarter, 16), quarter) if split else pl.ds(0, rows)
    straight = (0, 1, 2) if split else (0, 1)

    own = pltpu.make_async_copy(shard, out.at[yh, x, c], local_sem)
    own.start()
    sems.push(s_y, shard, out.at[yh, x, c], pc.ypair)
    yield
    for k in straight:
        sems.push(s_x[k][0], shard.at[band], out.at[yh, x, c, band], pc.xdev[k])
    yield
    sems.arrived(s_y, out.at[1 - yh, x, c], pc.ypair)
    for k in straight:
        piece = out.at[1 - yh, x, c, band]
        sems.push(s_x[k][1], piece, piece, pc.xdev[k])
    own.wait()
    sems.push(s_s[3], out.at[:, x, c], out.at[:, x, c], pc.sib)
    yield
    for k in straight:
        far = pc.xfrom[k]
        sems.arrived(s_x[k][0], out.at[yh, far, c, band], pc.xdev[k])
        sems.arrived(s_x[k][1], out.at[1 - yh, far, c, band], pc.xdev[k])
        if split:
            piece = out.at[:, far, c, band]
            for j in range(3):
                sems.push(s_z[k][j], piece, piece, pc.zdev[j])
        else:
            piece = out.at[k, far, c]
            sems.push(s_x[2][k], piece, piece, pc.xdev[k])
            sems.push(s_s[k], out.at[:, far, c], out.at[:, far, c], pc.sib)
    yield
    if split:
        for k in (0, 1, 2):
            far = pc.xfrom[k]
            for j in range(3):
                there = pl.ds(pl.multiple_of(pc.zfrom[j] * quarter, 16), quarter)
                sems.arrived(s_z[k][j], out.at[:, far, c, there], pc.zdev[j])
            sems.push(s_s[k], out.at[:, far, c], out.at[:, far, c], pc.sib)
    else:
        far = pc.xs[2]
        for k in (0, 1):
            sems.arrived(s_x[2][k], out.at[k, far, c], pc.xdev[k])
        sems.push(s_s[2], out.at[:, far, c], out.at[:, far, c], pc.sib)
    yield
    for k in (0, 1, 2, 3):
        far = x if k == 3 else pc.xfrom[k]
        sems.arrived(s_s[k], out.at[:, far, 1 - c], pc.sib)
    yield


def run_all(steps):
    live = list(steps)
    while live:
        for s in list(live):
            try:
                next(s)
            except StopIteration:
                live.remove(s)


REDUCE_SEMS = 32


def add_rows(dst, terms, shape):
    lead, rows = shape[:-2], shape[-2]
    blocks = rows // 16
    count = math.prod(lead) * blocks

    def body(i, carry):
        idx, rest = [], i // blocks
        for size in reversed(lead):
            idx.append(rest % size)
            rest = rest // size
        idx = tuple(reversed(idx))
        at = (*idx, pl.ds(pl.multiple_of((i % blocks) * 16, 16), 16))
        total = dst[at].astype(F32)
        for term in terms:
            total = total + term[at].astype(F32)
        dst[at] = total.astype(BF16)
        return carry

    lax.fori_loop(0, count, body, 0)


def reduce_scratch(rows, width, split):
    q = rows // 4
    return [
        pltpu.VMEM((2, 4, rows, width), BF16),
        pltpu.VMEM((3 if split else 2, 2, q if split else rows, width), BF16),
        pltpu.VMEM((3, rows // 2, width), BF16),
        pltpu.VMEM((3, rows // 2, width // 4), BF16),
        pltpu.VMEM((3, 3, 2, q, width) if split else (2, rows, width), BF16),
    ]


def reduce_steps(pc, sems, local_sem, part, final, buffers, split):
    yh, x, c, z, yl = pc.yh, pc.x, pc.c, pc.z, pc.yl
    acc, from_x, from_y, from_z, from_r = buffers
    rows, width = part.shape[-2:]
    q = rows // 4
    s_m = sems.take()
    s_y = [sems.take() for _ in range(3)]
    s_x = [sems.take() for _ in range(3)]
    s_z = [sems.take() for _ in range(3)]
    s_f = [sems.take() for _ in range(3)]
    s_r = [[sems.take() for _ in range(3)] for _ in range(3)]

    def band(k):
        return pl.ds(pl.multiple_of(k * q, 16), q)

    own = pltpu.make_async_copy(part, acc, local_sem)
    own.start()
    own.wait()
    if split:
        here = band(z)
        order = (2, 0, 1)
        for k in order:
            for j in range(3):
                piece = acc.at[:, pc.xs[k], band(pc.zs[j])]
                sems.push(s_r[k][j], piece, from_r.at[j, k], pc.zdev[j])
        yield
        for k in order:
            for j in range(3):
                sems.arrived(s_r[k][j], from_r.at[j, k], pc.zdev[j])
            mine = acc.at[:, pc.xs[k], here]
            add_rows(mine, [from_r.at[j, k] for j in range(3)], (2, q, width))
            sems.push(s_x[k], mine, from_x.at[k], pc.xdev[k])
        yield
        for k in range(3):
            sems.arrived(s_x[k], from_x.at[k], pc.xdev[k])
        add_rows(acc.at[:, x, here], [from_x.at[k] for k in range(3)], (2, q, width))
    else:
        for k in range(2):
            sems.push(s_r[0][k], acc.at[k, pc.xs[2]], from_r.at[k], pc.xdev[k])
        yield
        for k in range(2):
            sems.arrived(s_r[0][k], from_r.at[k], pc.xdev[k])
            add_rows(acc.at[k, pc.xs[k]], [from_r.at[k]], (rows, width))
            sems.push(s_x[k], acc.at[:, pc.xs[k]], from_x.at[k], pc.xdev[k])
        yield
        for k in range(2):
            sems.arrived(s_x[k], from_x.at[k], pc.xdev[k])
        add_rows(acc.at[:, x], [from_x.at[k] for k in range(2)], (2, rows, width))
    h, w = rows // 2, width // 4

    def side(k):
        return pl.ds(pl.multiple_of(k * h, 16), h)

    def column(k):
        return pl.ds(pl.multiple_of(k * w, 128), w)

    half, other = side(yl), side(1 - yl)
    for n, (there, k) in enumerate(((yh, 1 - yl), (1 - yh, yl), (1 - yh, 1 - yl))):
        dev = device(there, x, c, z, k)
        sems.push(s_y[n], acc.at[there, x, side(k)], from_y.at[n], dev)
    yield
    for n in range(3):
        sems.arrived(s_y[n], from_y.at[n], pc.sib)
    add_rows(acc.at[yh, x, half], [from_y.at[n] for n in range(3)], (h, width))
    for j in range(3):
        piece = acc.at[yh, x, half, column(pc.zs[j])]
        sems.push(s_z[j], piece, from_z.at[j], pc.zdev[j])
    yield
    for j in range(3):
        sems.arrived(s_z[j], from_z.at[j], pc.zdev[j])
    mine = acc.at[yh, x, half, column(z)]
    add_rows(mine, [from_z.at[j] for j in range(3)], (h, w))
    done = final.at[half, column(z)]
    done[...] = mine[...]
    for j in range(3):
        sems.push(s_f[j], done, done, pc.zdev[j])
    yield
    for j in range(3):
        sems.arrived(s_f[j], final.at[half, column(pc.zfrom[j])], pc.zdev[j])
    sems.push(s_m, final.at[half], final.at[half], pc.ylo)
    yield
    sems.arrived(s_m, final.at[other], pc.ylo)
    yield


def small_scratch(rows, width):
    q = rows // 4
    return [
        pltpu.VMEM((2, 4, rows, width), BF16),
        pltpu.VMEM((2, 4, rows, width), BF16),
        pltpu.VMEM((3, 2, 4, q, width), BF16),
        pltpu.VMEM((7, q, width), BF16),
        pltpu.VMEM((2, rows, width), BF16),
    ]


def small_steps(pc, sems, local_sem, part, final, buffers):
    yh, x, c, z, yl = pc.yh, pc.x, pc.c, pc.z, pc.yl
    acc, from_sib, from_z, from_xy, landed = buffers
    rows, width = part.shape[-2:]
    q = rows // 4
    s_s = sems.take()
    s_z = [sems.take() for _ in range(3)]
    s_xy = [sems.take() for _ in range(7)]
    s_f = [sems.take() for _ in range(7)]

    def band(k):
        return pl.ds(pl.multiple_of(k * q, 16), q)

    here = band(z)
    own = pltpu.make_async_copy(part.at[:, :, c], acc, local_sem)
    own.start()
    sems.push(s_s, part.at[:, :, 1 - c], from_sib, pc.sib)
    yield
    own.wait()
    sems.arrived(s_s, from_sib, pc.sib)
    add_rows(acc, [from_sib], acc.shape)
    for j in range(3):
        sems.push(s_z[j], acc.at[:, :, band(pc.zs[j])], from_z.at[j], pc.zdev[j])
    yield
    for j in range(3):
        sems.arrived(s_z[j], from_z.at[j], pc.zdev[j])
    add_rows(acc.at[:, :, here], [from_z.at[j] for j in range(3)], (2, 4, q, width))
    targets = [(yh, pc.xs[k], yl) for k in range(3)]
    targets += [(1 - yh, k, 1 - yl) for k in (*pc.xs, x)]
    for n, (there, k, side) in enumerate(targets):
        sems.push(s_xy[n], acc.at[there, k, here], from_xy.at[n], device(there, k, c, z, side))
    yield
    for n in range(7):
        sems.arrived(s_xy[n], from_xy.at[n], pc.sib)
    mine = acc.at[yh, x, here]
    add_rows(mine, [from_xy.at[n] for n in range(7)], (q, width))
    landed[yl, here] = mine[...]
    for n, (k, side) in enumerate([(k, yl) for k in pc.zs] + [(k, 1 - yl) for k in (*pc.zs, z)]):
        sems.push(s_f[n], mine, landed.at[yl, here], device(yh, x, c, k, side))
    yield
    for n, (k, side) in enumerate(
        [(k, yl) for k in pc.zfrom] + [(k, 1 - yl) for k in (*pc.zfrom, z)]
    ):
        sems.arrived(s_f[n], landed.at[side, band(k)], pc.sib)

    def body(i, carry):
        at = pl.ds(pl.multiple_of(i * 16, 16), 16)
        total = landed[0, at].astype(F32) + landed[1, at].astype(F32)
        final[at] = total.astype(BF16)
        return carry

    lax.fori_loop(0, rows // 16, body, 0)
    yield


class Column:
    def __init__(self, pc):
        self.z, self.yl = pc.z, pc.yl
        self.t = 2 * pc.z + pc.yl
        self.beside = pc.ylo
        self.pc = pc

    def own(self, step):
        return 2 * (self.z + step) + self.yl

    def other(self, step):
        return 2 * (self.z + step) + 1 - self.yl

    def device(self, step):
        pc = self.pc
        return device(pc.yh, pc.x, pc.c, (pc.z + step + 4) % 4, pc.yl)


def dot(a, b):
    return jnp.dot(a, b, preferred_element_type=F32)


def dot_tn(a, b):
    return lax.dot_general(a, b, (((0,), (0,)), ((), ())), preferred_element_type=F32)


def dot_nt(a, b):
    return lax.dot_general(a, b, (((1,), (1,)), ((), ())), preferred_element_type=F32)


def norm_scale(rows):
    return lax.rsqrt(jnp.sum(rows * rows, axis=-1, keepdims=True) * (1.0 / WIDTH) + EPS)


def norm_back(grad_normed, rows, scale, gain):
    unit = rows * scale
    grad_gain = jnp.sum(grad_normed * unit, axis=0)
    grad_unit = grad_normed * gain
    mean = jnp.sum(grad_unit * unit, axis=-1, keepdims=True) * (1.0 / WIDTH)
    return scale * (grad_unit - unit * mean), grad_gain


BLOCK = 256
PAIR = 2 * HEAD_WIDTH
STACK = GROUP * BLOCK
FACTOR = HEAD_WIDTH ** (-0.5)


def low_half(shape):
    return lax.broadcasted_iota(jnp.int32, shape, 1) % PAIR < HEAD_WIDTH


def swap_halves(tile):
    lane = lax.broadcasted_iota(jnp.int32, tile.shape, 1) % HEAD_WIDTH
    half = HEAD_WIDTH // 2
    return jnp.where(
        lane < half, pltpu.roll(tile, PAIR - half, 1), pltpu.roll(tile, half, 1)
    )


def flip(a):
    return a.astype(F32).T.astype(a.dtype)


def advance(*steps):
    for s in steps:
        next(s, None)


def drain(*steps):
    run_all(steps)


def tile_of(ref, tile):
    return ref[:, :, :, :, tile * PAIR : (tile + 1) * PAIR].reshape(PADDED, PAIR)


def gain_row(kv_w, which):
    pick = lax.broadcasted_iota(jnp.int32, (8, PAIR), 1) == HEAD_WIDTH + which
    return dot_nt(pick.astype(BF16), tile_of(kv_w, KV_TILES - 1))[0:1]


def copy_wait(sems, slot, ref, dev):
    pltpu.make_async_remote_copy(
        src_ref=ref,
        dst_ref=ref,
        send_sem=sems.send.at[slot],
        recv_sem=sems.recv.at[slot],
        device_id=dev,
        device_id_type=MESH,
    ).wait_send()


def forward_kernel(
    tokens_t,
    cosine,
    sine,
    select,
    kv_shard,
    q_shard,
    own_out,
    own_gate,
    own_up,
    own_down,
    kv_out,
    q_out,
    out_w,
    gate_w,
    up_a_w,
    up_b_w,
    down_w,
    normed_out,
    queries_out,
    kv_all,
    o_t,
    lse,
    mixed,
    gain_two,
    flat_out,
    kv_w,
    q_w,
    normed_t,
    q_t,
    flat,
    store,
    peak,
    wide,
    out_shard,
    gate_shard,
    up_a_shard,
    up_b_shard,
    down_shard,
    send,
    recv,
    local,
    kv_send,
    kv_recv,
):
    pc = Places()
    col = Column(pc)
    t, z, yl = col.t, pc.z, pc.yl
    greet([pc.sib, pc.ypair, pc.ylo, *pc.xdev, *pc.zdev])
    sems, kv_sems = Sems(send, recv), Sems(kv_send, kv_recv)
    g_kv = gather_steps(pc, sems, local.at[0], kv_shard, kv_w, True)
    g_q = gather_steps(pc, sems, local.at[1], q_shard, q_w, False)
    g_out = gather_steps(pc, sems, local.at[2], out_shard, out_w, False)
    g_gate = gather_steps(pc, sems, local.at[3], gate_shard, gate_w, True)
    g_up = gather_steps(pc, sems, local.at[4], up_a_shard, up_a_w, True)
    g_half = gather_steps(pc, sems, local.at[5], up_b_shard, up_b_w, False)
    g_down = gather_steps(pc, sems, local.at[6], down_shard, down_w, False)
    advance(g_kv, g_kv, g_q)
    ones = (
        lax.broadcasted_iota(jnp.int32, (PAD, ROWS), 0)
        == lax.broadcasted_iota(jnp.int32, (PAD, ROWS), 1)
    ).astype(BF16)
    gate_shard[...] = dot(ones, own_gate[...]).astype(BF16)
    advance(g_gate, g_gate)
    half = up_a_shard.shape[1]
    up_a_shard[...] = dot(ones, own_up[:, :half]).astype(BF16)
    up_b_shard[...] = dot(ones, own_up[:, half:]).astype(BF16)
    advance(g_up)
    down_shard[...] = dot(own_down[...], select[...]).astype(BF16)
    out_shard[...] = dot(ones, dot(own_out[...], select[...]).astype(BF16)).astype(BF16)
    x = dot_tn(tokens_t[...], select[...])
    flat[...] = x
    stores = [
        pltpu.make_async_copy(src, dst, store.at[n])
        for n, (src, dst) in enumerate(
            ((flat, flat_out), (kv_w, kv_out), (q_w, q_out), (normed_t, normed_out), (q_t, queries_out))
        )
    ]
    stores[0].start()
    scale = norm_scale(x)
    advance(g_kv, g_q)
    advance(g_kv, g_q, g_gate, g_up)
    advance(g_kv, g_out, g_half, g_down)
    advance(g_kv)
    stores[1].start()

    rows = (x * scale * gain_row(kv_w, 0)).astype(BF16)
    gain_two[...] = gain_row(kv_w, 1)
    cos, sin = cosine[...], sine[...]
    low = low_half((BLOCK, PAIR))

    def place_queries(product, tile):
        turned = (product * FACTOR).T.astype(BF16)
        for side in range(2):
            head = 2 * tile + side
            if head < QUERY_HEADS:
                h, g = head // GROUP, head % GROUP
                at = slice(g * BLOCK, (g + 1) * BLOCK)
                q_t[h, 0:HEAD_WIDTH, at] = turned[side * HEAD_WIDTH : (side + 1) * HEAD_WIDTH]
                q_t[h, HEAD_WIDTH:PAIR, at] = jnp.zeros((HEAD_WIDTH, BLOCK), BF16)

    for tile in range(KV_TILES):
        product = dot(rows, tile_of(kv_w, tile))
        if tile < 3:
            product = product * cos + swap_halves(product) * sin
        wide[tile] = product
    for h in range(KEY_VALUE_HEADS):
        k_tile, k_high = (h + 1) // 2, (h + 1) % 2
        v_tile, v_high = 3 + h // 2, h % 2
        k_part, v_part = wide[k_tile], wide[v_tile]
        if k_high:
            k_part = pltpu.roll(k_part, HEAD_WIDTH, 1)
        if not v_high:
            v_part = pltpu.roll(v_part, HEAD_WIDTH, 1)
        kv_all[t, h] = jnp.where(low, k_part, v_part).astype(BF16)
    for step in (1, 2, 3):

        @pl.when(z + step < 4)
        def _(step=step):
            kv_sems.push(step - 1, kv_all.at[t], kv_all.at[t], col.device(step))

    @pl.when(yl == 0)
    def _():
        kv_sems.push(3, kv_all.at[t], kv_all.at[t], col.beside)

    advance(g_gate, g_up, g_q)
    advance(g_out, g_half, g_down)
    place_queries(wide[0], 7)
    normed_t[...] = flip(rows)
    stores[3].start()
    advance(g_q, g_up, g_q)
    stores[2].start()
    for tile in range(Q_TILES):
        product = dot(rows, tile_of(q_w, tile))
        place_queries(product * cos + swap_halves(product) * sin, tile)
    stores[4].start()
    peak[...] = jnp.full_like(peak, -1e30)
    o_t[...] = jnp.zeros_like(o_t)

    def visit(j, diagonal):
        def per_head(h, carry):
            kv = kv_all[j, h]
            kv_t = flip(kv)
            ones = lax.broadcasted_iota(jnp.int32, (PAIR, BLOCK), 0) < HEAD_WIDTH
            ones_v = jnp.where(ones, 1.0, kv_t.astype(F32)).astype(BF16)
            scores = dot(kv, q_t[h])
            if diagonal:
                key = lax.broadcasted_iota(jnp.int32, (BLOCK, STACK), 0)
                query = lax.broadcasted_iota(jnp.int32, (BLOCK, STACK), 1) % BLOCK
                scores = jnp.where(key <= query, scores, -1e30)
            old = peak[h]
            new = jnp.maximum(old, jnp.max(scores, axis=0, keepdims=True))
            probs = jnp.exp(scores - new[0:1]).astype(BF16)
            o_t[h] = o_t[h] * jnp.exp(old - new)[0:1] + dot(ones_v, probs)
            peak[h] = new
            return carry

        lax.fori_loop(0, KEY_VALUE_HEADS, per_head, 0)

    advance(g_out, g_half, g_down)
    visit(t, True)
    for step in (1, 2, 3):

        @pl.when(z - step >= 0)
        def _(step=step):
            block = kv_all.at[col.own(-step)]
            kv_sems.arrived(step - 1, block, col.device(-step))
            kv_sems.push(3 + step, block, block, col.beside)
            visit(col.own(-step), False)

        if step == 1:
            advance(g_out, g_half, g_down)
        if step == 2:
            advance(g_gate)
        if step == 3:
            advance(g_out, g_half, g_down)
    for step in (0, 1, 2, 3):

        @pl.when((yl == 1) if step == 0 else (z - step >= 0))
        def _(step=step):
            block = kv_all.at[col.other(-step)]
            kv_sems.arrived(3 + step, block, col.beside)
            visit(col.other(-step), False)

        if step == 1:
            advance(g_up)

    for h in range(KEY_VALUE_HEADS):
        total = o_t[h, 0:1]
        o_t[h] = o_t[h] * (1.0 / total)
        lse[h] = peak[h] + jnp.log(total)
    for tile in range(8):
        parts = []
        for head in (2 * tile, min(2 * tile + 1, QUERY_HEADS - 1)):
            h, g = head // GROUP, head % GROUP
            parts.append(o_t[h, HEAD_WIDTH:PAIR, g * BLOCK : (g + 1) * BLOCK])
        joined = jnp.concatenate(parts, axis=0).T.astype(BF16)
        if tile < 7:
            mixed[:, tile * PAIR : (tile + 1) * PAIR] = joined
        else:
            mixed[:, tile * PAIR : tile * PAIR + HEAD_WIDTH] = joined[:, :HEAD_WIDTH]
    drain(g_gate, g_up, g_half, g_down, g_out)
    for copy in stores:
        copy.wait()
    for step in (1, 2, 3):

        @pl.when(z + step < 4)
        def _(step=step):
            copy_wait(kv_sems, step - 1, kv_all.at[t], col.device(step))

        @pl.when(z - step >= 0)
        def _(step=step):
            copy_wait(kv_sems, 3 + step, kv_all.at[t], col.beside)

    @pl.when(yl == 0)
    def _():
        copy_wait(kv_sems, 3, kv_all.at[t], col.beside)

    sems.finish()


def forward(values, shards, weights, collective_id):
    vmem, hbm = pl.BlockSpec(memory_space=pltpu.VMEM), pl.BlockSpec(memory_space=pl.ANY)
    hidden = weights[1].shape[1]
    rows = [PAD] * 6 + [weights[3].shape[0]]
    widths = [s.shape[1] for s in shards] + [PADDED, hidden, hidden // 2, hidden // 2, PADDED]
    padded = list(zip(rows, widths))
    gathered = [jax.ShapeDtypeStruct((2, 4, 2, *p), BF16) for p in padded]
    return pl.pallas_call(
        forward_kernel,
        out_shape=[
            *gathered,
            jax.ShapeDtypeStruct((PADDED, BLOCK), BF16),
            jax.ShapeDtypeStruct((KEY_VALUE_HEADS, PAIR, STACK), BF16),
            jax.ShapeDtypeStruct((8, KEY_VALUE_HEADS, BLOCK, PAIR), BF16),
            jax.ShapeDtypeStruct((KEY_VALUE_HEADS, PAIR, STACK), F32),
            jax.ShapeDtypeStruct((KEY_VALUE_HEADS, 8, STACK), F32),
            jax.ShapeDtypeStruct((BLOCK, WIDTH), BF16),
            jax.ShapeDtypeStruct((1, PADDED), F32),
            jax.ShapeDtypeStruct((BLOCK, PADDED), F32),
        ],
        in_specs=[vmem] * 4 + [hbm] * 2 + [vmem] * 4,
        out_specs=[hbm] * 9 + [vmem] * 5 + [hbm],
        scratch_shapes=[
            pltpu.VMEM(gathered[0].shape, BF16),
            pltpu.VMEM(gathered[1].shape, BF16),
            pltpu.VMEM((PADDED, BLOCK), BF16),
            pltpu.VMEM((KEY_VALUE_HEADS, PAIR, STACK), BF16),
            pltpu.VMEM((BLOCK, PADDED), F32),
            pltpu.SemaphoreType.DMA((5,)),
            pltpu.VMEM((KEY_VALUE_HEADS, 8, STACK), F32),
            pltpu.VMEM((KV_TILES, BLOCK, PAIR), F32),
            *[pltpu.VMEM(p, BF16) for p in padded[2:]],
            pltpu.SemaphoreType.DMA((7 * GATHER_SEMS,)),
            pltpu.SemaphoreType.DMA((7 * GATHER_SEMS,)),
            pltpu.SemaphoreType.DMA((7,)),
            pltpu.SemaphoreType.DMA((7,)),
            pltpu.SemaphoreType.DMA((7,)),
        ],
        compiler_params=pltpu.CompilerParams(
            collective_id=collective_id, has_side_effects=True, vmem_limit_bytes=60 << 20
        ),
    )(*values, *shards, *weights)


PARTS = 4
STEP = 640


def middle_kernel(
    flat,
    d_out_t,
    mixed,
    gain_two,
    select,
    out_w,
    gate_w,
    up_a_w,
    up_b_w,
    down_w,
    output_t,
    grad_resid,
    grad_gain_two,
    grad_mixed,
    gate_out,
    up_out,
    down_out,
    out_out,
    gate_acc,
    up_acc,
    down_acc,
    out_acc,
    store,
    gate_buf,
    up_buf,
    down_buf,
    gate_stage,
    up_stage,
    down_stage,
    out_stage,
    gate_sib,
    up_sib,
    down_sib,
    out_sib,
    total,
    back,
    load,
    local,
    send,
    recv,
):
    pc = Places()
    c = pc.c

    def loads(i):
        at = pl.ds(i * STEP, STEP)
        slot = i % 2
        up_w, side = (up_a_w, up_b_w)[i // 2], pl.ds(slot * STEP, STEP)
        return (
            pltpu.make_async_copy(gate_w.at[:, at], gate_buf.at[slot], load.at[slot, 0]),
            pltpu.make_async_copy(up_w.at[:, side], up_buf.at[slot], load.at[slot, 1]),
            pltpu.make_async_copy(down_w.at[at], down_buf.at[slot], load.at[slot, 2]),
        )

    def remote(src, dst, k):
        return pltpu.make_async_remote_copy(
            src_ref=src,
            dst_ref=dst,
            send_sem=send.at[k],
            recv_sem=recv.at[k],
            device_id=pc.sib,
            device_id_type=MESH,
        )

    def sends(i):
        at, slot = pl.ds(i * STEP, STEP), i % 2
        yh, xs = i // 2, pl.ds(2 * (i % 2), 2)
        gate, up, down = gate_stage.at[slot], up_stage.at[slot], down_stage.at[slot]
        return (
            remote(gate.at[:, :, 1 - c], gate_sib.at[:, :, :, at], 3 * i),
            remote(up.at[:, :, 1 - c], up_sib.at[:, :, :, at], 3 * i + 1),
            remote(down.at[:, 1 - c], down_sib.at[yh, xs], 3 * i + 2),
            pltpu.make_async_copy(gate.at[:, :, c], gate_acc.at[:, :, :, at], local.at[slot, 0]),
            pltpu.make_async_copy(up.at[:, :, c], up_acc.at[:, :, :, at], local.at[slot, 1]),
            pltpu.make_async_copy(down.at[:, c], down_acc.at[yh, xs], local.at[slot, 2]),
        )

    def sent(i):
        copies = sends(i)
        for copy in copies[:3]:
            copy.wait_send()
        for copy in copies[3:]:
            copy.wait()

    for copy in loads(0):
        copy.start()
    greet([pc.sib])
    mixed_p = dot(mixed[...], select[...]).astype(BF16)
    resid = flat[...] + dot(mixed_p, out_w[...])
    scale = norm_scale(resid)
    gain = gain_two[...]
    normed = (resid * scale * gain).astype(BF16)
    normed_t = flip(normed)
    grad = dot_tn(d_out_t[...], select[...]).astype(BF16)
    total[...] = resid
    back[...] = jnp.zeros_like(back)
    for i in range(PARTS):
        slot = i % 2
        if i + 1 < PARTS:
            for copy in loads(i + 1):
                copy.start()
        for copy in loads(i):
            copy.wait()
        if i >= 2:
            sent(i - 2)
        w_gate, w_up, w_down = gate_buf[slot], up_buf[slot], down_buf[slot]
        gate = dot(normed, w_gate)
        up = dot(normed, w_up)
        grad_hidden = dot_nt(grad, w_down)
        sigmoid = 0.5 * jnp.tanh(0.5 * gate) + 0.5
        swish = gate * sigmoid
        hidden = (swish * up).astype(BF16)
        grad_up_v = (grad_hidden * swish).astype(BF16)
        grad_gate_v = (grad_hidden * up * sigmoid * (1.0 + gate * (1.0 - sigmoid))).astype(BF16)
        total[...] += dot(hidden, w_down)
        back[...] += dot_nt(grad_gate_v, w_gate) + dot_nt(grad_up_v, w_up)
        shape = (2, 4, 2, PAD, STEP)
        gate_stage[slot] = dot(normed_t, grad_gate_v).astype(BF16).reshape(shape)
        up_stage[slot] = dot(normed_t, grad_up_v).astype(BF16).reshape(shape)
        down = dot(flip(hidden), grad).astype(BF16)
        down_stage[slot] = down.reshape(2, 2, STEP // 4, PADDED)
        for copy in sends(i):
            copy.start()
    output_t[...] = dot_nt(select[...], total[...].astype(BF16)).astype(BF16)
    term, grad_gain = norm_back(back[...], resid, scale, gain)
    grad_gain_two[...] = grad_gain[None, :]
    full = grad.astype(F32) + term
    grad_resid[...] = full
    branch = full.astype(BF16)
    out_stage[...] = dot(flip(mixed_p), branch).astype(BF16).reshape(2, 4, 2, PAD, PADDED)
    out_send = remote(out_stage.at[:, :, 1 - c], out_sib, 3 * PARTS)
    out_send.start()
    out_copy = pltpu.make_async_copy(out_stage.at[:, :, c], out_acc, local.at[0, 3])
    out_copy.start()
    inner = dot_nt(branch, out_w[...]).astype(BF16)
    grad_mixed[...] = dot_nt(inner, select[...]).astype(BF16)
    for i in (PARTS - 2, PARTS - 1):
        sent(i)
    for i in range(PARTS):
        for copy in sends(i)[:3]:
            copy.wait_recv()
    stores = []

    def finish(acc, other, out):
        add_rows(acc, [other], acc.shape)
        stores.append(pltpu.make_async_copy(acc, out, store.at[len(stores)]))
        stores[-1].start()

    finish(gate_acc, gate_sib, gate_out)
    finish(up_acc, up_sib, up_out)
    finish(down_acc, down_sib, down_out)
    out_send.wait()
    out_copy.wait()
    finish(out_acc, out_sib, out_out)
    for copy in stores:
        copy.wait()


def middle(values, weights, collective_id):
    vmem, hbm = pl.BlockSpec(memory_space=pltpu.VMEM), pl.BlockSpec(memory_space=pl.ANY)
    hidden = weights[0].shape[1]
    tall = hidden // SHARDS
    accs = [(2, 4, PAD, hidden), (2, 4, PAD, hidden), (2, 4, tall, PADDED), (2, 4, PAD, PADDED)]
    return pl.pallas_call(
        middle_kernel,
        out_shape=[
            jax.ShapeDtypeStruct((WIDTH, BLOCK), BF16),
            jax.ShapeDtypeStruct((BLOCK, PADDED), F32),
            jax.ShapeDtypeStruct((1, PADDED), F32),
            jax.ShapeDtypeStruct((BLOCK, WIDTH), BF16),
            *[jax.ShapeDtypeStruct(a, BF16) for a in accs],
        ],
        in_specs=[vmem] * len(values) + [hbm] * 4,
        out_specs=[vmem] * 4 + [hbm] * 4,
        scratch_shapes=[
            *[pltpu.VMEM(a, BF16) for a in accs],
            pltpu.SemaphoreType.DMA((4,)),
            pltpu.VMEM((2, PADDED, STEP), BF16),
            pltpu.VMEM((2, PADDED, STEP), BF16),
            pltpu.VMEM((2, STEP, PADDED), BF16),
            pltpu.VMEM((2, 2, 4, 2, PAD, STEP), BF16),
            pltpu.VMEM((2, 2, 4, 2, PAD, STEP), BF16),
            pltpu.VMEM((2, 2, 2, STEP // 4, PADDED), BF16),
            pltpu.VMEM((2, 4, 2, PAD, PADDED), BF16),
            *[pltpu.VMEM(a, BF16) for a in accs],
            pltpu.VMEM((BLOCK, PADDED), F32),
            pltpu.VMEM((BLOCK, PADDED), F32),
            pltpu.SemaphoreType.DMA((2, 3)),
            pltpu.SemaphoreType.DMA((2, 4)),
            pltpu.SemaphoreType.DMA((3 * PARTS + 1,)),
            pltpu.SemaphoreType.DMA((3 * PARTS + 1,)),
        ],
        compiler_params=pltpu.CompilerParams(
            collective_id=collective_id, has_side_effects=True, vmem_limit_bytes=62 << 20
        ),
    )(*values, *weights)


def backward_kernel(
    gate_part,
    up_part,
    down_part,
    out_part,
    flat_in,
    grad_resid_in,
    grad_gain_two,
    cosine,
    sine,
    kv_in,
    q_in,
    normed_t,
    q_t,
    kv_all,
    o_t,
    lse,
    grad_mixed,
    gate_sum,
    up_sum,
    down_sum,
    out_sum,
    q_sum,
    kv_sum,
    d_tokens,
    flat,
    grad_resid,
    kv_w,
    q_w,
    load,
    do_t,
    do_n,
    q_n,
    dq_t,
    delta,
    dkv,
    landed,
    beside,
    grad_qkv,
    q_part,
    kv_part,
    send,
    recv,
    local,
    kv_send,
    kv_recv,
    *buffers,
):
    pc = Places()
    col = Column(pc)
    t, z, yl = col.t, pc.z, pc.yl
    loads = [
        pltpu.make_async_copy(src, dst, load.at[n])
        for n, (src, dst) in enumerate(
            ((q_in, q_w), (kv_in, kv_w), (flat_in, flat), (grad_resid_in, grad_resid))
        )
    ]
    greet([pc.sib, pc.ypair, pc.ylo, pc.yopp, *pc.xdev, *pc.zdev, *pc.xdiag, *pc.zdiag])
    sems, kv_sems = Sems(send, recv), Sems(kv_send, kv_recv)
    parts = (gate_part, up_part, down_part, out_part, q_part, kv_part)
    finals = (gate_sum, up_sum, down_sum, out_sum, q_sum, kv_sum)
    reduces = [
        reduce_steps(
            pc, sems, local.at[k], parts[k], finals[k], buffers[5 * k : 5 * k + 5], split
        )
        for k, split in enumerate(REDUCE_SPLITS)
    ]
    reduces += [
        small_steps(pc, sems, local.at[4 + k], parts[4 + k], finals[4 + k], buffers[20 + 5 * k : 25 + 5 * k])
        for k in range(2)
    ]
    r_gate, r_up, r_down, r_out, r_q, r_kv = reduces
    early = (r_up, r_down, r_gate, r_out)
    advance(r_up, r_gate, r_down, r_out)

    for copy in loads:
        copy.start()
    do_t[...] = jnp.zeros_like(do_t)
    for tile in range(8):
        if tile < 7:
            turned = flip(grad_mixed[:, tile * PAIR : (tile + 1) * PAIR])
        else:
            turned = flip(grad_mixed[:, tile * PAIR : tile * PAIR + HEAD_WIDTH])
        for side in range(2):
            head = 2 * tile + side
            if head < QUERY_HEADS:
                h, g = head // GROUP, head % GROUP
                do_t[h, HEAD_WIDTH:PAIR, g * BLOCK : (g + 1) * BLOCK] = turned[
                    side * HEAD_WIDTH : (side + 1) * HEAD_WIDTH
                ]
    for h in range(KEY_VALUE_HEADS):
        do_n[h] = flip(do_t[h])
        q_n[h] = flip(q_t[h])
        both = do_t[h, HEAD_WIDTH:PAIR].astype(F32) * o_t[h, HEAD_WIDTH:PAIR]
        delta[h] = jnp.broadcast_to(jnp.sum(both, axis=0, keepdims=True), (8, STACK))
    dq_t[...] = jnp.zeros_like(dq_t)

    def visit(j, diagonal):
        def per_head(h, carry):
            kv = kv_all[j, h]
            scores = dot(kv, q_t[h])
            if diagonal:
                key = lax.broadcasted_iota(jnp.int32, (BLOCK, STACK), 0)
                query = lax.broadcasted_iota(jnp.int32, (BLOCK, STACK), 1) % BLOCK
                scores = jnp.where(key <= query, scores, -1e30)
            probs = jnp.exp(scores - lse[h][0:1])
            grad_probs = dot(kv, do_t[h])
            grad_scores = (probs * (grad_probs - delta[h][0:1])).astype(BF16)
            both = dot(grad_scores, q_n[h]) + dot(probs.astype(BF16), do_n[h])
            dkv[j, h] = both.astype(BF16)
            dq_t[h] += dot(flip(kv), grad_scores)
            return carry

        lax.fori_loop(0, KEY_VALUE_HEADS, per_head, 0)


    for step in (3, 2, 1, 0):

        @pl.when((yl == 1) if step == 0 else (z - step >= 0))
        def _(step=step):
            j = col.other(-step)
            visit(j, False)
            kv_sems.push(step, dkv.at[j], beside.at[step], col.beside)

        if step == 3:
            pass
        if step == 2:
            advance(r_up)
        if step == 1:
            pass
        if step == 0:
            advance(r_down)
    for step in (3, 2, 1):

        @pl.when(z - step >= 0)
        def _(step=step):
            j = col.own(-step)
            visit(j, False)
            kv_sems.arrived(step, beside.at[step], col.beside)
            for h in range(KEY_VALUE_HEADS):
                total = dkv[j, h].astype(F32) + beside[step, h].astype(F32)
                dkv[j, h] = total.astype(BF16)
            kv_sems.push(3 + step, dkv.at[j], landed.at[step - 1], col.device(-step))

        if step == 3:
            pass
        if step == 2:
            pass
        if step == 1:
            pass
    visit(t, True)
    advance(r_gate, r_out)

    cos, sin = cosine[...], sine[...]

    def turn(tile):
        return tile * cos - swap_halves(tile) * sin

    for tile in range(8):
        pieces = []
        for head in (2 * tile, min(2 * tile + 1, QUERY_HEADS - 1)):
            h, g = head // GROUP, head % GROUP
            pieces.append(dq_t[h, 0:HEAD_WIDTH, g * BLOCK : (g + 1) * BLOCK])
        joined = turn(jnp.concatenate(pieces, axis=0).T * FACTOR)
        grad_qkv[:, tile * PAIR : (tile + 1) * PAIR] = joined.astype(BF16)
    rows = normed_t[...]
    for tile in range(Q_TILES):
        product = dot(rows, grad_qkv[:, tile * PAIR : (tile + 1) * PAIR])
        q_part[:, :, :, :, tile * PAIR : (tile + 1) * PAIR] = product.astype(BF16).reshape(
            2, 4, 2, PAD, PAIR
        )
    advance(r_q)
    advance(r_up)
    for copy in loads:
        copy.wait()
    from_queries = dot_nt(
        grad_qkv[:, : Q_TILES * PAIR], q_w[...].reshape(PADDED, Q_TILES * PAIR)
    )

    @pl.when(yl == 0)
    def _():
        kv_sems.arrived(0, beside.at[0], col.beside)
        for h in range(KEY_VALUE_HEADS):
            total = dkv[t, h].astype(F32) + beside[0, h].astype(F32)
            dkv[t, h] = total.astype(BF16)

    for step in (1, 2, 3):

        @pl.when(z + step < 4)
        def _(step=step):
            kv_sems.arrived(3 + step, landed.at[step - 1], col.device(step))

    advance(r_q)
    low = low_half((BLOCK, PAIR))
    totals = []
    for h in range(KEY_VALUE_HEADS):

        def add(k, total, h=h):
            return total + landed[k, h].astype(F32)

        totals.append(lax.fori_loop(0, 3 - z, add, dkv[t, h].astype(F32)))
    zero = jnp.zeros((BLOCK, PAIR), F32)
    left = grad_qkv[:, 7 * PAIR : 8 * PAIR].astype(F32)
    first = turn(pltpu.roll(totals[0], HEAD_WIDTH, 1))
    grad_qkv[:, 7 * PAIR : 8 * PAIR] = jnp.where(low, left, first).astype(BF16)
    for n, (a, b) in enumerate(((1, 2), (3, 4))):
        keys = turn(jnp.where(low, totals[a], pltpu.roll(totals[b], HEAD_WIDTH, 1)))
        grad_qkv[:, (8 + n) * PAIR : (9 + n) * PAIR] = keys.astype(BF16)
    for n, (a, b) in enumerate(((0, 1), (2, 3), (4, None))):
        high = zero if b is None else totals[b]
        vals = jnp.where(low, pltpu.roll(totals[a], HEAD_WIDTH, 1), high)
        grad_qkv[:, (10 + n) * PAIR : (11 + n) * PAIR] = vals.astype(BF16)

    x = flat[...]
    scale = norm_scale(x)
    grad_normed = from_queries + dot_nt(
        grad_qkv[:, Q_TILES * PAIR :], kv_w[...].reshape(PADDED, KV_TILES * PAIR)
    )
    token_term, grad_gain = norm_back(grad_normed, x, scale, gain_row(kv_w, 0))
    row = lax.broadcasted_iota(jnp.int32, (8, PADDED), 0)
    gains = jnp.where(row == 0, grad_gain[None, :], jnp.where(row == 1, grad_gain_two[...], 0.0))
    lane = lax.broadcasted_iota(jnp.int32, (8, PAIR), 1)
    which = lax.broadcasted_iota(jnp.int32, (8, PAIR), 0)
    put = (lane == which + HEAD_WIDTH) & (which < 2)
    for tile in range(KV_TILES):
        at = Q_TILES + tile
        product = dot(rows, grad_qkv[:, at * PAIR : (at + 1) * PAIR])
        if tile == KV_TILES - 1:
            product = product + dot_tn(gains.astype(BF16), put.astype(BF16))
        kv_part[:, :, :, :, tile * PAIR : (tile + 1) * PAIR] = product.astype(BF16).reshape(
            2, 4, 2, PAD, PAIR
        )
    advance(r_kv)
    advance(r_down)
    d_tokens[...] = (grad_resid[...] + token_term).astype(BF16)

    drain(r_kv, r_q, *early)

    for step in (0, 1, 2, 3):

        @pl.when((yl == 1) if step == 0 else (z - step >= 0))
        def _(step=step):
            copy_wait(kv_sems, step, beside.at[step], col.beside)

    for step in (1, 2, 3):

        @pl.when(z - step >= 0)
        def _(step=step):
            copy_wait(kv_sems, 3 + step, landed.at[step - 1], col.device(-step))

    sems.finish()


REDUCE_SPLITS = (True, False, False, False)


def backward(parts, values, collective_id):
    vmem, hbm = pl.BlockSpec(memory_space=pltpu.VMEM), pl.BlockSpec(memory_space=pl.ANY)
    q_shape = (2, 4, 2, PAD, Q_TILES * PAIR)
    kv_shape = (2, 4, 2, PAD, KV_TILES * PAIR)
    shapes = [p.shape for p in parts] + [q_shape, kv_shape]
    scratch = [
        pltpu.VMEM((BLOCK, PADDED), F32),
        pltpu.VMEM((BLOCK, PADDED), F32),
        pltpu.VMEM(kv_shape, BF16),
        pltpu.VMEM(q_shape, BF16),
        pltpu.SemaphoreType.DMA((4,)),
        pltpu.VMEM((KEY_VALUE_HEADS, PAIR, STACK), BF16),
        pltpu.VMEM((KEY_VALUE_HEADS, STACK, PAIR), BF16),
        pltpu.VMEM((KEY_VALUE_HEADS, STACK, PAIR), BF16),
        pltpu.VMEM((KEY_VALUE_HEADS, PAIR, STACK), F32),
        pltpu.VMEM((KEY_VALUE_HEADS, 8, STACK), F32),
        pltpu.VMEM((8, KEY_VALUE_HEADS, BLOCK, PAIR), BF16),
        pltpu.VMEM((3, KEY_VALUE_HEADS, BLOCK, PAIR), BF16),
        pltpu.VMEM((4, KEY_VALUE_HEADS, BLOCK, PAIR), BF16),
        pltpu.VMEM((BLOCK, (Q_TILES + KV_TILES) * PAIR), BF16),
        pltpu.VMEM(q_shape, BF16),
        pltpu.VMEM(kv_shape, BF16),
        pltpu.SemaphoreType.DMA((6 * REDUCE_SEMS,)),
        pltpu.SemaphoreType.DMA((6 * REDUCE_SEMS,)),
        pltpu.SemaphoreType.DMA((6,)),
        pltpu.SemaphoreType.DMA((7,)),
        pltpu.SemaphoreType.DMA((7,)),
    ]
    for s, split in zip(shapes, REDUCE_SPLITS):
        scratch += reduce_scratch(*s[-2:], split)
    scratch += small_scratch(*q_shape[-2:]) + small_scratch(*kv_shape[-2:])
    return pl.pallas_call(
        backward_kernel,
        out_shape=[jax.ShapeDtypeStruct(s[-2:], BF16) for s in shapes]
        + [jax.ShapeDtypeStruct((BLOCK, PADDED), BF16)],
        in_specs=[hbm] * 6 + [vmem] * 3 + [hbm] * 2 + [vmem] * (len(values) - 7),
        out_specs=[vmem] * 7,
        scratch_shapes=scratch,
        compiler_params=pltpu.CompilerParams(
            collective_id=collective_id, has_side_effects=True, vmem_limit_bytes=63 << 20
        ),
    )(*parts, *values)


def rotary_tables(token_positions):
    half = HEAD_WIDTH // 2
    freqs = ROPE_BASE ** (-jnp.arange(half, dtype=F32) * 2.0 / HEAD_WIDTH)
    angles = token_positions.astype(F32)[:, None] * freqs[None, :]
    cosine, sine = jnp.cos(angles), jnp.sin(angles)
    return (
        jnp.concatenate([cosine] * 4, axis=1),
        jnp.concatenate([-sine, sine] * 2, axis=1),
    )


def on_device(
    tokens,
    attn_gain,
    w_query,
    key_weight,
    value_weight,
    w_out,
    ffn_gain,
    w_gate,
    w_up,
    w_down,
    d_out,
):
    block = tokens.shape[1]
    token_positions = lax.axis_index("ctx") * block + jnp.arange(block, dtype=jnp.int32)
    cosine, sine = rotary_tables(token_positions)
    feature = jnp.arange(WIDTH, dtype=jnp.int32)
    place_of = feature // ROWS * PAD + feature % ROWS
    select = (place_of[:, None] == jnp.arange(PADDED, dtype=jnp.int32)[None, :]).astype(BF16)

    qkv_shard = jnp.pad(
        jnp.concatenate(
            [w_query, key_weight, value_weight, jnp.stack([attn_gain, ffn_gain]).T], axis=1
        ),
        ((0, PAD - ROWS), (0, (Q_TILES + KV_TILES) * PAIR - WIDTH - 2 * KV_WIDTH - 2)),
    )
    q_shard, kv_shard = qkv_shard[:, : Q_TILES * PAIR], qkv_shard[:, Q_TILES * PAIR :]
    kv_w, q_w, out_w, gate_w, up_a_w, up_b_w, down_w, *kept = forward(
        (tokens[0].T, cosine, sine, select),
        (kv_shard, q_shard),
        (w_out, w_gate, w_up, w_down),
        0,
    )
    normed_t, q_t, kv_all, o_t, lse, mixed, gain_two, flat = kept
    out_w = out_w.reshape(PADDED, PADDED)
    ffn_w = [w.reshape(PADDED, -1) for w in (gate_w, up_a_w, up_b_w)]
    ffn_w.append(down_w.reshape(-1, PADDED))
    output_t, grad_resid, grad_gain_two, grad_mixed, *parts = middle(
        (flat, d_out[0].T, mixed, gain_two, select, out_w), ffn_w, 2
    )
    sum_gate, sum_up, sum_down, sum_out, sum_q, sum_kv, d_tokens = backward(
        parts,
        (
            flat,
            grad_resid,
            grad_gain_two,
            cosine,
            sine,
            kv_w,
            q_w,
            normed_t,
            q_t,
            kv_all,
            o_t,
            lse,
            grad_mixed,
        ),
        1,
    )
    d_tokens = dot_nt(d_tokens, select).astype(BF16)
    sum_qkv = jnp.concatenate([sum_q, sum_kv], axis=1)[:ROWS].astype(F32)
    ends = (WIDTH, WIDTH + KV_WIDTH, WIDTH + 2 * KV_WIDTH)
    return (
        output_t.T[None],
        d_tokens[None],
        sum_qkv[:, ends[2]],
        sum_qkv[:, : ends[0]],
        sum_qkv[:, ends[0] : ends[1]],
        sum_qkv[:, ends[1] : ends[2]],
        dot_nt(sum_out[:ROWS], select),
        sum_qkv[:, ends[2] + 1],
        sum_gate[:ROWS].astype(F32),
        sum_up[:ROWS].astype(F32),
        dot_nt(sum_down, select),
    )


def solution(mesh):
    rows, whole, line = P("fsdp", None), P("fsdp", "ctx", None), P("fsdp")
    weights = (line, rows, rows, rows, rows, line, rows, rows, rows)
    return jax.shard_map(
        on_device,
        mesh=mesh,
        in_specs=(whole, *weights, whole),
        out_specs=(whole, whole, *weights),
        check_vma=False,
    )
```

```python
import functools
import math

import jax
import jax.numpy as jnp
from jax import lax
from jax.experimental import pallas as pl
from jax.experimental.pallas import tpu as pltpu
from jax.sharding import PartitionSpec as P

QUERY_HEADS = 15
KEY_VALUE_HEADS = 5
HEAD_WIDTH = 64
GROUP = QUERY_HEADS // KEY_VALUE_HEADS
WIDTH = 960
ROWS = 60
PAD = 64
SHARDS = 16
PADDED = SHARDS * PAD
KV_WIDTH = KEY_VALUE_HEADS * HEAD_WIDTH
Q_TILES = 7
KV_TILES = 6

EPS = 1e-05
ROPE_BASE = 10000.0
MESH = pl.DeviceIdType.MESH
BF16 = jnp.bfloat16
F32 = jnp.float32


def place():
    f, t = lax.axis_index("fsdp"), lax.axis_index("ctx")
    return f // 8, (f // 2) % 4, f % 2, t // 2, t % 2


def device(yh, x, c, z, yl):
    return ((yh * 4 + x) * 2 + c, z * 2 + yl)


class Places:
    def __init__(self):
        yh, x, c, z, yl = place()
        self.yh, self.x, self.c, self.z, self.yl = yh, x, c, z, yl
        self.sib = device(yh, x, 1 - c, z, yl)
        self.ypair = device(1 - yh, x, c, z, 1 - yl)
        self.ylo = device(yh, x, c, z, 1 - yl)
        self.xs = [(x + 1) % 4, (x + 3) % 4, (x + 2) % 4]
        self.zs = [(z + 1) % 4, (z + 3) % 4, (z + 2) % 4]
        self.yopp = device(1 - yh, x, c, z, yl)
        self.xdiag = [device(1 - yh, k, c, z, 1 - yl) for k in self.xs]
        self.zdiag = [device(yh, x, c, k, 1 - yl) for k in self.zs]
        self.xdev = [device(yh, k, c, z, yl) for k in self.xs]
        self.zdev = [device(yh, x, c, k, yl) for k in self.zs]
        self.xfrom = [self.xs[1], self.xs[0], self.xs[2]]
        self.zfrom = [self.zs[1], self.zs[0], self.zs[2]]


def greet(devices):
    barrier = pltpu.get_barrier_semaphore()
    for d in devices:
        pl.semaphore_signal(barrier, inc=1, device_id=d, device_id_type=MESH)
    pl.semaphore_wait(barrier, len(devices))


class Sems:
    def __init__(self, send, recv):
        self.send, self.recv, self.at, self.open = send, recv, 0, []

    def take(self, count=1):
        at = self.at
        self.at += count
        return at

    def push(self, slot, src, dst, dev):
        copy = pltpu.make_async_remote_copy(
            src_ref=src,
            dst_ref=dst,
            send_sem=self.send.at[slot],
            recv_sem=self.recv.at[slot],
            device_id=dev,
            device_id_type=MESH,
        )
        copy.start()
        self.open.append(copy)

    def arrived(self, slot, dst, dev):
        pltpu.make_async_remote_copy(
            src_ref=dst,
            dst_ref=dst,
            send_sem=self.send.at[slot],
            recv_sem=self.recv.at[slot],
            device_id=dev,
            device_id_type=MESH,
        ).wait_recv()

    def finish(self):
        for copy in self.open:
            copy.wait_send()
        self.open = []


GATHER_SEMS = 24


def gather_steps(pc, sems, local_sem, shard, out, split):
    rows = shard.shape[0]
    quarter = rows // 4
    yh, x, c, z = pc.yh, pc.x, pc.c, pc.z
    s_y = sems.take()
    s_x = [[sems.take() for _ in range(2)] for _ in range(3)]
    s_z = [[sems.take() for _ in range(3)] for _ in range(3)] if split else None
    s_s = [sems.take() for _ in range(4)]
    band = pl.ds(pl.multiple_of(z * quarter, 16), quarter) if split else pl.ds(0, rows)
    straight = (0, 1, 2) if split else (0, 1)

    own = pltpu.make_async_copy(shard, out.at[yh, x, c], local_sem)
    own.start()
    sems.push(s_y, shard, out.at[yh, x, c], pc.ypair)
    yield
    for k in straight:
        sems.push(s_x[k][0], shard.at[band], out.at[yh, x, c, band], pc.xdev[k])
    yield
    sems.arrived(s_y, out.at[1 - yh, x, c], pc.ypair)
    for k in straight:
        piece = out.at[1 - yh, x, c, band]
        sems.push(s_x[k][1], piece, piece, pc.xdev[k])
    own.wait()
    sems.push(s_s[3], out.at[:, x, c], out.at[:, x, c], pc.sib)
    yield
    for k in straight:
        far = pc.xfrom[k]
        sems.arrived(s_x[k][0], out.at[yh, far, c, band], pc.xdev[k])
        sems.arrived(s_x[k][1], out.at[1 - yh, far, c, band], pc.xdev[k])
        if split:
            piece = out.at[:, far, c, band]
            for j in range(3):
                sems.push(s_z[k][j], piece, piece, pc.zdev[j])
        else:
            piece = out.at[k, far, c]
            sems.push(s_x[2][k], piece, piece, pc.xdev[k])
            sems.push(s_s[k], out.at[:, far, c], out.at[:, far, c], pc.sib)
    yield
    if split:
        for k in (0, 1, 2):
            far = pc.xfrom[k]
            for j in range(3):
                there = pl.ds(pl.multiple_of(pc.zfrom[j] * quarter, 16), quarter)
                sems.arrived(s_z[k][j], out.at[:, far, c, there], pc.zdev[j])
            sems.push(s_s[k], out.at[:, far, c], out.at[:, far, c], pc.sib)
    else:
        far = pc.xs[2]
        for k in (0, 1):
            sems.arrived(s_x[2][k], out.at[k, far, c], pc.xdev[k])
        sems.push(s_s[2], out.at[:, far, c], out.at[:, far, c], pc.sib)
    yield
    for k in (0, 1, 2, 3):
        far = x if k == 3 else pc.xfrom[k]
        sems.arrived(s_s[k], out.at[:, far, 1 - c], pc.sib)
    yield


def run_all(steps):
    live = list(steps)
    while live:
        for s in list(live):
            try:
                next(s)
            except StopIteration:
                live.remove(s)


REDUCE_SEMS = 32


def add_rows(dst, terms, shape):
    lead, rows = shape[:-2], shape[-2]
    blocks = rows // 16
    count = math.prod(lead) * blocks

    def body(i, carry):
        idx, rest = [], i // blocks
        for size in reversed(lead):
            idx.append(rest % size)
            rest = rest // size
        idx = tuple(reversed(idx))
        at = (*idx, pl.ds(pl.multiple_of((i % blocks) * 16, 16), 16))
        total = dst[at].astype(F32)
        for term in terms:
            total = total + term[at].astype(F32)
        dst[at] = total.astype(BF16)
        return carry

    lax.fori_loop(0, count, body, 0)


def reduce_scratch(rows, width, split):
    q = rows // 4
    return [
        pltpu.VMEM((2, 4, rows, width), BF16),
        pltpu.VMEM((3 if split else 2, 2, q if split else rows, width), BF16),
        pltpu.VMEM((3, rows // 2, width), BF16),
        pltpu.VMEM((3, rows // 2, width // 4), BF16),
        pltpu.VMEM((3, 3, 2, q, width) if split else (2, rows, width), BF16),
    ]


def reduce_steps(pc, sems, local_sem, part, final, buffers, split):
    yh, x, c, z, yl = pc.yh, pc.x, pc.c, pc.z, pc.yl
    acc, from_x, from_y, from_z, from_r = buffers
    rows, width = part.shape[-2:]
    q = rows // 4
    s_m = sems.take()
    s_y = [sems.take() for _ in range(3)]
    s_x = [sems.take() for _ in range(3)]
    s_z = [sems.take() for _ in range(3)]
    s_f = [sems.take() for _ in range(3)]
    s_r = [[sems.take() for _ in range(3)] for _ in range(3)]

    def band(k):
        return pl.ds(pl.multiple_of(k * q, 16), q)

    own = pltpu.make_async_copy(part, acc, local_sem)
    own.start()
    own.wait()
    if split:
        here = band(z)
        order = (2, 0, 1)
        for k in order:
            for j in range(3):
                piece = acc.at[:, pc.xs[k], band(pc.zs[j])]
                sems.push(s_r[k][j], piece, from_r.at[j, k], pc.zdev[j])
        yield
        for k in order:
            for j in range(3):
                sems.arrived(s_r[k][j], from_r.at[j, k], pc.zdev[j])
            mine = acc.at[:, pc.xs[k], here]
            add_rows(mine, [from_r.at[j, k] for j in range(3)], (2, q, width))
            sems.push(s_x[k], mine, from_x.at[k], pc.xdev[k])
        yield
        for k in range(3):
            sems.arrived(s_x[k], from_x.at[k], pc.xdev[k])
        add_rows(acc.at[:, x, here], [from_x.at[k] for k in range(3)], (2, q, width))
    else:
        for k in range(2):
            sems.push(s_r[0][k], acc.at[k, pc.xs[2]], from_r.at[k], pc.xdev[k])
        yield
        for k in range(2):
            sems.arrived(s_r[0][k], from_r.at[k], pc.xdev[k])
            add_rows(acc.at[k, pc.xs[k]], [from_r.at[k]], (rows, width))
            sems.push(s_x[k], acc.at[:, pc.xs[k]], from_x.at[k], pc.xdev[k])
        yield
        for k in range(2):
            sems.arrived(s_x[k], from_x.at[k], pc.xdev[k])
        add_rows(acc.at[:, x], [from_x.at[k] for k in range(2)], (2, rows, width))
    h, w = rows // 2, width // 4

    def side(k):
        return pl.ds(pl.multiple_of(k * h, 16), h)

    def column(k):
        return pl.ds(pl.multiple_of(k * w, 128), w)

    half, other = side(yl), side(1 - yl)
    for n, (there, k) in enumerate(((yh, 1 - yl), (1 - yh, yl), (1 - yh, 1 - yl))):
        dev = device(there, x, c, z, k)
        sems.push(s_y[n], acc.at[there, x, side(k)], from_y.at[n], dev)
    yield
    for n in range(3):
        sems.arrived(s_y[n], from_y.at[n], pc.sib)
    add_rows(acc.at[yh, x, half], [from_y.at[n] for n in range(3)], (h, width))
    for j in range(3):
        piece = acc.at[yh, x, half, column(pc.zs[j])]
        sems.push(s_z[j], piece, from_z.at[j], pc.zdev[j])
    yield
    for j in range(3):
        sems.arrived(s_z[j], from_z.at[j], pc.zdev[j])
    mine = acc.at[yh, x, half, column(z)]
    add_rows(mine, [from_z.at[j] for j in range(3)], (h, w))
    done = final.at[half, column(z)]
    done[...] = mine[...]
    for j in range(3):
        sems.push(s_f[j], done, done, pc.zdev[j])
    yield
    for j in range(3):
        sems.arrived(s_f[j], final.at[half, column(pc.zfrom[j])], pc.zdev[j])
    sems.push(s_m, final.at[half], final.at[half], pc.ylo)
    yield
    sems.arrived(s_m, final.at[other], pc.ylo)
    yield


def small_scratch(rows, width):
    q = rows // 4
    return [
        pltpu.VMEM((2, 4, rows, width), BF16),
        pltpu.VMEM((2, 4, rows, width), BF16),
        pltpu.VMEM((3, 2, 4, q, width), BF16),
        pltpu.VMEM((7, q, width), BF16),
        pltpu.VMEM((2, rows, width), BF16),
    ]


def small_steps(pc, sems, local_sem, part, final, buffers):
    yh, x, c, z, yl = pc.yh, pc.x, pc.c, pc.z, pc.yl
    acc, from_sib, from_z, from_xy, landed = buffers
    rows, width = part.shape[-2:]
    q = rows // 4
    s_s = sems.take()
    s_z = [sems.take() for _ in range(3)]
    s_xy = [sems.take() for _ in range(7)]
    s_f = [sems.take() for _ in range(7)]

    def band(k):
        return pl.ds(pl.multiple_of(k * q, 16), q)

    here = band(z)
    own = pltpu.make_async_copy(part.at[:, :, c], acc, local_sem)
    own.start()
    sems.push(s_s, part.at[:, :, 1 - c], from_sib, pc.sib)
    yield
    own.wait()
    sems.arrived(s_s, from_sib, pc.sib)
    add_rows(acc, [from_sib], acc.shape)
    for j in range(3):
        sems.push(s_z[j], acc.at[:, :, band(pc.zs[j])], from_z.at[j], pc.zdev[j])
    yield
    for j in range(3):
        sems.arrived(s_z[j], from_z.at[j], pc.zdev[j])
    add_rows(acc.at[:, :, here], [from_z.at[j] for j in range(3)], (2, 4, q, width))
    targets = [(yh, pc.xs[k], yl) for k in range(3)]
    targets += [(1 - yh, k, 1 - yl) for k in (*pc.xs, x)]
    for n, (there, k, side) in enumerate(targets):
        sems.push(s_xy[n], acc.at[there, k, here], from_xy.at[n], device(there, k, c, z, side))
    yield
    for n in range(7):
        sems.arrived(s_xy[n], from_xy.at[n], pc.sib)
    mine = acc.at[yh, x, here]
    add_rows(mine, [from_xy.at[n] for n in range(7)], (q, width))
    landed[yl, here] = mine[...]
    for n, (k, side) in enumerate([(k, yl) for k in pc.zs] + [(k, 1 - yl) for k in (*pc.zs, z)]):
        sems.push(s_f[n], mine, landed.at[yl, here], device(yh, x, c, k, side))
    yield
    for n, (k, side) in enumerate(
        [(k, yl) for k in pc.zfrom] + [(k, 1 - yl) for k in (*pc.zfrom, z)]
    ):
        sems.arrived(s_f[n], landed.at[side, band(k)], pc.sib)

    def body(i, carry):
        at = pl.ds(pl.multiple_of(i * 16, 16), 16)
        total = landed[0, at].astype(F32) + landed[1, at].astype(F32)
        final[at] = total.astype(BF16)
        return carry

    lax.fori_loop(0, rows // 16, body, 0)
    yield


class Column:
    def __init__(self, pc):
        self.z, self.yl = pc.z, pc.yl
        self.t = 2 * pc.z + pc.yl
        self.beside = pc.ylo
        self.pc = pc

    def own(self, step):
        return 2 * (self.z + step) + self.yl

    def other(self, step):
        return 2 * (self.z + step) + 1 - self.yl

    def device(self, step):
        pc = self.pc
        return device(pc.yh, pc.x, pc.c, (pc.z + step + 4) % 4, pc.yl)


def dot(a, b):
    return jnp.dot(a, b, preferred_element_type=F32)


def dot_tn(a, b):
    return lax.dot_general(a, b, (((0,), (0,)), ((), ())), preferred_element_type=F32)


def dot_nt(a, b):
    return lax.dot_general(a, b, (((1,), (1,)), ((), ())), preferred_element_type=F32)


def norm_scale(rows):
    return lax.rsqrt(jnp.sum(rows * rows, axis=-1, keepdims=True) * (1.0 / WIDTH) + EPS)


def norm_back(grad_normed, rows, scale, gain):
    unit = rows * scale
    grad_gain = jnp.sum(grad_normed * unit, axis=0)
    grad_unit = grad_normed * gain
    mean = jnp.sum(grad_unit * unit, axis=-1, keepdims=True) * (1.0 / WIDTH)
    return scale * (grad_unit - unit * mean), grad_gain


BLOCK = 256
PAIR = 2 * HEAD_WIDTH
STACK = GROUP * BLOCK
FACTOR = HEAD_WIDTH ** (-0.5)


def low_half(shape):
    return lax.broadcasted_iota(jnp.int32, shape, 1) % PAIR < HEAD_WIDTH


def swap_halves(tile):
    lane = lax.broadcasted_iota(jnp.int32, tile.shape, 1) % HEAD_WIDTH
    half = HEAD_WIDTH // 2
    return jnp.where(
        lane < half, pltpu.roll(tile, PAIR - half, 1), pltpu.roll(tile, half, 1)
    )


def flip(a):
    return a.astype(F32).T.astype(a.dtype)


def advance(*steps):
    for s in steps:
        next(s, None)


def drain(*steps):
    run_all(steps)


def tile_of(ref, tile):
    return ref[:, :, :, :, tile * PAIR : (tile + 1) * PAIR].reshape(PADDED, PAIR)


def gain_row(kv_w, which):
    pick = lax.broadcasted_iota(jnp.int32, (8, PAIR), 1) == HEAD_WIDTH + which
    return dot_nt(pick.astype(BF16), tile_of(kv_w, KV_TILES - 1))[0:1]


def copy_wait(sems, slot, ref, dev):
    pltpu.make_async_remote_copy(
        src_ref=ref,
        dst_ref=ref,
        send_sem=sems.send.at[slot],
        recv_sem=sems.recv.at[slot],
        device_id=dev,
        device_id_type=MESH,
    ).wait_send()


def forward_kernel(
    tokens_t,
    cosine,
    sine,
    select,
    kv_shard,
    q_shard,
    own_out,
    own_gate,
    own_up,
    own_down,
    kv_out,
    q_out,
    out_w,
    gate_w,
    up_a_w,
    up_b_w,
    down_w,
    normed_out,
    queries_out,
    kv_all,
    o_t,
    lse,
    mixed,
    gain_two,
    flat_out,
    kv_w,
    q_w,
    normed_t,
    q_t,
    flat,
    store,
    peak,
    wide,
    out_shard,
    gate_shard,
    up_a_shard,
    up_b_shard,
    down_shard,
    send,
    recv,
    local,
    kv_send,
    kv_recv,
):
    pc = Places()
    col = Column(pc)
    t, z, yl = col.t, pc.z, pc.yl
    greet([pc.sib, pc.ypair, pc.ylo, *pc.xdev, *pc.zdev])
    sems, kv_sems = Sems(send, recv), Sems(kv_send, kv_recv)
    g_kv = gather_steps(pc, sems, local.at[0], kv_shard, kv_w, True)
    g_q = gather_steps(pc, sems, local.at[1], q_shard, q_w, False)
    g_out = gather_steps(pc, sems, local.at[2], out_shard, out_w, False)
    g_gate = gather_steps(pc, sems, local.at[3], gate_shard, gate_w, True)
    g_up = gather_steps(pc, sems, local.at[4], up_a_shard, up_a_w, True)
    g_half = gather_steps(pc, sems, local.at[5], up_b_shard, up_b_w, False)
    g_down = gather_steps(pc, sems, local.at[6], down_shard, down_w, False)
    advance(g_kv, g_kv, g_q)
    ones = (
        lax.broadcasted_iota(jnp.int32, (PAD, ROWS), 0)
        == lax.broadcasted_iota(jnp.int32, (PAD, ROWS), 1)
    ).astype(BF16)
    gate_shard[...] = dot(ones, own_gate[...]).astype(BF16)
    advance(g_gate, g_gate)
    half = up_a_shard.shape[1]
    up_a_shard[...] = dot(ones, own_up[:, :half]).astype(BF16)
    up_b_shard[...] = dot(ones, own_up[:, half:]).astype(BF16)
    advance(g_up)
    down_shard[...] = dot(own_down[...], select[...]).astype(BF16)
    out_shard[...] = dot(ones, dot(own_out[...], select[...]).astype(BF16)).astype(BF16)
    x = dot_tn(tokens_t[...], select[...])
    flat[...] = x
    stores = [
        pltpu.make_async_copy(src, dst, store.at[n])
        for n, (src, dst) in enumerate(
            ((flat, flat_out), (kv_w, kv_out), (q_w, q_out), (normed_t, normed_out), (q_t, queries_out))
        )
    ]
    stores[0].start()
    scale = norm_scale(x)
    advance(g_kv, g_q)
    advance(g_kv, g_q, g_gate, g_up)
    advance(g_kv, g_out, g_half, g_down)
    advance(g_kv)
    stores[1].start()

    rows = (x * scale * gain_row(kv_w, 0)).astype(BF16)
    gain_two[...] = gain_row(kv_w, 1)
    cos, sin = cosine[...], sine[...]
    low = low_half((BLOCK, PAIR))

    def place_queries(product, tile):
        turned = (product * FACTOR).T.astype(BF16)
        for side in range(2):
            head = 2 * tile + side
            if head < QUERY_HEADS:
                h, g = head // GROUP, head % GROUP
                at = slice(g * BLOCK, (g + 1) * BLOCK)
                q_t[h, 0:HEAD_WIDTH, at] = turned[side * HEAD_WIDTH : (side + 1) * HEAD_WIDTH]
                q_t[h, HEAD_WIDTH:PAIR, at] = jnp.zeros((HEAD_WIDTH, BLOCK), BF16)

    for tile in range(KV_TILES):
        product = dot(rows, tile_of(kv_w, tile))
        if tile < 3:
            product = product * cos + swap_halves(product) * sin
        wide[tile] = product
    for h in range(KEY_VALUE_HEADS):
        k_tile, k_high = (h + 1) // 2, (h + 1) % 2
        v_tile, v_high = 3 + h // 2, h % 2
        k_part, v_part = wide[k_tile], wide[v_tile]
        if k_high:
            k_part = pltpu.roll(k_part, HEAD_WIDTH, 1)
        if not v_high:
            v_part = pltpu.roll(v_part, HEAD_WIDTH, 1)
        kv_all[t, h] = jnp.where(low, k_part, v_part).astype(BF16)
    for step in (1, 2, 3):

        @pl.when(z + step < 4)
        def _(step=step):
            kv_sems.push(step - 1, kv_all.at[t], kv_all.at[t], col.device(step))

    @pl.when(yl == 0)
    def _():
        kv_sems.push(3, kv_all.at[t], kv_all.at[t], col.beside)

    advance(g_gate, g_up, g_q)
    advance(g_out, g_half, g_down)
    place_queries(wide[0], 7)
    normed_t[...] = flip(rows)
    stores[3].start()
    advance(g_q, g_up, g_q)
    stores[2].start()
    for tile in range(Q_TILES):
        product = dot(rows, tile_of(q_w, tile))
        place_queries(product * cos + swap_halves(product) * sin, tile)
    stores[4].start()
    peak[...] = jnp.full_like(peak, -1e30)
    o_t[...] = jnp.zeros_like(o_t)

    def visit(j, diagonal):
        def per_head(h, carry):
            kv = kv_all[j, h]
            kv_t = flip(kv)
            ones = lax.broadcasted_iota(jnp.int32, (PAIR, BLOCK), 0) < HEAD_WIDTH
            ones_v = jnp.where(ones, 1.0, kv_t.astype(F32)).astype(BF16)
            scores = dot(kv, q_t[h])
            if diagonal:
                key = lax.broadcasted_iota(jnp.int32, (BLOCK, STACK), 0)
                query = lax.broadcasted_iota(jnp.int32, (BLOCK, STACK), 1) % BLOCK
                scores = jnp.where(key <= query, scores, -1e30)
            old = peak[h]
            new = jnp.maximum(old, jnp.max(scores, axis=0, keepdims=True))
            probs = jnp.exp(scores - new[0:1]).astype(BF16)
            o_t[h] = o_t[h] * jnp.exp(old - new)[0:1] + dot(ones_v, probs)
            peak[h] = new
            return carry

        lax.fori_loop(0, KEY_VALUE_HEADS, per_head, 0)

    advance(g_out, g_half, g_down)
    visit(t, True)
    for step in (1, 2, 3):

        @pl.when(z - step >= 0)
        def _(step=step):
            block = kv_all.at[col.own(-step)]
            kv_sems.arrived(step - 1, block, col.device(-step))
            kv_sems.push(3 + step, block, block, col.beside)
            visit(col.own(-step), False)

        if step == 1:
            advance(g_out, g_half, g_down)
        if step == 2:
            advance(g_gate)
        if step == 3:
            advance(g_out, g_half, g_down)
    for step in (0, 1, 2, 3):

        @pl.when((yl == 1) if step == 0 else (z - step >= 0))
        def _(step=step):
            block = kv_all.at[col.other(-step)]
            kv_sems.arrived(3 + step, block, col.beside)
            visit(col.other(-step), False)

        if step == 1:
            advance(g_up)

    for h in range(KEY_VALUE_HEADS):
        total = o_t[h, 0:1]
        o_t[h] = o_t[h] * (1.0 / total)
        lse[h] = peak[h] + jnp.log(total)
    for tile in range(8):
        parts = []
        for head in (2 * tile, min(2 * tile + 1, QUERY_HEADS - 1)):
            h, g = head // GROUP, head % GROUP
            parts.append(o_t[h, HEAD_WIDTH:PAIR, g * BLOCK : (g + 1) * BLOCK])
        joined = jnp.concatenate(parts, axis=0).T.astype(BF16)
        if tile < 7:
            mixed[:, tile * PAIR : (tile + 1) * PAIR] = joined
        else:
            mixed[:, tile * PAIR : tile * PAIR + HEAD_WIDTH] = joined[:, :HEAD_WIDTH]
    drain(g_gate, g_up, g_half, g_down, g_out)
    for copy in stores:
        copy.wait()
    for step in (1, 2, 3):

        @pl.when(z + step < 4)
        def _(step=step):
            copy_wait(kv_sems, step - 1, kv_all.at[t], col.device(step))

        @pl.when(z - step >= 0)
        def _(step=step):
            copy_wait(kv_sems, 3 + step, kv_all.at[t], col.beside)

    @pl.when(yl == 0)
    def _():
        copy_wait(kv_sems, 3, kv_all.at[t], col.beside)

    sems.finish()


def forward(values, shards, weights, collective_id):
    vmem, hbm = pl.BlockSpec(memory_space=pltpu.VMEM), pl.BlockSpec(memory_space=pl.ANY)
    hidden = weights[1].shape[1]
    rows = [PAD] * 6 + [weights[3].shape[0]]
    widths = [s.shape[1] for s in shards] + [PADDED, hidden, hidden // 2, hidden // 2, PADDED]
    padded = list(zip(rows, widths))
    gathered = [jax.ShapeDtypeStruct((2, 4, 2, *p), BF16) for p in padded]
    return pl.pallas_call(
        forward_kernel,
        out_shape=[
            *gathered,
            jax.ShapeDtypeStruct((PADDED, BLOCK), BF16),
            jax.ShapeDtypeStruct((KEY_VALUE_HEADS, PAIR, STACK), BF16),
            jax.ShapeDtypeStruct((8, KEY_VALUE_HEADS, BLOCK, PAIR), BF16),
            jax.ShapeDtypeStruct((KEY_VALUE_HEADS, PAIR, STACK), F32),
            jax.ShapeDtypeStruct((KEY_VALUE_HEADS, 8, STACK), F32),
            jax.ShapeDtypeStruct((BLOCK, WIDTH), BF16),
            jax.ShapeDtypeStruct((1, PADDED), F32),
            jax.ShapeDtypeStruct((BLOCK, PADDED), F32),
        ],
        in_specs=[vmem] * 4 + [hbm] * 2 + [vmem] * 4,
        out_specs=[hbm] * 9 + [vmem] * 5 + [hbm],
        scratch_shapes=[
            pltpu.VMEM(gathered[0].shape, BF16),
            pltpu.VMEM(gathered[1].shape, BF16),
            pltpu.VMEM((PADDED, BLOCK), BF16),
            pltpu.VMEM((KEY_VALUE_HEADS, PAIR, STACK), BF16),
            pltpu.VMEM((BLOCK, PADDED), F32),
            pltpu.SemaphoreType.DMA((5,)),
            pltpu.VMEM((KEY_VALUE_HEADS, 8, STACK), F32),
            pltpu.VMEM((KV_TILES, BLOCK, PAIR), F32),
            *[pltpu.VMEM(p, BF16) for p in padded[2:]],
            pltpu.SemaphoreType.DMA((7 * GATHER_SEMS,)),
            pltpu.SemaphoreType.DMA((7 * GATHER_SEMS,)),
            pltpu.SemaphoreType.DMA((7,)),
            pltpu.SemaphoreType.DMA((7,)),
            pltpu.SemaphoreType.DMA((7,)),
        ],
        compiler_params=pltpu.CompilerParams(
            collective_id=collective_id, has_side_effects=True, vmem_limit_bytes=60 << 20
        ),
    )(*values, *shards, *weights)


PARTS = 4
STEP = 640


def middle_kernel(
    flat_in,
    d_out_t,
    mixed,
    gain_two,
    select,
    out_in,
    gate_w,
    up_a_w,
    up_b_w,
    down_w,
    output_t,
    grad_resid,
    grad_gain_two,
    grad_mixed,
    gate_out,
    up_out,
    down_out,
    out_out,
    gate_acc,
    up_acc,
    down_acc,
    out_acc,
    flat,
    out_w,
    first,
    store,
    gate_buf,
    up_buf,
    down_buf,
    gate_stage,
    up_stage,
    down_stage,
    out_stage,
    gate_sib,
    up_sib,
    down_sib,
    out_sib,
    total,
    back,
    load,
    local,
    send,
    recv,
):
    pc = Places()
    c = pc.c

    def loads(i):
        at = pl.ds(i * STEP, STEP)
        slot = i % 2
        up_w, side = (up_a_w, up_b_w)[i // 2], pl.ds(slot * STEP, STEP)
        return (
            pltpu.make_async_copy(gate_w.at[:, at], gate_buf.at[slot], load.at[slot, 0]),
            pltpu.make_async_copy(up_w.at[:, side], up_buf.at[slot], load.at[slot, 1]),
            pltpu.make_async_copy(down_w.at[at], down_buf.at[slot], load.at[slot, 2]),
        )

    def remote(src, dst, k):
        return pltpu.make_async_remote_copy(
            src_ref=src,
            dst_ref=dst,
            send_sem=send.at[k],
            recv_sem=recv.at[k],
            device_id=pc.sib,
            device_id_type=MESH,
        )

    def sends(i):
        at, slot = pl.ds(i * STEP, STEP), i % 2
        yh, xs = i // 2, pl.ds(2 * (i % 2), 2)
        gate, up, down = gate_stage.at[slot], up_stage.at[slot], down_stage.at[slot]
        return (
            remote(gate.at[:, :, 1 - c], gate_sib.at[:, :, :, at], 3 * i),
            remote(up.at[:, :, 1 - c], up_sib.at[:, :, :, at], 3 * i + 1),
            remote(down.at[:, 1 - c], down_sib.at[yh, xs], 3 * i + 2),
            pltpu.make_async_copy(gate.at[:, :, c], gate_acc.at[:, :, :, at], local.at[slot, 0]),
            pltpu.make_async_copy(up.at[:, :, c], up_acc.at[:, :, :, at], local.at[slot, 1]),
            pltpu.make_async_copy(down.at[:, c], down_acc.at[yh, xs], local.at[slot, 2]),
        )

    def sent(i):
        copies = sends(i)
        for copy in copies[:3]:
            copy.wait_send()
        for copy in copies[3:]:
            copy.wait()

    firsts = (
        pltpu.make_async_copy(out_in, out_w, first.at[0]),
        pltpu.make_async_copy(flat_in, flat, first.at[1]),
    )
    for copy in (*firsts, *loads(0)):
        copy.start()
    grad = dot_tn(d_out_t[...], select[...]).astype(BF16)
    mixed_p = dot(mixed[...], select[...]).astype(BF16)
    for copy in firsts:
        copy.wait()
    resid = flat[...] + dot(mixed_p, out_w[...])
    scale = norm_scale(resid)
    gain = gain_two[...]
    normed = (resid * scale * gain).astype(BF16)
    normed_t = flip(normed)
    total[...] = resid
    back[...] = jnp.zeros_like(back)
    for i in range(PARTS):
        slot = i % 2
        if i + 1 < PARTS:
            for copy in loads(i + 1):
                copy.start()
        for copy in loads(i):
            copy.wait()
        if i >= 2:
            sent(i - 2)
        w_gate, w_up, w_down = gate_buf[slot], up_buf[slot], down_buf[slot]
        gate = dot(normed, w_gate)
        up = dot(normed, w_up)
        grad_hidden = dot_nt(grad, w_down)
        sigmoid = 0.5 * jnp.tanh(0.5 * gate) + 0.5
        swish = gate * sigmoid
        hidden = (swish * up).astype(BF16)
        grad_up_v = (grad_hidden * swish).astype(BF16)
        grad_gate_v = (grad_hidden * up * sigmoid * (1.0 + gate * (1.0 - sigmoid))).astype(BF16)
        total[...] += dot(hidden, w_down)
        back[...] += dot_nt(grad_gate_v, w_gate) + dot_nt(grad_up_v, w_up)
        shape = (2, 4, 2, PAD, STEP)
        gate_stage[slot] = dot(normed_t, grad_gate_v).astype(BF16).reshape(shape)
        up_stage[slot] = dot(normed_t, grad_up_v).astype(BF16).reshape(shape)
        down = dot(flip(hidden), grad).astype(BF16)
        down_stage[slot] = down.reshape(2, 2, STEP // 4, PADDED)
        if i == 0:
            greet([pc.sib])
        for copy in sends(i):
            copy.start()
    output_t[...] = dot_nt(select[...], total[...].astype(BF16)).astype(BF16)
    term, grad_gain = norm_back(back[...], resid, scale, gain)
    grad_gain_two[...] = grad_gain[None, :]
    full = grad.astype(F32) + term
    grad_resid[...] = full
    branch = full.astype(BF16)
    out_stage[...] = dot(flip(mixed_p), branch).astype(BF16).reshape(2, 4, 2, PAD, PADDED)
    out_send = remote(out_stage.at[:, :, 1 - c], out_sib, 3 * PARTS)
    out_send.start()
    out_copy = pltpu.make_async_copy(out_stage.at[:, :, c], out_acc, local.at[0, 3])
    out_copy.start()
    inner = dot_nt(branch, out_w[...]).astype(BF16)
    grad_mixed[...] = dot_nt(inner, select[...]).astype(BF16)
    for i in (PARTS - 2, PARTS - 1):
        sent(i)
    for i in range(PARTS):
        for copy in sends(i)[:3]:
            copy.wait_recv()
    stores = []

    def finish(acc, other, out):
        add_rows(acc, [other], acc.shape)
        stores.append(pltpu.make_async_copy(acc, out, store.at[len(stores)]))
        stores[-1].start()

    finish(gate_acc, gate_sib, gate_out)
    finish(up_acc, up_sib, up_out)
    finish(down_acc, down_sib, down_out)
    out_send.wait()
    out_copy.wait()
    finish(out_acc, out_sib, out_out)
    for copy in stores:
        copy.wait()


def middle(values, weights, collective_id):
    vmem, hbm = pl.BlockSpec(memory_space=pltpu.VMEM), pl.BlockSpec(memory_space=pl.ANY)
    hidden = weights[0].shape[1]
    tall = hidden // SHARDS
    accs = [(2, 4, PAD, hidden), (2, 4, PAD, hidden), (2, 4, tall, PADDED), (2, 4, PAD, PADDED)]
    return pl.pallas_call(
        middle_kernel,
        out_shape=[
            jax.ShapeDtypeStruct((WIDTH, BLOCK), BF16),
            jax.ShapeDtypeStruct((BLOCK, PADDED), F32),
            jax.ShapeDtypeStruct((1, PADDED), F32),
            jax.ShapeDtypeStruct((BLOCK, WIDTH), BF16),
            *[jax.ShapeDtypeStruct(a, BF16) for a in accs],
        ],
        in_specs=[hbm] + [vmem] * (len(values) - 2) + [hbm] * 5,
        out_specs=[vmem] * 4 + [hbm] * 4,
        scratch_shapes=[
            *[pltpu.VMEM(a, BF16) for a in accs],
            pltpu.VMEM((BLOCK, PADDED), F32),
            pltpu.VMEM((PADDED, PADDED), BF16),
            pltpu.SemaphoreType.DMA((2,)),
            pltpu.SemaphoreType.DMA((4,)),
            pltpu.VMEM((2, PADDED, STEP), BF16),
            pltpu.VMEM((2, PADDED, STEP), BF16),
            pltpu.VMEM((2, STEP, PADDED), BF16),
            pltpu.VMEM((2, 2, 4, 2, PAD, STEP), BF16),
            pltpu.VMEM((2, 2, 4, 2, PAD, STEP), BF16),
            pltpu.VMEM((2, 2, 2, STEP // 4, PADDED), BF16),
            pltpu.VMEM((2, 4, 2, PAD, PADDED), BF16),
            *[pltpu.VMEM(a, BF16) for a in accs],
            pltpu.VMEM((BLOCK, PADDED), F32),
            pltpu.VMEM((BLOCK, PADDED), F32),
            pltpu.SemaphoreType.DMA((2, 3)),
            pltpu.SemaphoreType.DMA((2, 4)),
            pltpu.SemaphoreType.DMA((3 * PARTS + 1,)),
            pltpu.SemaphoreType.DMA((3 * PARTS + 1,)),
        ],
        compiler_params=pltpu.CompilerParams(
            collective_id=collective_id, has_side_effects=True, vmem_limit_bytes=62 << 20
        ),
    )(*values, *weights)


def backward_kernel(
    gate_part,
    up_part,
    down_part,
    out_part,
    flat_in,
    grad_resid_in,
    grad_gain_two,
    cosine,
    sine,
    kv_in,
    q_in,
    normed_t,
    q_t,
    kv_all,
    o_t,
    lse,
    grad_mixed,
    gate_sum,
    up_sum,
    down_sum,
    out_sum,
    q_sum,
    kv_sum,
    d_tokens,
    flat,
    grad_resid,
    kv_w,
    q_w,
    load,
    do_t,
    do_n,
    q_n,
    dq_t,
    delta,
    dkv,
    landed,
    beside,
    grad_qkv,
    q_part,
    kv_part,
    send,
    recv,
    local,
    kv_send,
    kv_recv,
    *buffers,
):
    pc = Places()
    col = Column(pc)
    t, z, yl = col.t, pc.z, pc.yl
    loads = [
        pltpu.make_async_copy(src, dst, load.at[n])
        for n, (src, dst) in enumerate(
            ((q_in, q_w), (kv_in, kv_w), (flat_in, flat), (grad_resid_in, grad_resid))
        )
    ]
    greet([pc.sib, pc.ypair, pc.ylo, pc.yopp, *pc.xdev, *pc.zdev, *pc.xdiag, *pc.zdiag])
    sems, kv_sems = Sems(send, recv), Sems(kv_send, kv_recv)
    parts = (gate_part, up_part, down_part, out_part, q_part, kv_part)
    finals = (gate_sum, up_sum, down_sum, out_sum, q_sum, kv_sum)
    reduces = [
        reduce_steps(
            pc, sems, local.at[k], parts[k], finals[k], buffers[5 * k : 5 * k + 5], split
        )
        for k, split in enumerate(REDUCE_SPLITS)
    ]
    reduces += [
        small_steps(pc, sems, local.at[4 + k], parts[4 + k], finals[4 + k], buffers[20 + 5 * k : 25 + 5 * k])
        for k in range(2)
    ]
    r_gate, r_up, r_down, r_out, r_q, r_kv = reduces
    early = (r_up, r_down, r_gate, r_out)
    advance(r_up, r_gate, r_down, r_out)

    for copy in loads:
        copy.start()
    do_t[...] = jnp.zeros_like(do_t)
    for tile in range(8):
        if tile < 7:
            turned = flip(grad_mixed[:, tile * PAIR : (tile + 1) * PAIR])
        else:
            turned = flip(grad_mixed[:, tile * PAIR : tile * PAIR + HEAD_WIDTH])
        for side in range(2):
            head = 2 * tile + side
            if head < QUERY_HEADS:
                h, g = head // GROUP, head % GROUP
                do_t[h, HEAD_WIDTH:PAIR, g * BLOCK : (g + 1) * BLOCK] = turned[
                    side * HEAD_WIDTH : (side + 1) * HEAD_WIDTH
                ]
    for h in range(KEY_VALUE_HEADS):
        do_n[h] = flip(do_t[h])
        q_n[h] = flip(q_t[h])
        both = do_t[h, HEAD_WIDTH:PAIR].astype(F32) * o_t[h, HEAD_WIDTH:PAIR]
        delta[h] = jnp.broadcast_to(jnp.sum(both, axis=0, keepdims=True), (8, STACK))
    dq_t[...] = jnp.zeros_like(dq_t)

    def visit(j, diagonal):
        def per_head(h, carry):
            kv = kv_all[j, h]
            scores = dot(kv, q_t[h])
            if diagonal:
                key = lax.broadcasted_iota(jnp.int32, (BLOCK, STACK), 0)
                query = lax.broadcasted_iota(jnp.int32, (BLOCK, STACK), 1) % BLOCK
                scores = jnp.where(key <= query, scores, -1e30)
            probs = jnp.exp(scores - lse[h][0:1])
            grad_probs = dot(kv, do_t[h])
            grad_scores = (probs * (grad_probs - delta[h][0:1])).astype(BF16)
            both = dot(grad_scores, q_n[h]) + dot(probs.astype(BF16), do_n[h])
            dkv[j, h] = both.astype(BF16)
            dq_t[h] += dot(flip(kv), grad_scores)
            return carry

        lax.fori_loop(0, KEY_VALUE_HEADS, per_head, 0)


    for step in (3, 2, 1, 0):

        @pl.when((yl == 1) if step == 0 else (z - step >= 0))
        def _(step=step):
            j = col.other(-step)
            visit(j, False)
            kv_sems.push(step, dkv.at[j], beside.at[step], col.beside)

        if step == 3:
            pass
        if step == 2:
            advance(r_up)
        if step == 1:
            pass
        if step == 0:
            advance(r_down)
    for step in (3, 2, 1):

        @pl.when(z - step >= 0)
        def _(step=step):
            j = col.own(-step)
            visit(j, False)
            kv_sems.arrived(step, beside.at[step], col.beside)
            for h in range(KEY_VALUE_HEADS):
                total = dkv[j, h].astype(F32) + beside[step, h].astype(F32)
                dkv[j, h] = total.astype(BF16)
            kv_sems.push(3 + step, dkv.at[j], landed.at[step - 1], col.device(-step))

        if step == 3:
            pass
        if step == 2:
            pass
        if step == 1:
            pass
    visit(t, True)
    advance(r_gate, r_out)

    cos, sin = cosine[...], sine[...]

    def turn(tile):
        return tile * cos - swap_halves(tile) * sin

    for tile in range(8):
        pieces = []
        for head in (2 * tile, min(2 * tile + 1, QUERY_HEADS - 1)):
            h, g = head // GROUP, head % GROUP
            pieces.append(dq_t[h, 0:HEAD_WIDTH, g * BLOCK : (g + 1) * BLOCK])
        joined = turn(jnp.concatenate(pieces, axis=0).T * FACTOR)
        grad_qkv[:, tile * PAIR : (tile + 1) * PAIR] = joined.astype(BF16)
    rows = normed_t[...]
    for tile in range(Q_TILES):
        product = dot(rows, grad_qkv[:, tile * PAIR : (tile + 1) * PAIR])
        q_part[:, :, :, :, tile * PAIR : (tile + 1) * PAIR] = product.astype(BF16).reshape(
            2, 4, 2, PAD, PAIR
        )
    advance(r_q)
    advance(r_up)
    for copy in loads:
        copy.wait()
    from_queries = dot_nt(
        grad_qkv[:, : Q_TILES * PAIR], q_w[...].reshape(PADDED, Q_TILES * PAIR)
    )

    @pl.when(yl == 0)
    def _():
        kv_sems.arrived(0, beside.at[0], col.beside)
        for h in range(KEY_VALUE_HEADS):
            total = dkv[t, h].astype(F32) + beside[0, h].astype(F32)
            dkv[t, h] = total.astype(BF16)

    for step in (1, 2, 3):

        @pl.when(z + step < 4)
        def _(step=step):
            kv_sems.arrived(3 + step, landed.at[step - 1], col.device(step))

    advance(r_q)
    low = low_half((BLOCK, PAIR))
    totals = []
    for h in range(KEY_VALUE_HEADS):

        def add(k, total, h=h):
            return total + landed[k, h].astype(F32)

        totals.append(lax.fori_loop(0, 3 - z, add, dkv[t, h].astype(F32)))
    zero = jnp.zeros((BLOCK, PAIR), F32)
    left = grad_qkv[:, 7 * PAIR : 8 * PAIR].astype(F32)
    first = turn(pltpu.roll(totals[0], HEAD_WIDTH, 1))
    grad_qkv[:, 7 * PAIR : 8 * PAIR] = jnp.where(low, left, first).astype(BF16)
    for n, (a, b) in enumerate(((1, 2), (3, 4))):
        keys = turn(jnp.where(low, totals[a], pltpu.roll(totals[b], HEAD_WIDTH, 1)))
        grad_qkv[:, (8 + n) * PAIR : (9 + n) * PAIR] = keys.astype(BF16)
    for n, (a, b) in enumerate(((0, 1), (2, 3), (4, None))):
        high = zero if b is None else totals[b]
        vals = jnp.where(low, pltpu.roll(totals[a], HEAD_WIDTH, 1), high)
        grad_qkv[:, (10 + n) * PAIR : (11 + n) * PAIR] = vals.astype(BF16)

    x = flat[...]
    scale = norm_scale(x)
    grad_normed = from_queries + dot_nt(
        grad_qkv[:, Q_TILES * PAIR :], kv_w[...].reshape(PADDED, KV_TILES * PAIR)
    )
    token_term, grad_gain = norm_back(grad_normed, x, scale, gain_row(kv_w, 0))
    row = lax.broadcasted_iota(jnp.int32, (8, PADDED), 0)
    gains = jnp.where(row == 0, grad_gain[None, :], jnp.where(row == 1, grad_gain_two[...], 0.0))
    lane = lax.broadcasted_iota(jnp.int32, (8, PAIR), 1)
    which = lax.broadcasted_iota(jnp.int32, (8, PAIR), 0)
    put = (lane == which + HEAD_WIDTH) & (which < 2)
    for tile in range(KV_TILES):
        at = Q_TILES + tile
        product = dot(rows, grad_qkv[:, at * PAIR : (at + 1) * PAIR])
        if tile == KV_TILES - 1:
            product = product + dot_tn(gains.astype(BF16), put.astype(BF16))
        kv_part[:, :, :, :, tile * PAIR : (tile + 1) * PAIR] = product.astype(BF16).reshape(
            2, 4, 2, PAD, PAIR
        )
    advance(r_kv)
    advance(r_down)
    d_tokens[...] = (grad_resid[...] + token_term).astype(BF16)

    drain(r_kv, r_q, *early)

    for step in (0, 1, 2, 3):

        @pl.when((yl == 1) if step == 0 else (z - step >= 0))
        def _(step=step):
            copy_wait(kv_sems, step, beside.at[step], col.beside)

    for step in (1, 2, 3):

        @pl.when(z - step >= 0)
        def _(step=step):
            copy_wait(kv_sems, 3 + step, landed.at[step - 1], col.device(-step))

    sems.finish()


REDUCE_SPLITS = (True, False, False, False)


def backward(parts, values, collective_id):
    vmem, hbm = pl.BlockSpec(memory_space=pltpu.VMEM), pl.BlockSpec(memory_space=pl.ANY)
    q_shape = (2, 4, 2, PAD, Q_TILES * PAIR)
    kv_shape = (2, 4, 2, PAD, KV_TILES * PAIR)
    shapes = [p.shape for p in parts] + [q_shape, kv_shape]
    scratch = [
        pltpu.VMEM((BLOCK, PADDED), F32),
        pltpu.VMEM((BLOCK, PADDED), F32),
        pltpu.VMEM(kv_shape, BF16),
        pltpu.VMEM(q_shape, BF16),
        pltpu.SemaphoreType.DMA((4,)),
        pltpu.VMEM((KEY_VALUE_HEADS, PAIR, STACK), BF16),
        pltpu.VMEM((KEY_VALUE_HEADS, STACK, PAIR), BF16),
        pltpu.VMEM((KEY_VALUE_HEADS, STACK, PAIR), BF16),
        pltpu.VMEM((KEY_VALUE_HEADS, PAIR, STACK), F32),
        pltpu.VMEM((KEY_VALUE_HEADS, 8, STACK), F32),
        pltpu.VMEM((8, KEY_VALUE_HEADS, BLOCK, PAIR), BF16),
        pltpu.VMEM((3, KEY_VALUE_HEADS, BLOCK, PAIR), BF16),
        pltpu.VMEM((4, KEY_VALUE_HEADS, BLOCK, PAIR), BF16),
        pltpu.VMEM((BLOCK, (Q_TILES + KV_TILES) * PAIR), BF16),
        pltpu.VMEM(q_shape, BF16),
        pltpu.VMEM(kv_shape, BF16),
        pltpu.SemaphoreType.DMA((6 * REDUCE_SEMS,)),
        pltpu.SemaphoreType.DMA((6 * REDUCE_SEMS,)),
        pltpu.SemaphoreType.DMA((6,)),
        pltpu.SemaphoreType.DMA((7,)),
        pltpu.SemaphoreType.DMA((7,)),
    ]
    for s, split in zip(shapes, REDUCE_SPLITS):
        scratch += reduce_scratch(*s[-2:], split)
    scratch += small_scratch(*q_shape[-2:]) + small_scratch(*kv_shape[-2:])
    return pl.pallas_call(
        backward_kernel,
        out_shape=[jax.ShapeDtypeStruct(s[-2:], BF16) for s in shapes]
        + [jax.ShapeDtypeStruct((BLOCK, PADDED), BF16)],
        in_specs=[hbm] * 6 + [vmem] * 3 + [hbm] * 2 + [vmem] * (len(values) - 7),
        out_specs=[vmem] * 7,
        scratch_shapes=scratch,
        compiler_params=pltpu.CompilerParams(
            collective_id=collective_id, has_side_effects=True, vmem_limit_bytes=63 << 20
        ),
    )(*parts, *values)


def rotary_tables(token_positions):
    half = HEAD_WIDTH // 2
    freqs = ROPE_BASE ** (-jnp.arange(half, dtype=F32) * 2.0 / HEAD_WIDTH)
    angles = token_positions.astype(F32)[:, None] * freqs[None, :]
    cosine, sine = jnp.cos(angles), jnp.sin(angles)
    return (
        jnp.concatenate([cosine] * 4, axis=1),
        jnp.concatenate([-sine, sine] * 2, axis=1),
    )


def on_device(
    tokens,
    attn_gain,
    w_query,
    key_weight,
    value_weight,
    w_out,
    ffn_gain,
    w_gate,
    w_up,
    w_down,
    d_out,
):
    block = tokens.shape[1]
    token_positions = lax.axis_index("ctx") * block + jnp.arange(block, dtype=jnp.int32)
    cosine, sine = rotary_tables(token_positions)
    feature = jnp.arange(WIDTH, dtype=jnp.int32)
    place_of = feature // ROWS * PAD + feature % ROWS
    select = (place_of[:, None] == jnp.arange(PADDED, dtype=jnp.int32)[None, :]).astype(BF16)

    qkv_shard = jnp.pad(
        jnp.concatenate(
            [w_query, key_weight, value_weight, jnp.stack([attn_gain, ffn_gain]).T], axis=1
        ),
        ((0, PAD - ROWS), (0, (Q_TILES + KV_TILES) * PAIR - WIDTH - 2 * KV_WIDTH - 2)),
    )
    q_shard, kv_shard = qkv_shard[:, : Q_TILES * PAIR], qkv_shard[:, Q_TILES * PAIR :]
    kv_w, q_w, out_w, gate_w, up_a_w, up_b_w, down_w, *kept = forward(
        (tokens[0].T, cosine, sine, select),
        (kv_shard, q_shard),
        (w_out, w_gate, w_up, w_down),
        0,
    )
    normed_t, q_t, kv_all, o_t, lse, mixed, gain_two, flat = kept
    out_w = out_w.reshape(PADDED, PADDED)
    ffn_w = [w.reshape(PADDED, -1) for w in (gate_w, up_a_w, up_b_w)]
    ffn_w.append(down_w.reshape(-1, PADDED))
    output_t, grad_resid, grad_gain_two, grad_mixed, *parts = middle(
        (flat, d_out[0].T, mixed, gain_two, select, out_w), ffn_w, 2
    )
    sum_gate, sum_up, sum_down, sum_out, sum_q, sum_kv, d_tokens = backward(
        parts,
        (
            flat,
            grad_resid,
            grad_gain_two,
            cosine,
            sine,
            kv_w,
            q_w,
            normed_t,
            q_t,
            kv_all,
            o_t,
            lse,
            grad_mixed,
        ),
        1,
    )
    d_tokens = dot_nt(d_tokens, select).astype(BF16)
    sum_q, sum_kv = sum_q[:ROWS].astype(F32), sum_kv[:ROWS].astype(F32)
    ends = (HEAD_WIDTH, HEAD_WIDTH + KV_WIDTH, HEAD_WIDTH + 2 * KV_WIDTH)
    return (
        output_t.T[None],
        d_tokens[None],
        sum_kv[:, ends[2]],
        jnp.concatenate([sum_q, sum_kv[:, : ends[0]]], axis=1),
        sum_kv[:, ends[0] : ends[1]],
        sum_kv[:, ends[1] : ends[2]],
        dot_nt(sum_out[:ROWS], select),
        sum_kv[:, ends[2] + 1],
        sum_gate[:ROWS].astype(F32),
        sum_up[:ROWS].astype(F32),
        dot_nt(sum_down, select),
    )


def solution(mesh):
    rows, whole, line = P("fsdp", None), P("fsdp", "ctx", None), P("fsdp")
    weights = (line, rows, rows, rows, rows, line, rows, rows, rows)
    return jax.shard_map(
        on_device,
        mesh=mesh,
        in_specs=(whole, *weights, whole),
        out_specs=(whole, whole, *weights),
        check_vma=False,
    )
```
